128 devices in a mesh: gx: 16 (over x, y), gy: 8 (over z, core).
Axes of the slice: x: 4, y: 4, z: 4, core: 2. Of those that a mesh axis runs over, the one named last changes fastest.
Arguments:
- density: bfloat16 [32768, 256], P(('gx', 'gy')), may hold values from -0.015625 to 0.015625
- pair_tiles: int32 [32768, 4], P(('gx', 'gy')), may hold values from 0 to 127, all different within a row; in each aligned block of 256 rows (0 to 255, 256 to 511, ...) at most 16 rows name the same one
- pair_slots: int32 [32768, 4, 2], P(('gx', 'gy')), may hold values from 0 to 71
- pair_sizes: int32 [32768, 2], P(('gx', 'gy')), may hold values from 4 to 16
- basis_table: bfloat16 [128, 1152, 2048], P(('gx', 'gy')), may hold values from -6 to 6
- tile_extent: int32 [128, 2, 72], P(('gx', 'gy')), may hold values from 0 to 32, as said below
Outputs:
- hamiltonian: float32 [32768, 256], P(('gx', 'gy'))
- potential: float32 [512, 512], P('gx', 'gy')
The draws below stay inside these ranges and needn't reach their ends.
Inputs may be any that keep to these rules, and one draw needn't show every extreme that they name: `pair_tiles`: each pair names 4 different tiles; among the pairs of one device no tile is named more than 16 times, a bound that some block reaches. `pair_slots`: the same slot pair may reach one tile from several pairs; their blocks then add. `tile_extent`: the first row is below 16 and the last bound above it.
All inputs are finite; a program needn't handle non-finite values.
Results may differ from the reference program's by a relative error of at most 0.0031.
Values may be sent and summed in bfloat16 or wider, within the bound.
A program may use at most 128 MiB of HBM per device.

```python
import math
import jax
import jax.numpy as jnp
import numpy as np
from jax import lax

NB = 16
A_T = 72
CX = 32
CY = 64
PAIR_DEV = 256
KT = 4
TILES = 128
PAIRS = 32768
CAP = 16
NX = 512
NY = 512
N_GX = 16
N_GY = 8


def draw_tile_extent(key, part):
    key = jax.random.fold_in(key, 7)
    lower_key, upper_key = jax.random.split(key)
    lower_row = jax.random.randint(lower_key, (TILES, 1, A_T), 0, CX // 2)
    upper_row = jax.random.randint(upper_key, (TILES, 1, A_T), CX // 2 + 1, CX + 1)
    return jnp.concatenate([lower_row, upper_row], axis=1).astype(jnp.int32)


def set_ends(array, rng, smallest, largest):
    place = [jax.random.randint(jax.random.fold_in(rng, axis), (), 0, length) for axis, length in enumerate(array.shape)]
    widest = array.shape.index(max(array.shape))
    beside = place[:widest] + [(place[widest] + 1) % array.shape[widest]] + place[widest + 1:]
    return array.at[tuple(place)].set(smallest).at[tuple(beside)].set(largest)


def level_of(key, dims, cuts, least, largest):
    loudness = 1.0
    for dim, parts in cuts:
        heights = jax.random.uniform(jax.random.fold_in(jax.random.fold_in(key, 6), dim), (parts,), jnp.float32, least / len(cuts), largest / len(cuts))
        loudness = loudness * jnp.repeat(jnp.exp(heights), dims[dim] // parts).reshape((-1,) + (1,) * (len(dims) - 1 - dim))
    return loudness


def assign_block(stream_key, own, number, rows, number_of, top, most, skew):
    ranking = jax.random.permutation(stream_key, number_of)
    heavy_load, ordinary = portions_of(number_of, rows * top, most, skew, True), portions_of(number_of, rows * top, most, skew, False)
    places = jnp.arange(number_of)

    def named(sizes, rotation):
        used = int((sizes > 0).sum())
        fixed = max(1, used // 4)
        passed = fixed + (places - fixed + rotation * (used - fixed)) % max(1, number_of - fixed)
        return jnp.zeros((number_of,), jnp.int32).at[ranking[jnp.where(places < fixed, places, passed)]].set(jnp.asarray(sizes, jnp.int32))

    sizes = jnp.where(number % 4 == 0, named(heavy_load, number // 4), named(ordinary, number - number // 4 - 1))
    mixed = jax.random.permutation(jax.random.fold_in(own, 3), number_of)
    source_of, taker = mixed[0:number_of // 2 * 2:2], mixed[1:number_of // 2 * 2:2]
    slack = jnp.minimum(sizes[source_of] - 1, most - sizes[taker]) // 2
    slack = jnp.where((source_of == ranking[0]) | (taker == ranking[0]) | (sizes[taker] == 0), 0, jnp.maximum(slack, 0))
    passed = jax.random.randint(jax.random.fold_in(own, 4), (number_of // 2,), 0, 1 << 20) % (slack + 1)
    sizes = sizes.at[source_of].add(-passed).at[taker].add(passed)
    items = jnp.searchsorted(jnp.cumsum(sizes), jnp.arange(rows * top), side="right").astype(jnp.int32)
    grid = items.reshape(top, rows).T
    grid = grid[jax.random.permutation(jax.random.fold_in(own, 1), rows)]
    rotation = jax.random.randint(jax.random.fold_in(own, 2), (rows, 1), 0, top)
    return jnp.take_along_axis(grid, (jnp.arange(top)[None, :] + rotation) % top, axis=1)


def portions_of(amount, total, limit, lean, full):
    loads = [(1 << 20) // math.isqrt(grade ** lean) + 1 for grade in range(1, amount + 1)]
    largest = limit if full else min(limit, max(-(-total // amount), total * loads[0] // sum(loads)))
    least = 1 if total - largest >= amount - 1 else 0
    holding, surplus = [largest] + [least] * (amount - 1), total - largest - least * (amount - 1)
    while surplus > 0:
        candidates = [i for i in range(1, amount) if holding[i] < largest] or [i for i in range(1, amount) if holding[i] < limit]
        mass, remaining = sum([loads[i] for i in candidates]), surplus
        for i in candidates:
            addition = min(limit - holding[i], max(1, remaining * loads[i] // mass), surplus)
            holding[i] = holding[i] + addition
            surplus = surplus - addition
    return np.array(holding)


def bell_draw(own_key, shape, scale, reach, cuts=(), held_as=jnp.bfloat16):
    gain = level_of(own_key, shape, cuts, -0.22, 0.18) if cuts else 1.0
    values = jax.random.normal(own_key, shape, jnp.float32) * scale * gain
    return jnp.minimum(jnp.maximum(values, -reach), reach).astype(held_as)


def setup_inputs(seed: int = 0) -> dict:
    key_list = jax.random.split(jax.random.key(seed), 7)
    density = bell_draw(key_list[0], (PAIRS, NB * NB), (1.0 / (12 * (PAIR_DEV * KT) ** 0.5)), 0.015625, ((0, 128),))
    pair_tiles_keys = jax.random.split(jax.random.fold_in(key_list[1], 1), PAIRS // PAIR_DEV)
    pair_tiles_turns = jax.random.permutation(jax.random.fold_in(key_list[1], 3), PAIRS // PAIR_DEV)
    pair_tiles = jax.vmap(lambda own, number: assign_block(jax.random.fold_in(key_list[1], 2), own, number, PAIR_DEV, TILES, KT, CAP, 2))(pair_tiles_keys, pair_tiles_turns).reshape((PAIRS, KT))
    pair_slots = set_ends(jax.random.randint(key_list[2], (PAIRS, KT, 2), 0, A_T), jax.random.fold_in(key_list[2], 1), 0, A_T - 1).astype(jnp.int32)
    pair_sizes = set_ends(jax.random.randint(key_list[3], (PAIRS, 2), 4, 17), jax.random.fold_in(key_list[3], 1), 4, 16).astype(jnp.int32)
    basis_table = bell_draw(key_list[4], (TILES, A_T * NB, CX * CY), 1.0, 6.0, ((0, 128),))
    tile_extent = draw_tile_extent(jax.random.fold_in(key_list[6], 71), 0)
    return dict(density=density, pair_tiles=pair_tiles, pair_slots=pair_slots, pair_sizes=pair_sizes, basis_table=basis_table, tile_extent=tile_extent)


gradient_weight = 1.0

def masked_basis(tables, extent):
    cell_row = jnp.arange(CX * CY, dtype=jnp.int32) // CY
    inside = (cell_row[None, :] >= extent[0][:, None]) & (cell_row[None, :] < extent[1][:, None])
    shaped = tables.reshape(A_T, NB, CX * CY)
    masked = jnp.where(inside[:, None, :], shaped, jnp.zeros((), shaped.dtype))
    return masked.reshape(A_T * NB, CX * CY)

def reference(density, pair_tiles, pair_slots, pair_sizes, basis_table, tile_extent):
    row_index = jnp.arange(NB, dtype=jnp.int32)
    size_mask = (row_index[None, :, None] < pair_sizes[:, 0, None, None]) & (row_index[None, None, :] < pair_sizes[:, 1, None, None])
    size_mask = size_mask.reshape(PAIRS, NB * NB)
    blocks = jnp.where(size_mask, density, jnp.zeros((), density.dtype)).astype(jnp.float32)
    first_slot = pair_slots[:, :, 0]
    second_slot = pair_slots[:, :, 1]
    factor = jnp.where(first_slot == second_slot, 1.0, 2.0).astype(jnp.float32)
    outgoing = (blocks[:, None, :] * factor[:, :, None]).reshape(PAIRS * KT, NB * NB)
    slot_codes = (first_slot * A_T + second_slot).reshape(-1).astype(jnp.int32)
    flat_tiles = pair_tiles.reshape(-1).astype(jnp.int32)
    tile_list = jnp.arange(TILES, dtype=jnp.int32)

    def collocate(inputs):
        tile_index, tables, extent = inputs
        chosen = jnp.where((flat_tiles == tile_index)[:, None], outgoing, jnp.zeros((), outgoing.dtype))
        gathered = jax.ops.segment_sum(chosen, slot_codes, num_segments=A_T * A_T)
        rounded = lax.optimization_barrier(gathered.astype(jnp.bfloat16))
        matrix = rounded.astype(jnp.float32).reshape(A_T, A_T, NB, NB).transpose(0, 2, 1, 3).reshape(A_T * NB, A_T * NB)
        basis = masked_basis(tables, extent).astype(jnp.float32)
        spread = jnp.dot(matrix, basis, precision=lax.Precision.HIGHEST)
        return lax.optimization_barrier(jnp.sum(basis * spread, axis=0))
    charge = lax.map(collocate, (tile_list, basis_table, tile_extent))
    field = charge.reshape(N_GX, N_GY, CX, CY).transpose(0, 2, 1, 3).reshape(NX, NY)
    slope_first = 0.5 * (jnp.roll(field, -1, 0) - jnp.roll(field, 1, 0))
    slope_second = 0.5 * (jnp.roll(field, -1, 1) - jnp.roll(field, 1, 1))
    potential = field * lax.rsqrt(1.0 + field * field + gradient_weight * (slope_first * slope_first + slope_second * slope_second))
    tile_potential = potential.reshape(N_GX, CX, N_GY, CY).transpose(0, 2, 1, 3).reshape(TILES, CX * CY)

    def integrate(totals, inputs):
        tile_index, tables, extent, local_potential = inputs
        basis = masked_basis(tables, extent).astype(jnp.float32)
        weighted = lax.optimization_barrier((basis * local_potential[None, :]).astype(jnp.bfloat16))
        hamilton = jnp.dot(basis, weighted.astype(jnp.float32).T, precision=lax.Precision.HIGHEST) * (CX * CY) ** (-0.5)
        flat_blocks = hamilton.reshape(A_T, NB, A_T, NB).transpose(0, 2, 1, 3).reshape(A_T * A_T, NB * NB)
        picked = flat_blocks[slot_codes]
        totals = totals + jnp.where((flat_tiles == tile_index)[:, None], picked, jnp.zeros((), picked.dtype))
        return (totals, None)
    start = jnp.zeros((PAIRS * KT, NB * NB), jnp.float32)
    totals, unused = lax.scan(integrate, start, (tile_list, basis_table, tile_extent, tile_potential))
    summed = lax.optimization_barrier(jnp.sum(totals.reshape(PAIRS, KT, NB * NB), axis=1))
    hamiltonian = jnp.where(size_mask, summed, jnp.zeros((), summed.dtype))
    return (hamiltonian, potential)
```

```python
import functools

import jax
import jax.numpy as jnp
from jax import lax
from jax.experimental import pallas as pl
from jax.experimental.pallas import tpu as pltpu
from jax.sharding import PartitionSpec as P

NB = 16
CX = 32
CY = 64
LANES = 128
GROUPS = LANES // NB
WIDTH = NB * NB
CAP = 16
BATCH = 16
MESH = pl.DeviceIdType.MESH
F32 = jnp.float32
BF16 = jnp.bfloat16
I32 = jnp.int32
VMEM_BYTES = 60 * 1024 * 1024
gradient_weight = 1.0
NT = (((1,), (1,)), ((), ()))


def iota(shape, dim):
    return lax.broadcasted_iota(I32, shape, dim)


def dot(a, b, dims=(((1,), (0,)), ((), ()))):
    return lax.dot_general(a, b, dims, preferred_element_type=F32)


def ones_where(condition):
    return jnp.where(condition, 1.0, 0.0)


def size_mask_of(sizes):
    pairs = sizes.shape[1]
    eye = ones_where(iota((pairs, pairs), 0) == iota((pairs, pairs), 1)).astype(BF16)
    wide = sizes.astype(F32)
    first = dot(eye, jnp.broadcast_to(wide[0:1], (WIDTH, pairs)).astype(BF16), NT)
    second = dot(eye, jnp.broadcast_to(wide[1:2], (WIDTH, pairs)).astype(BF16), NT)
    lane = iota((pairs, WIDTH), 1)
    row = (lane // NB).astype(F32)
    col = (lane % NB).astype(F32)
    return (row < first) & (col < second)


def key_offset(column_tile):
    half = column_tile // 2
    return 16 * (half + 1) * (half + column_tile % 2)


def turned():
    row, lane = iota((WIDTH, WIDTH), 0), iota((WIDTH, WIDTH), 1)
    return ones_where((row // NB == lane % NB) & (row % NB == lane // NB)).astype(BF16)


def pack(tiles, slots_ref, masked, chunks, codes, picks):
    targets, pairs = tiles.shape
    devices = chunks.shape[0]
    tile_id = iota((devices, pairs), 0)
    chosen = jnp.zeros((devices, pairs), F32)
    kind = jnp.zeros((devices, pairs), F32)
    asked = []
    for k in range(targets):
        mark = ones_where(tiles[k : k + 1] == tile_id)
        slots = slots_ref[k].astype(F32)
        first, second = slots[0:1], slots[1:2]
        chosen = chosen + mark
        kind = kind + mark * (ones_where(first < second) + 2.0 * ones_where(first > second))
        asked += [tiles[k : k + 1].astype(F32), jnp.minimum(first, second), jnp.maximum(first, second)]
    asked = jnp.concatenate(asked + [jnp.zeros((16 - 3 * targets, pairs), F32)], axis=0).astype(BF16)
    before = ones_where(iota((pairs, pairs), 0) < iota((pairs, pairs), 1)).astype(BF16)
    rank = dot(chosen.astype(BF16), before)
    marked = jnp.where(chosen > 0.5, rank * 4.0 + kind, -4.0)
    blocks = jnp.concatenate([masked, dot(masked, turned()).astype(BF16)], axis=0)
    step = 32
    own = (4 * (iota((step * CAP, pairs), 0) % CAP)).astype(F32)
    for start in range(0, devices, step):
        rows = jnp.broadcast_to(marked[start : start + step, None, :], (step, CAP, pairs))
        rows = rows.reshape(step * CAP, pairs) - own
        same, upper, lower = ones_where(rows == 0.0), ones_where(rows == 1.0), ones_where(rows == 2.0)
        straight = (same + upper).astype(BF16)
        across = lower.astype(BF16)
        here = slice(start * CAP, (start + step) * CAP)
        picks[here, :pairs] = straight
        picks[here, pairs:] = across
        weights = jnp.concatenate([(same + 2.0 * upper).astype(BF16), (2.0 * lower).astype(BF16)], axis=1)
        chunks[start : start + step] = dot(weights, blocks).astype(BF16).reshape(step, CAP, WIDTH)
        told = dot(asked, straight + across, NT)
        tile = (start + iota((1, step * CAP), 1) // CAP).astype(F32)
        first = jnp.zeros((1, step * CAP), F32)
        second = jnp.zeros((1, step * CAP), F32)
        for k in range(targets):
            hit = told[3 * k : 3 * k + 1] == tile
            first = first + jnp.where(hit, told[3 * k + 1 : 3 * k + 2], 0.0)
            second = second + jnp.where(hit, told[3 * k + 2 : 3 * k + 3], 0.0)
        column_tile = jnp.floor(second * (1.0 / GROUPS))
        half = jnp.floor(column_tile * 0.5)
        key = 16.0 * (half + 1.0) * (column_tile - half) + first
        code = key * GROUPS + (second - column_tile * GROUPS)
        for n in range(step * CAP // LANES):
            codes[start * CAP // LANES + n] = code[:, n * LANES : (n + 1) * LANES]


INNER = [(j % 4, (j // 4 + j) % 4, (j + 3 * (j // 4)) % 4) for j in range(BATCH)]


def places(b, gx, gy, outward):
    core = gy % 2
    other = (core + b % 2) % 2
    turn = 1 + 2 * core if outward else 3 - 2 * other
    x, y, z = gx // 4, gx % 4, gy // 2
    xs = [((x + d * turn) % 4) * 4 for d in range(4)]
    ys = [(y + d * turn) % 4 for d in range(4)]
    zs = [((z + (b // 2 + d) * turn) % 4) * 2 + other for d in range(4)]
    return [(xs[dx] + ys[dy], zs[dz]) for dx, dy, dz in INNER]


def remote(source, target, send_sem, recv_sem, place):
    return pltpu.make_async_remote_copy(
        src_ref=source, dst_ref=target, send_sem=send_sem, recv_sem=recv_sem, device_id=place, device_id_type=MESH,
    )


def mask_basis(basis, extent):
    functions, cells = basis.shape
    atoms = functions // NB
    extent = extent.astype(F32)
    own = ones_where(iota((functions, atoms), 0) // NB == iota((functions, atoms), 1)).astype(BF16)
    half = (iota((functions, LANES), 1) // CY).astype(F32)
    low = dot(own, jnp.broadcast_to(extent[0:1], (LANES, atoms)).astype(BF16), NT) - half
    high = dot(own, jnp.broadcast_to(extent[1:2], (LANES, atoms)).astype(BF16), NT) - half
    for c in range(cells // LANES):
        row = float(c * (LANES // CY))
        inside = ones_where((low <= row) & (high > row)).astype(BF16)
        lanes = slice(c * LANES, (c + 1) * LANES)
        basis[:, lanes] = basis[:, lanes] * inside


def fill_spread(spread, fold):
    wide = 2 * LANES
    for c in range(NB // 2):
        row, lane = iota((WIDTH, wide), 0), iota((WIDTH, wide), 1)
        same = (row // NB == 2 * c + lane // LANES) & (row % NB == lane % NB)
        spread[:, c * wide : (c + 1) * wide] = ones_where(same).astype(BF16)
        row, lane = iota((wide, WIDTH), 0), iota((wide, WIDTH), 1)
        same = (lane // NB == 2 * c + row // LANES) & (lane % NB == row % NB)
        fold[c * wide : (c + 1) * wide, :] = ones_where(same).astype(BF16)


def collect(recv, got, b, lane_group, spread, gathered, keys, groups):
    entries = BATCH * CAP
    codes = got[pl.ds(b * BATCH, BATCH), 0, :]
    key = jnp.floor(codes * (1.0 / GROUPS))
    group = (codes - key * GROUPS).astype(BF16)
    coarse = jnp.floor(key * (1.0 / 16.0)) * 16.0
    fine = (key - coarse).astype(BF16)
    coarse = coarse.astype(BF16)
    row, lane = iota((LANES, entries), 0), iota((LANES, entries), 1)
    own = ones_where(row == lane_group * CAP + lane % CAP).astype(BF16)
    keyed = dot(fine, own) + dot(coarse, own)
    keyed = jnp.where(iota((BATCH, entries), 0) == iota((BATCH, entries), 1) // CAP, keyed, 0.0)
    key_row = jnp.sum(keyed, axis=0, keepdims=True).astype(I32)
    key_rows = gathered.shape[0]
    onehot = ones_where(iota((key_rows, entries), 0) == key_row).astype(BF16)
    slot = ones_where(iota((entries, BATCH), 0) // CAP == iota((entries, BATCH), 1)).astype(BF16)
    row, lane = iota((entries, LANES), 0), iota((entries, LANES), 1)
    own = lane == lane_group * CAP + row % CAP
    every = jnp.ones((LANES, LANES), BF16)
    parts = [jnp.where(own, dot(slot, part), 0.0).astype(BF16) for part in (fine, coarse, group)]
    key = dot(parts[0], every) + dot(parts[1], every)
    group = dot(parts[2], every)
    here = pl.ds(pl.multiple_of(b * entries, entries), entries)
    keys[here, :] = key
    groups[here, :] = group
    blocks = recv[pl.ds(b * BATCH, BATCH)].reshape(entries, WIDTH)
    wide = 2 * LANES
    inside = (iota((entries, wide), 1) % LANES // NB).astype(F32) == jnp.concatenate([group, group], axis=1)
    for c in range(NB // 2):
        lanes = slice(c * wide, (c + 1) * wide)
        spaced = jnp.where(inside, dot(blocks, spread[:, lanes]), 0.0).astype(BF16)
        gathered[:, lanes] = gathered[:, lanes] + dot(onehot, spaced)


def pick(b, picked, keys, groups, fold, spaced, back):
    entries = BATCH * CAP
    here = pl.ds(pl.multiple_of(b * entries, entries), entries)
    key, group = keys[here, :], groups[here, :]
    lane = iota((entries, LANES), 1).astype(F32)
    onehot = jnp.concatenate(
        [ones_where(lane + float(n * LANES) == key).astype(BF16) for n in range(picked.shape[0] // LANES)], axis=1
    )
    wide = 2 * LANES
    inside = (iota((entries, wide), 1) % LANES // NB).astype(F32) == jnp.concatenate([group, group], axis=1)
    for c in range(NB // 2):
        lanes = slice(c * wide, (c + 1) * wide)
        spaced[:, lanes] = jnp.where(inside, dot(onehot, picked[:, lanes]), 0.0).astype(BF16)
    blocks = dot(spaced[...], fold[...]).astype(BF16)
    back[pl.ds(b * BATCH, BATCH)] = blocks.reshape(BATCH, CAP, WIDTH)


def potential_of(charge, below, above, left, right):
    rows = charge.shape[0]
    lane = iota((rows, LANES), 1)
    row = iota((rows, LANES), 0)
    swapped = pltpu.roll(charge, CY, 1)
    first_of_above = pltpu.roll(above, CY, 1)[0:1]
    last_of_below = pltpu.roll(below, CY, 1)[rows - 1 : rows]
    up = jnp.where(row == rows - 1, first_of_above, pltpu.roll(swapped, rows - 1, 0))
    next_x = jnp.where(lane < CY, swapped, up)
    down = jnp.where(row == 0, last_of_below, pltpu.roll(swapped, 1, 0))
    last_x = jnp.where(lane < CY, down, swapped)
    next_y = jnp.where(lane % CY == CY - 1, pltpu.roll(right, CY - 1, 1), pltpu.roll(charge, LANES - 1, 1))
    last_y = jnp.where(lane % CY == 0, pltpu.roll(left, LANES - CY + 1, 1), pltpu.roll(charge, 1, 1))
    slope_x = 0.5 * (next_x - last_x)
    slope_y = 0.5 * (next_y - last_y)
    return charge * lax.rsqrt(
        1.0 + charge * charge + gradient_weight * (slope_x * slope_x + slope_y * slope_y)
    )


def whole_kernel(
    tiles_hbm, slots_hbm, sizes_hbm, density_hbm, extent_hbm, basis_hbm,
    out_hbm, potential_hbm,
    tiles_ref, slots_ref, sizes_ref, density_ref, extent_ref, out_ref, potential_ref,
    basis, weighted, chunks, recv, back, returned, codes, got, picks, picks_turned, spread, fold, gathered, keys, groups,
    square, matrix, picked, spaced, charge, halo,
    send_sems, recv_sems, code_sems, return_sem, halo_send, halo_recv, local_sem,
):
    devices = chunks.shape[0]
    functions, cells = basis.shape
    atoms = functions // NB
    column_tiles = functions // LANES
    batches = devices // BATCH
    gx, gy = lax.axis_index("gx"), lax.axis_index("gy")
    me = gx * 8 + gy
    load = pltpu.make_async_copy(basis_hbm, basis, local_sem.at[0])
    inputs = [
        pltpu.make_async_copy(source, target, local_sem.at[1 + n])
        for n, (source, target) in enumerate((
            (tiles_hbm, tiles_ref), (slots_hbm, slots_ref), (sizes_hbm, sizes_ref), (density_hbm, density_ref),
            (extent_hbm, extent_ref),
        ))
    ]
    for copy in inputs:
        copy.start()
    load.start()
    barrier = pltpu.get_barrier_semaphore()

    def greet(b, carry):
        for j, place in enumerate(places(b, gx, gy, True)):
            def signal():
                pl.semaphore_signal(barrier, inc=1, device_id=place, device_id_type=MESH)

            if j == 0:
                pl.when(b > 0)(signal)
            else:
                signal()
        return carry

    lax.fori_loop(0, batches, greet, 0)
    for copy in inputs:
        copy.wait()
    mask = size_mask_of(sizes_ref[...])
    masked = jnp.where(mask, density_ref[...].astype(F32), 0.0).astype(BF16)
    pack(tiles_ref[...], slots_ref, masked, chunks, codes, picks)
    pl.semaphore_wait(barrier, devices - 1)
    tiles_per_row = LANES // CAP
    pltpu.make_async_copy(codes.at[me // tiles_per_row], got.at[0], code_sems.at[0]).start()
    pltpu.make_async_copy(chunks.at[me], recv.at[0], recv_sems.at[0]).start()

    def push(b, carry):
        for j, (px, py) in enumerate(places(b, gx, gy, True)):
            def start():
                slot = b * BATCH + j
                remote(codes.at[px], got.at[slot], send_sems.at[0], code_sems.at[b], (px, py)).start()
                remote(chunks.at[px * 8 + py], recv.at[slot], send_sems.at[1], recv_sems.at[b], (px, py)).start()

            if j == 0:
                pl.when(b > 0)(start)
            else:
                start()
        return carry

    lax.fori_loop(0, batches, push, 0)
    pairs = density_ref.shape[0]
    for half in range(2):
        for n in range(devices * CAP // 512):
            part = picks[n * 512 : (n + 1) * 512, half * pairs : (half + 1) * pairs].astype(F32)
            lanes = half * devices * CAP + n * 512
            picks_turned[:, lanes : lanes + 512] = jnp.transpose(part).astype(BF16)
    square[...] = jnp.zeros_like(square)
    fill_spread(spread, fold)
    gathered[...] = jnp.zeros_like(gathered)
    picked[...] = jnp.zeros_like(picked)
    load.wait()
    mask_basis(basis, extent_ref[...])

    def arrive(b, carry):
        slots = pl.ds(b * BATCH, BATCH)
        remote(got.at[slots], got.at[slots], send_sems.at[0], code_sems.at[b], (gx, gy)).wait_recv()
        remote(recv.at[slots], recv.at[slots], send_sems.at[1], recv_sems.at[b], (gx, gy)).wait_recv()
        collect(recv, got, b, gy, spread, gathered, keys, groups)
        return carry

    lax.fori_loop(0, batches, arrive, 0)
    for c in range(column_tiles):
        low = key_offset(c)
        count = GROUPS * (c + 1)
        for i in range(NB):
            block = gathered[low : low + count, i * LANES : (i + 1) * LANES]
            square[c, pl.ds(i, count, stride=NB), :] = block
        matrix[:, c * LANES : (c + 1) * LANES] = square[c].astype(BF16)
    step = 2 * LANES
    part = 3 * LANES
    for c in range(cells // step):
        columns = basis[:, c * step : (c + 1) * step]
        total = jnp.zeros((1, step), F32)
        for low in range(0, functions, part):
            product = dot(matrix[low : low + part, low:], columns[low:])
            product = product * columns[low : low + part].astype(F32)
            total = total + jnp.sum(product, axis=0, keepdims=True)
        charge[2 * c : 2 * c + 1, :] = total[:, :LANES]
        charge[2 * c + 1 : 2 * c + 2, :] = total[:, LANES:]
    edges = [
        remote(charge, halo.at[n], halo_send.at[n], halo_recv.at[n], place)
        for n, place in enumerate(
            (((gx + 1) % 16, gy), ((gx + 15) % 16, gy), (gx, (gy + 7) % 8), (gx, (gy + 1) % 8))
        )
    ]
    for copy in edges:
        copy.start()
    for copy in edges:
        copy.wait()
    potential = potential_of(charge[...], halo[0], halo[1], halo[3], halo[2])
    for half in range(2):
        rows = potential if half == 0 else pltpu.roll(potential, CY, 1)
        potential_ref[pl.ds(half, CX // 2, stride=2), :] = rows[:, :CY]
    potential_out = pltpu.make_async_copy(potential_ref, potential_hbm, local_sem.at[1])
    potential_out.start()
    for c in range(cells // LANES):
        lanes = slice(c * LANES, (c + 1) * LANES)
        weighted[:, lanes] = (basis[:, lanes].astype(F32) * potential[c : c + 1]).astype(BF16)
    for start in range(0, column_tiles, 2):
        stop = min(start + 2, column_tiles)
        rows = weighted[start * LANES : stop * LANES, :]
        high = stop * LANES
        product = dot(basis[:high, :], rows, NT) * float(cells) ** -0.5
        for c in range(start, stop):
            square[c, :high, :] = product[:, (c - start) * LANES : (c - start + 1) * LANES]
            low = key_offset(c)
            count = GROUPS * (c + 1)
            for i in range(NB):
                block = square[c, pl.ds(i, count, stride=NB), :]
                picked[low : low + count, i * LANES : (i + 1) * LANES] = block.astype(BF16)
    keep = pltpu.make_async_copy(back.at[0], returned.at[me], return_sem)

    def give(b, carry):
        pick(b, picked, keys, groups, fold, spaced, back)

        for j, place in enumerate(places(b, gx, gy, False)):
            def start():
                remote(back.at[b * BATCH + j], returned.at[me], send_sems.at[2], return_sem, place).start()

            if j == 0:
                pl.when(b > 0)(start)
                pl.when(b == 0)(keep.start)
            else:
                start()
        return carry

    lax.fori_loop(0, batches, give, 0)
    remote(returned, returned, send_sems.at[2], return_sem, (gx, gy)).wait_recv()
    blocks = returned[...].reshape(devices * CAP, WIDTH)
    blocks = jnp.concatenate([blocks, dot(blocks, turned()).astype(BF16)], axis=0)
    out_ref[...] = jnp.where(size_mask_of(sizes_ref[...]), dot(picks_turned[...], blocks), 0.0)
    out = pltpu.make_async_copy(out_ref, out_hbm, local_sem.at[2])
    out.start()
    out.wait()
    potential_out.wait()
    others = pl.ds(0, devices - 1)
    remote(got.at[others], got.at[others], send_sems.at[0], code_sems.at[0], (gx, gy)).wait_send()
    remote(chunks.at[others], recv.at[others], send_sems.at[1], recv_sems.at[0], (gx, gy)).wait_send()
    remote(back.at[others], returned.at[others], send_sems.at[2], return_sem, (gx, gy)).wait_send()


def finish_kernel(summed, field, out, potential, sems):
    copies = [
        pltpu.make_async_copy(source, target, sems.at[n])
        for n, (source, target) in enumerate(((summed, out), (field, potential)))
    ]
    for copy in copies:
        copy.start()
    for copy in copies:
        copy.wait()


ANY_SPEC = pl.BlockSpec(memory_space=pl.ANY)
DMA = pltpu.SemaphoreType.DMA


def shards(density, pair_tiles, pair_slots, pair_sizes, basis_table, tile_extent):
    devices = lax.axis_size("gx") * lax.axis_size("gy")
    pairs, targets = pair_tiles.shape
    atoms = tile_extent.shape[2]
    functions, cells = basis_table.shape[1:]
    rows = cells // LANES
    key_rows = key_offset(functions // LANES)
    chunk = pltpu.VMEM((devices, CAP, WIDTH), BF16)
    entries = devices * CAP
    spaced = NB * LANES
    results = pl.pallas_call(
        whole_kernel,
        name="whole",
        out_shape=[
            jax.ShapeDtypeStruct((pairs, WIDTH), F32),
            jax.ShapeDtypeStruct((CX, CY), F32),
        ],
        in_specs=[ANY_SPEC] * 6,
        out_specs=[ANY_SPEC] * 2,
        scratch_shapes=[
            pltpu.VMEM((targets, pairs), I32),
            pltpu.VMEM((targets, 2, pairs), I32),
            pltpu.VMEM((2, pairs), I32),
            pltpu.VMEM((pairs, WIDTH), BF16),
            pltpu.VMEM((2, atoms), I32),
            pltpu.VMEM((pairs, WIDTH), F32),
            pltpu.VMEM((CX, CY), F32),
            pltpu.VMEM((functions, cells), BF16),
            pltpu.VMEM((functions, cells), BF16),
            chunk,
            chunk,
            chunk,
            chunk,
            pltpu.VMEM((devices * CAP // LANES, 1, LANES), F32),
            pltpu.VMEM((devices, 1, LANES), F32),
            pltpu.VMEM((entries, 2 * pairs), BF16),
            pltpu.VMEM((pairs, 2 * entries), BF16),
            pltpu.VMEM((WIDTH, spaced), BF16),
            pltpu.VMEM((spaced, WIDTH), BF16),
            pltpu.VMEM((key_rows, spaced), F32),
            pltpu.VMEM((entries, LANES), F32),
            pltpu.VMEM((entries, LANES), F32),
            pltpu.VMEM((functions // LANES, functions, LANES), F32),
            pltpu.VMEM((functions, functions), BF16),
            pltpu.VMEM((-(-key_rows // LANES) * LANES, spaced), BF16),
            pltpu.VMEM((BATCH * CAP, spaced), BF16),
            pltpu.VMEM((rows, LANES), F32),
            pltpu.VMEM((4, rows, LANES), F32),
            DMA((3,)),
            DMA((devices // BATCH,)),
            DMA((devices // BATCH,)),
            DMA,
            DMA((4,)),
            DMA((4,)),
            DMA((6,)),
        ],
        compiler_params=pltpu.CompilerParams(
            vmem_limit_bytes=VMEM_BYTES, collective_id=1, has_side_effects=True
        ),
    )(pair_tiles.T, pair_slots.transpose(1, 2, 0), pair_sizes.T, density, tile_extent[0], basis_table[0])
    return tuple(pl.pallas_call(
        finish_kernel,
        name="finish",
        out_shape=[jax.ShapeDtypeStruct(result.shape, result.dtype) for result in results],
        in_specs=[ANY_SPEC] * 2,
        out_specs=[ANY_SPEC] * 2,
        scratch_shapes=[DMA((2,))],
        compiler_params=pltpu.CompilerParams(vmem_limit_bytes=VMEM_BYTES),
    )(*results))


def solution(mesh):
    in_specs = (
        P(("gx", "gy"), None),
        P(("gx", "gy"), None),
        P(("gx", "gy"), None, None),
        P(("gx", "gy"), None),
        P(("gx", "gy"), None, None),
        P(("gx", "gy"), None, None),
    )
    out_specs = (P(("gx", "gy"), None), P("gx", "gy"))
    return jax.shard_map(shards, mesh=mesh, in_specs=in_specs, out_specs=out_specs, check_vma=False)
```

```python
import functools

import jax
import jax.numpy as jnp
import numpy as np
from jax import lax
from jax.experimental import pallas as pl
from jax.experimental.pallas import tpu as pltpu
from jax.sharding import PartitionSpec as P

NB = 16
CX = 32
CY = 64
LANES = 128
GROUPS = LANES // NB
WIDTH = NB * NB
CAP = 16
BATCH = 16
STEP = 32
MESH = pl.DeviceIdType.MESH
F32 = jnp.float32
BF16 = jnp.bfloat16
I32 = jnp.int32
VMEM_BYTES = 60 * 1024 * 1024
gradient_weight = 1.0
NT = (((1,), (1,)), ((), ()))


def iota(shape, dim):
    return lax.broadcasted_iota(I32, shape, dim)


def dot(a, b, dims=(((1,), (0,)), ((), ()))):
    return lax.dot_general(a, b, dims, preferred_element_type=F32)


def ones_where(condition):
    return jnp.where(condition, 1.0, 0.0)


def size_mask_of(sizes, eye):
    pairs = sizes.shape[1]
    wide = sizes.astype(F32)
    first = dot(eye, jnp.broadcast_to(wide[0:1], (WIDTH, pairs)).astype(BF16), NT)
    second = dot(eye, jnp.broadcast_to(wide[1:2], (WIDTH, pairs)).astype(BF16), NT)
    lane = iota((pairs, WIDTH), 1)
    row = (lane // NB).astype(F32)
    col = (lane % NB).astype(F32)
    return (row < first) & (col < second)


def key_offset(column_tile):
    half = column_tile // 2
    return 16 * (half + 1) * (half + column_tile % 2)


def plan(tiles, slots_ref, tile_id, before, marks):
    targets, pairs = tiles.shape
    devices = marks.shape[0]
    chosen = jnp.zeros((devices, pairs), F32)
    kind = jnp.zeros((devices, pairs), F32)
    asked = []
    for k in range(targets):
        mark = ones_where(tiles[k : k + 1] == tile_id)
        slots = slots_ref[k].astype(F32)
        first, second = slots[0:1], slots[1:2]
        chosen = chosen + mark
        kind = kind + mark * (ones_where(first < second) + 2.0 * ones_where(first > second))
        asked += [tiles[k : k + 1].astype(F32), jnp.minimum(first, second), jnp.maximum(first, second)]
    rank = dot(chosen.astype(BF16), before)
    marks[...] = jnp.where(chosen > 0.5, rank * 4.0 + kind, -4.0)
    return jnp.concatenate(asked + [jnp.zeros((16 - 3 * targets, pairs), F32)], axis=0).astype(BF16)


def pack(b, tile, asked, blocks, marks, chunks, codes, picks):
    pairs = marks.shape[1]
    entries = STEP * CAP
    own = (4 * (iota((entries, pairs), 0) % CAP)).astype(F32)
    rows = jnp.broadcast_to(marks[pl.ds(b * STEP, STEP), :][:, None, :], (STEP, CAP, pairs))
    rows = rows.reshape(entries, pairs) - own
    same, upper, lower = ones_where(rows == 0.0), ones_where(rows == 1.0), ones_where(rows == 2.0)
    straight = (same + upper).astype(BF16)
    across = lower.astype(BF16)
    here = pl.ds(pl.multiple_of(b * entries, entries), entries)
    picks[here, :pairs] = straight
    picks[here, pairs:] = across
    weights = jnp.concatenate([(same + 2.0 * upper).astype(BF16), (2.0 * lower).astype(BF16)], axis=1)
    chunks[pl.ds(b * STEP, STEP)] = dot(weights, blocks).astype(BF16).reshape(STEP, CAP, WIDTH)
    told = dot(asked, straight + across, NT)
    first = jnp.zeros((1, entries), F32)
    second = jnp.zeros((1, entries), F32)
    for k in range(asked.shape[0] // 3):
        hit = told[3 * k : 3 * k + 1] == tile
        first = first + jnp.where(hit, told[3 * k + 1 : 3 * k + 2], 0.0)
        second = second + jnp.where(hit, told[3 * k + 2 : 3 * k + 3], 0.0)
    column_tile = jnp.floor(second * (1.0 / GROUPS))
    half = jnp.floor(column_tile * 0.5)
    key = 16.0 * (half + 1.0) * (column_tile - half) + first
    code = key * GROUPS + (second - column_tile * GROUPS)
    for n in range(entries // LANES):
        codes[b * (entries // LANES) + n] = code[:, n * LANES : (n + 1) * LANES]


INNER = [(j % 4, (j // 4 + j) % 4, (j + 3 * (j // 4)) % 4) for j in range(BATCH)]


def places(b, gx, gy, outward):
    core = gy % 2
    other = (core + b % 2) % 2
    turn = 1 + 2 * core if outward else 3 - 2 * other
    x, y, z = gx // 4, gx % 4, gy // 2
    xs = [((x + d * turn) % 4) * 4 for d in range(4)]
    ys = [(y + d * turn) % 4 for d in range(4)]
    zs = [((z + (b // 2 + d) * turn) % 4) * 2 + other for d in range(4)]
    return [(xs[dx] + ys[dy], zs[dz]) for dx, dy, dz in INNER]


def tile_of(slot, gx, gy):
    b, j = slot >> 4, slot & 15
    dx, dy, dz = j & 3, ((j >> 2) + j) & 3, ((b >> 1) + j + 3 * (j >> 2)) & 3
    core = gy % 2
    turn = 1 + 2 * core
    px = ((gx // 4 + dx * turn) & 3) * 4 + ((gx % 4 + dy * turn) & 3)
    return px * 8 + ((gy // 2 + dz * turn) & 3) * 2 + ((core + b) & 1)


def remote(source, target, send_sem, recv_sem, place):
    return pltpu.make_async_remote_copy(
        src_ref=source, dst_ref=target, send_sem=send_sem, recv_sem=recv_sem, device_id=place, device_id_type=MESH,
    )


def mask_basis(basis, extent):
    functions, cells = basis.shape
    atoms = functions // NB
    extent = extent.astype(F32)
    own = ones_where(iota((functions, atoms), 0) // NB == iota((functions, atoms), 1)).astype(BF16)
    half = (iota((functions, LANES), 1) // CY).astype(F32)
    low = dot(own, jnp.broadcast_to(extent[0:1], (LANES, atoms)).astype(BF16), NT) - half
    high = dot(own, jnp.broadcast_to(extent[1:2], (LANES, atoms)).astype(BF16), NT) - half
    for c in range(cells // LANES):
        row = c * (LANES // CY)
        inside = low <= float(row) if row < CX // 2 else high > float(row)
        lanes = slice(c * LANES, (c + 1) * LANES)
        basis[:, lanes] = basis[:, lanes] * ones_where(inside).astype(BF16)


def constants():
    row, lane = np.arange(WIDTH)[:, None], np.arange(WIDTH)[None, :]
    before = row < lane
    turned = (row // NB == lane % NB) & (row % NB == lane // NB)
    wide = np.arange(NB * LANES)[None, :]
    spread = (row // NB == wide // LANES) & (row % NB == wide % NB)
    square = np.concatenate([before, turned, row == lane], axis=1)
    return [np.asarray(x, np.float32) for x in (square, spread, spread.T)]


def collect(recv, got, b, spread, gathered, keys, groups):
    entries = STEP * CAP
    codes = got[pl.ds(b * STEP, STEP), 0, :]
    key = jnp.floor(codes * (1.0 / GROUPS))
    group = (codes - key * GROUPS).astype(BF16)
    coarse = jnp.floor(key * (1.0 / 16.0)) * 16.0
    fine = (key - coarse).astype(BF16)
    coarse = coarse.astype(BF16)
    row, lane = iota((LANES, entries), 0), iota((LANES, entries), 1)
    own = ones_where(row == lane % LANES).astype(BF16)
    keyed = dot(fine, own) + dot(coarse, own)
    keyed = jnp.where(iota((STEP, entries), 0) == iota((STEP, entries), 1) // CAP, keyed, 0.0)
    key_row = jnp.sum(keyed, axis=0, keepdims=True).astype(I32)
    key_rows = gathered.shape[0]
    onehot = ones_where(iota((key_rows, entries), 0) == key_row).astype(BF16)
    slot = ones_where(iota((entries, STEP), 0) // CAP == iota((entries, STEP), 1)).astype(BF16)
    row, lane = iota((entries, LANES), 0), iota((entries, LANES), 1)
    own = lane == row % LANES
    every = jnp.ones((LANES, LANES), BF16)
    parts = [jnp.where(own, dot(slot, part), 0.0).astype(BF16) for part in (fine, coarse, group)]
    key = dot(parts[0], every) + dot(parts[1], every)
    group = dot(parts[2], every)
    here = pl.ds(pl.multiple_of(b * entries, entries), entries)
    keys[here, :] = key
    groups[here, :] = group
    blocks = recv[pl.ds(b * STEP, STEP)].reshape(entries, WIDTH)
    wide = 2 * LANES
    inside = (iota((entries, wide), 1) % LANES // NB).astype(F32) == jnp.concatenate([group, group], axis=1)
    for c in range(NB // 2):
        lanes = slice(c * wide, (c + 1) * wide)
        spaced = jnp.where(inside, dot(blocks, spread[:, lanes]), 0.0).astype(BF16)
        gathered[:, lanes] = gathered[:, lanes] + dot(onehot, spaced)


def pick(b, picked, keys, groups, fold, spaced, back):
    entries = STEP * CAP
    here = pl.ds(pl.multiple_of(b * entries, entries), entries)
    key, group = keys[here, :], groups[here, :]
    lane = iota((entries, LANES), 1).astype(F32)
    onehot = jnp.concatenate(
        [ones_where(lane + float(n * LANES) == key).astype(BF16) for n in range(picked.shape[0] // LANES)], axis=1
    )
    wide = 2 * LANES
    inside = (iota((entries, wide), 1) % LANES // NB).astype(F32) == jnp.concatenate([group, group], axis=1)
    for c in range(NB // 2):
        lanes = slice(c * wide, (c + 1) * wide)
        spaced[:, lanes] = jnp.where(inside, dot(onehot, picked[:, lanes]), 0.0).astype(BF16)
    blocks = dot(spaced[...], fold[...]).astype(BF16)
    back[pl.ds(b * STEP, STEP)] = blocks.reshape(STEP, CAP, WIDTH)


def potential_of(charge, below, above, left, right):
    rows = charge.shape[0]
    lane = iota((rows, LANES), 1)
    row = iota((rows, LANES), 0)
    swapped = pltpu.roll(charge, CY, 1)
    first_of_above = pltpu.roll(above, CY, 1)[0:1]
    last_of_below = pltpu.roll(below, CY, 1)[rows - 1 : rows]
    up = jnp.where(row == rows - 1, first_of_above, pltpu.roll(swapped, rows - 1, 0))
    next_x = jnp.where(lane < CY, swapped, up)
    down = jnp.where(row == 0, last_of_below, pltpu.roll(swapped, 1, 0))
    last_x = jnp.where(lane < CY, down, swapped)
    next_y = jnp.where(lane % CY == CY - 1, pltpu.roll(right, CY - 1, 1), pltpu.roll(charge, LANES - 1, 1))
    last_y = jnp.where(lane % CY == 0, pltpu.roll(left, LANES - CY + 1, 1), pltpu.roll(charge, 1, 1))
    slope_x = 0.5 * (next_x - last_x)
    slope_y = 0.5 * (next_y - last_y)
    return charge * lax.rsqrt(
        1.0 + charge * charge + gradient_weight * (slope_x * slope_x + slope_y * slope_y)
    )


def whole_kernel(
    tiles_hbm, slots_hbm, sizes_hbm, density_hbm, extent_hbm, basis_hbm, ones_hbm, spread_hbm, fold_hbm,
    out_hbm, potential_hbm,
    tiles_ref, slots_ref, sizes_ref, density_ref, extent_ref, ones_ref, spread_ref, fold_ref, out_ref, potential_ref,
    basis, weighted, chunks, recv, back, returned, codes, got, marks, picks, picks_turned, spread, fold, gathered, keys, groups,
    square, matrix, picked, spaced, charge, halo,
    send_sems, recv_sems, code_sems, return_sem, halo_send, halo_recv, local_sem,
):
    devices = chunks.shape[0]
    functions, cells = basis.shape
    atoms = functions // NB
    column_tiles = functions // LANES
    batches = devices // BATCH
    gx, gy = lax.axis_index("gx"), lax.axis_index("gy")
    load = pltpu.make_async_copy(basis_hbm, basis, local_sem.at[0])
    inputs = [
        pltpu.make_async_copy(source, target, local_sem.at[1 + n])
        for n, (source, target) in enumerate((
            (tiles_hbm, tiles_ref), (slots_hbm, slots_ref), (sizes_hbm, sizes_ref), (density_hbm, density_ref),
            (ones_hbm, ones_ref), (extent_hbm, extent_ref), (spread_hbm, spread_ref), (fold_hbm, fold_ref),
        ))
    ]
    for copy in inputs:
        copy.start()
    load.start()
    barrier = pltpu.get_barrier_semaphore()

    def greet(b, carry):
        for j, place in enumerate(places(b, gx, gy, True)):
            def signal():
                pl.semaphore_signal(barrier, inc=1, device_id=place, device_id_type=MESH)

            if j == 0:
                pl.when(b > 0)(signal)
            else:
                signal()
        return carry

    lax.fori_loop(0, batches, greet, 0)
    gathered[...] = jnp.zeros_like(gathered)
    for c in range(column_tiles):
        low, high = (c + 1) * LANES, (c // 3 + 1) * 3 * LANES
        if low < high:
            square[c, low:high, :] = jnp.zeros((high - low, LANES), F32)
        low, high = key_offset(c) + GROUPS * (c + 1), key_offset(c + 1)
        high = picked.shape[0] if c + 1 == column_tiles else high
        if low < high:
            picked[low:high, :] = jnp.zeros((high - low, picked.shape[1]), BF16)
    for copy in inputs[:5]:
        copy.wait()
    pairs = density_ref.shape[0]
    before, turned, eye = (ones_ref[:, n * WIDTH : (n + 1) * WIDTH].astype(BF16) for n in range(3))
    mask = size_mask_of(sizes_ref[...], eye)
    masked = jnp.where(mask, density_ref[...].astype(F32), 0.0).astype(BF16)
    blocks = jnp.concatenate([masked, dot(masked, turned).astype(BF16)], axis=0)
    asked = plan(tiles_ref[...], slots_ref, tile_of(iota((devices, 1), 0), gx, gy), before, marks)
    pl.semaphore_wait(barrier, devices - 1)
    rows_per_batch = BATCH * CAP // LANES

    def push(b, carry):
        for j, place in enumerate(places(b, gx, gy, True)):
            slot = b * BATCH + j
            row = b * rows_per_batch + j * CAP // LANES

            def start():
                remote(codes.at[row], got.at[slot], send_sems.at[0], code_sems.at[b], place).start()
                remote(chunks.at[slot], recv.at[slot], send_sems.at[1], recv_sems.at[b], place).start()

            def keep():
                pltpu.make_async_copy(codes.at[0], got.at[0], code_sems.at[0]).start()
                pltpu.make_async_copy(chunks.at[0], recv.at[0], recv_sems.at[0]).start()

            if j == 0:
                pl.when(b > 0)(start)
                pl.when(b == 0)(keep)
            else:
                start()
        return carry

    steps = devices // STEP
    per_step = STEP // BATCH

    def fill(n, carry):
        tile = tile_of(n * STEP + iota((1, STEP * CAP), 1) // CAP, gx, gy).astype(F32)
        pack(n, tile, asked, blocks, marks, chunks, codes, picks)
        return lax.fori_loop(n * per_step, (n + 1) * per_step, push, carry)

    lax.fori_loop(0, steps, fill, 0)
    for copy in inputs[5:]:
        copy.wait()
    spread[...] = spread_ref[...].astype(BF16)
    fold[...] = fold_ref[...].astype(BF16)
    load.wait()
    mask_basis(basis, extent_ref[...])

    def arrive(n, carry):
        for k in range(per_step):
            b = n * per_step + k
            slots = pl.ds(b * BATCH, BATCH)
            remote(got.at[slots], got.at[slots], send_sems.at[0], code_sems.at[b], (gx, gy)).wait_recv()
            remote(recv.at[slots], recv.at[slots], send_sems.at[1], recv_sems.at[b], (gx, gy)).wait_recv()
        collect(recv, got, n, spread, gathered, keys, groups)
        return carry

    lax.fori_loop(0, steps, arrive, 0)
    for c in range(column_tiles):
        low = key_offset(c)
        count = GROUPS * (c + 1)
        for i in range(NB):
            block = gathered[low : low + count, i * LANES : (i + 1) * LANES]
            square[c, pl.ds(i, count, stride=NB), :] = block
        matrix[:, c * LANES : (c + 1) * LANES] = square[c].astype(BF16)
    step = 2 * LANES
    part = 3 * LANES
    for c in range(cells // step):
        columns = basis[:, c * step : (c + 1) * step]
        total = jnp.zeros((1, step), F32)
        for low in range(0, functions, part):
            product = dot(matrix[low : low + part, low:], columns[low:])
            product = product * columns[low : low + part].astype(F32)
            total = total + jnp.sum(product, axis=0, keepdims=True)
        charge[2 * c : 2 * c + 1, :] = total[:, :LANES]
        charge[2 * c + 1 : 2 * c + 2, :] = total[:, LANES:]
    edges = [
        remote(charge, halo.at[n], halo_send.at[n], halo_recv.at[n], place)
        for n, place in enumerate(
            (((gx + 1) % 16, gy), ((gx + 15) % 16, gy), (gx, (gy + 7) % 8), (gx, (gy + 1) % 8))
        )
    ]
    for copy in edges:
        copy.start()
    for copy in edges:
        copy.wait()
    potential = potential_of(charge[...], halo[0], halo[1], halo[3], halo[2])
    for half in range(2):
        rows = potential if half == 0 else pltpu.roll(potential, CY, 1)
        potential_ref[pl.ds(half, CX // 2, stride=2), :] = rows[:, :CY]
    potential_out = pltpu.make_async_copy(potential_ref, potential_hbm, local_sem.at[1])
    potential_out.start()
    for c in range(cells // LANES):
        lanes = slice(c * LANES, (c + 1) * LANES)
        weighted[:, lanes] = (basis[:, lanes].astype(F32) * potential[c : c + 1]).astype(BF16)
    for start in range(0, column_tiles, 2):
        stop = min(start + 2, column_tiles)
        rows = weighted[start * LANES : stop * LANES, :]
        high = stop * LANES
        product = dot(basis[:high, :], rows, NT) * float(cells) ** -0.5
        for c in range(start, stop):
            square[c, :high, :] = product[:, (c - start) * LANES : (c - start + 1) * LANES]
            low = key_offset(c)
            count = GROUPS * (c + 1)
            for i in range(NB):
                block = square[c, pl.ds(i, count, stride=NB), :]
                picked[low : low + count, i * LANES : (i + 1) * LANES] = block.astype(BF16)
    keep = pltpu.make_async_copy(back.at[0], returned.at[0], return_sem)

    def hand_back(b, carry):
        for j, place in enumerate(places(b, gx, gy, False)):
            slot = b * BATCH + j

            def start():
                remote(back.at[slot], returned.at[slot], send_sems.at[2], return_sem, place).start()

            if j == 0:
                pl.when(b > 0)(start)
                pl.when(b == 0)(keep.start)
            else:
                start()
        return carry

    def give(n, carry):
        pick(n, picked, keys, groups, fold, spaced, back)
        return lax.fori_loop(n * per_step, (n + 1) * per_step, hand_back, carry)

    lax.fori_loop(0, steps, give, 0)
    for half in range(2):
        for n in range(devices * CAP // 512):
            part = picks[n * 512 : (n + 1) * 512, half * pairs : (half + 1) * pairs].astype(F32)
            lanes = half * devices * CAP + n * 512
            picks_turned[:, lanes : lanes + 512] = jnp.transpose(part).astype(BF16)
    mask = size_mask_of(sizes_ref[...], eye)
    remote(returned, returned, send_sems.at[2], return_sem, (gx, gy)).wait_recv()
    blocks = returned[...].reshape(devices * CAP, WIDTH)
    blocks = jnp.concatenate([blocks, dot(blocks, turned).astype(BF16)], axis=0)
    out_ref[...] = jnp.where(mask, dot(picks_turned[...], blocks), 0.0)
    out = pltpu.make_async_copy(out_ref, out_hbm, local_sem.at[2])
    out.start()
    out.wait()
    potential_out.wait()
    others = pl.ds(0, devices - 1)
    remote(got.at[others], got.at[others], send_sems.at[0], code_sems.at[0], (gx, gy)).wait_send()
    remote(chunks.at[others], recv.at[others], send_sems.at[1], recv_sems.at[0], (gx, gy)).wait_send()
    remote(back.at[others], returned.at[others], send_sems.at[2], return_sem, (gx, gy)).wait_send()


def finish_kernel(summed, field, out, potential):
    out[...] = summed[...]
    potential[...] = field[...]


VMEM_SPEC = pl.BlockSpec(memory_space=pltpu.VMEM)
ANY_SPEC = pl.BlockSpec(memory_space=pl.ANY)
DMA = pltpu.SemaphoreType.DMA


def shards(density, pair_tiles, pair_slots, pair_sizes, basis_table, tile_extent):
    devices = lax.axis_size("gx") * lax.axis_size("gy")
    pairs, targets = pair_tiles.shape
    atoms = tile_extent.shape[2]
    functions, cells = basis_table.shape[1:]
    rows = cells // LANES
    key_rows = key_offset(functions // LANES)
    chunk = pltpu.VMEM((devices, CAP, WIDTH), BF16)
    entries = devices * CAP
    spaced = NB * LANES
    results = pl.pallas_call(
        whole_kernel,
        name="whole",
        out_shape=[
            jax.ShapeDtypeStruct((pairs, WIDTH), F32),
            jax.ShapeDtypeStruct((CX, CY), F32),
        ],
        in_specs=[ANY_SPEC] * 9,
        out_specs=[ANY_SPEC] * 2,
        scratch_shapes=[
            pltpu.VMEM((targets, pairs), I32),
            pltpu.VMEM((targets, 2, pairs), I32),
            pltpu.VMEM((2, pairs), I32),
            pltpu.VMEM((pairs, WIDTH), BF16),
            pltpu.VMEM((2, atoms), I32),
            pltpu.VMEM((WIDTH, 3 * WIDTH), F32),
            pltpu.VMEM((WIDTH, spaced), F32),
            pltpu.VMEM((spaced, WIDTH), F32),
            pltpu.VMEM((pairs, WIDTH), F32),
            pltpu.VMEM((CX, CY), F32),
            pltpu.VMEM((functions, cells), BF16),
            pltpu.VMEM((functions, cells), BF16),
            chunk,
            chunk,
            chunk,
            chunk,
            pltpu.VMEM((devices * CAP // LANES, 1, LANES), F32),
            pltpu.VMEM((devices, 1, LANES), F32),
            pltpu.VMEM((devices, pairs), F32),
            pltpu.VMEM((entries, 2 * pairs), BF16),
            pltpu.VMEM((pairs, 2 * entries), BF16),
            pltpu.VMEM((WIDTH, spaced), BF16),
            pltpu.VMEM((spaced, WIDTH), BF16),
            pltpu.VMEM((key_rows, spaced), F32),
            pltpu.VMEM((entries, LANES), F32),
            pltpu.VMEM((entries, LANES), F32),
            pltpu.VMEM((functions // LANES, functions, LANES), F32),
            pltpu.VMEM((functions, functions), BF16),
            pltpu.VMEM((-(-key_rows // LANES) * LANES, spaced), BF16),
            pltpu.VMEM((STEP * CAP, spaced), BF16),
            pltpu.VMEM((rows, LANES), F32),
            pltpu.VMEM((4, rows, LANES), F32),
            DMA((3,)),
            DMA((devices // BATCH,)),
            DMA((devices // BATCH,)),
            DMA,
            DMA((4,)),
            DMA((4,)),
            DMA((9,)),
        ],
        compiler_params=pltpu.CompilerParams(
            vmem_limit_bytes=VMEM_BYTES, collective_id=1, has_side_effects=True
        ),
    )(pair_tiles.T, pair_slots.transpose(1, 2, 0), pair_sizes.T, density, tile_extent[0], basis_table[0], *constants())
    return tuple(pl.pallas_call(
        finish_kernel,
        name="finish",
        out_shape=[jax.ShapeDtypeStruct(result.shape, result.dtype) for result in results],
        in_specs=[VMEM_SPEC] * 2,
        out_specs=[VMEM_SPEC] * 2,
        compiler_params=pltpu.CompilerParams(vmem_limit_bytes=VMEM_BYTES),
    )(*results))


def solution(mesh):
    in_specs = (
        P(("gx", "gy"), None),
        P(("gx", "gy"), None),
        P(("gx", "gy"), None, None),
        P(("gx", "gy"), None),
        P(("gx", "gy"), None, None),
        P(("gx", "gy"), None, None),
    )
    out_specs = (P(("gx", "gy"), None), P("gx", "gy"))
    return jax.shard_map(shards, mesh=mesh, in_specs=in_specs, out_specs=out_specs, check_vma=False)
```

```python
import functools

import jax
import jax.numpy as jnp
import numpy as np
from jax import lax
from jax.experimental import pallas as pl
from jax.experimental.pallas import tpu as pltpu
from jax.sharding import PartitionSpec as P

NB = 16
CX = 32
CY = 64
LANES = 128
GROUPS = LANES // NB
WIDTH = NB * NB
CAP = 16
BATCH = 16
STEP = 32
MESH = pl.DeviceIdType.MESH
F32 = jnp.float32
BF16 = jnp.bfloat16
I32 = jnp.int32
VMEM_BYTES = 60 * 1024 * 1024
gradient_weight = 1.0
NT = (((1,), (1,)), ((), ()))


def iota(shape, dim):
    return lax.broadcasted_iota(I32, shape, dim)


def dot(a, b, dims=(((1,), (0,)), ((), ()))):
    return lax.dot_general(a, b, dims, preferred_element_type=F32)


def ones_where(condition):
    return jnp.where(condition, 1.0, 0.0)


def size_mask_of(sizes, eye):
    pairs = sizes.shape[1]
    wide = sizes.astype(F32)
    first = dot(eye, jnp.broadcast_to(wide[0:1], (WIDTH, pairs)).astype(BF16), NT)
    second = dot(eye, jnp.broadcast_to(wide[1:2], (WIDTH, pairs)).astype(BF16), NT)
    lane = iota((pairs, WIDTH), 1)
    row = (lane // NB).astype(F32)
    col = (lane % NB).astype(F32)
    return (row < first) & (col < second)


def key_offset(column_tile):
    half = column_tile // 2
    return 16 * (half + 1) * (half + column_tile % 2)


def plan(tiles, slots_ref, tile_id, before, marks):
    targets, pairs = tiles.shape
    devices = marks.shape[0]
    chosen = jnp.zeros((devices, pairs), F32)
    kind = jnp.zeros((devices, pairs), F32)
    asked = []
    for k in range(targets):
        mark = ones_where(tiles[k : k + 1] == tile_id)
        slots = slots_ref[k].astype(F32)
        first, second = slots[0:1], slots[1:2]
        chosen = chosen + mark
        kind = kind + mark * (ones_where(first < second) + 2.0 * ones_where(first > second))
        asked += [tiles[k : k + 1].astype(F32), jnp.minimum(first, second), jnp.maximum(first, second)]
    rank = dot(chosen.astype(BF16), before)
    marks[...] = jnp.where(chosen > 0.5, rank * 4.0 + kind, -4.0)
    return jnp.concatenate(asked + [jnp.zeros((16 - 3 * targets, pairs), F32)], axis=0).astype(BF16)


def pack(n, blocks, marks, chunks, picks):
    pairs = marks.shape[1]
    entries = STEP * CAP
    own = (4 * (iota((entries, pairs), 0) % CAP)).astype(F32)
    rows = jnp.broadcast_to(marks[pl.ds(n * STEP, STEP), :][:, None, :], (STEP, CAP, pairs))
    rows = rows.reshape(entries, pairs) - own
    same, upper, lower = ones_where(rows == 0.0), ones_where(rows == 1.0), ones_where(rows == 2.0)
    here = pl.ds(pl.multiple_of(n * entries, entries), entries)
    picks[here, :pairs] = (same + upper).astype(BF16)
    picks[here, pairs:] = lower.astype(BF16)
    weights = jnp.concatenate([(same + 2.0 * upper).astype(BF16), (2.0 * lower).astype(BF16)], axis=1)
    chunks[pl.ds(n * STEP, STEP)] = dot(weights, blocks).astype(BF16).reshape(STEP, CAP, WIDTH)


def encode(asked, tile, picks, codes):
    pairs = asked.shape[1]
    told = dot(asked, picks[:, :pairs] + picks[:, pairs:], NT)
    first = jnp.zeros(tile.shape, F32)
    second = jnp.zeros(tile.shape, F32)
    for k in range(asked.shape[0] // 4):
        hit = told[3 * k : 3 * k + 1] == tile
        first = first + jnp.where(hit, told[3 * k + 1 : 3 * k + 2], 0.0)
        second = second + jnp.where(hit, told[3 * k + 2 : 3 * k + 3], 0.0)
    column_tile = jnp.floor(second * (1.0 / GROUPS))
    half = jnp.floor(column_tile * 0.5)
    key = 16.0 * (half + 1.0) * (column_tile - half) + first
    code = key * GROUPS + (second - column_tile * GROUPS)
    for n in range(tile.shape[1] // LANES):
        codes[n] = code[:, n * LANES : (n + 1) * LANES]


INNER = [(j % 4, (j // 4 + j) % 4) for j in range(BATCH)]
SHIFT = [(j + 3 * (j // 4)) % 4 for j in range(BATCH)]
ROWS = BATCH * CAP // LANES


def columns_of(batch):
    return [(batch // 4) * 4 + (batch + SHIFT[j]) % 4 for j in range(BATCH)]


def places(batch, gx, gy, outward):
    core = gy % 2
    other = (core + batch // 4) % 2
    turn = 1 + 2 * other if outward else 3 - 2 * core
    x, y, z = gx // 4, gx % 4, gy // 2
    xs = [((x + d * turn) % 4) * 4 for d in range(4)]
    ys = [(y + d * turn) % 4 for d in range(4)]
    zs = [((z + (batch + d) * turn) % 4) * 2 + other for d in range(4)]
    return [(xs[dx] + ys[dy], zs[shift]) for (dx, dy), shift in zip(INNER, SHIFT)]


def tile_of(slot, gx, gy):
    b, j = slot >> 4, slot & 15
    dx, dy, dz, dc = j & 3, ((j >> 2) + j) & 3, b & 3, b >> 2
    other = (gy % 2 + dc) & 1
    turn = 1 + 2 * other
    px = ((gx // 4 + dx * turn) & 3) * 4 + ((gx % 4 + dy * turn) & 3)
    return px * 8 + ((gy // 2 + dz * turn) & 3) * 2 + other


def remote(source, target, send_sem, recv_sem, place):
    return pltpu.make_async_remote_copy(
        src_ref=source, dst_ref=target, send_sem=send_sem, recv_sem=recv_sem, device_id=place, device_id_type=MESH,
    )


def mask_basis(basis, extent):
    functions, cells = basis.shape
    atoms = functions // NB
    extent = extent.astype(F32)
    own = ones_where(iota((functions, atoms), 0) // NB == iota((functions, atoms), 1)).astype(BF16)
    half = (iota((functions, LANES), 1) // CY).astype(F32)
    low = dot(own, jnp.broadcast_to(extent[0:1], (LANES, atoms)).astype(BF16), NT) - half
    high = dot(own, jnp.broadcast_to(extent[1:2], (LANES, atoms)).astype(BF16), NT) - half
    for c in range(cells // LANES):
        row = c * (LANES // CY)
        inside = low <= float(row) if row < CX // 2 else high > float(row)
        lanes = slice(c * LANES, (c + 1) * LANES)
        basis[:, lanes] = basis[:, lanes] * ones_where(inside).astype(BF16)


def constants():
    row, lane = np.arange(WIDTH)[:, None], np.arange(WIDTH)[None, :]
    before = row < lane
    turned = (row // NB == lane % NB) & (row % NB == lane // NB)
    wide = np.arange(NB * LANES)[None, :]
    spread = (row // NB == wide // LANES) & (row % NB == wide % NB)
    square = np.concatenate([before, turned, row == lane], axis=1)
    return [np.asarray(x, np.float32) for x in (square, spread, spread.T)]


def collect(recv, got, n, spread, gathered, keys, groups):
    entries = BATCH * CAP
    own = iota((GROUPS, LANES), 0) == iota((GROUPS, LANES), 1) // CAP
    held = got.shape[0] // BATCH
    lines = [got[j * held + column * ROWS + j // GROUPS] for j, column in enumerate(columns_of(n))]
    code = []
    for h in range(ROWS):
        part = jnp.concatenate(lines[h * GROUPS : (h + 1) * GROUPS], axis=0)
        code.append(jnp.sum(jnp.where(own, part, 0.0), axis=0, keepdims=True))
    code = jnp.concatenate(code, axis=1)
    key_row = jnp.floor(code * (1.0 / GROUPS))
    group_row = code - key_row * GROUPS
    key_rows = gathered.shape[0]
    onehot = ones_where(iota((key_rows, entries), 0).astype(F32) == key_row).astype(BF16)
    key = jnp.transpose(jnp.broadcast_to(key_row, (LANES, entries)))
    group = jnp.transpose(jnp.broadcast_to(group_row, (LANES, entries)))
    here = pl.ds(pl.multiple_of(n * entries, entries), entries)
    keys[here, :] = key
    groups[here, :] = group
    blocks = recv[pl.ds(n * BATCH, BATCH)].reshape(entries, WIDTH)
    wide = 2 * LANES
    inside = (iota((entries, wide), 1) % LANES // NB).astype(F32) == jnp.concatenate([group, group], axis=1)
    for c in range(NB // 2):
        lanes = slice(c * wide, (c + 1) * wide)
        spaced = jnp.where(inside, dot(blocks, spread[:, lanes]), 0.0).astype(BF16)
        gathered[:, lanes] = gathered[:, lanes] + dot(onehot, spaced)


def pick(b, picked, keys, groups, fold, spaced, back):
    entries = BATCH * CAP
    here = pl.ds(pl.multiple_of(b * entries, entries), entries)
    key, group = keys[here, :], groups[here, :]
    lane = iota((entries, LANES), 1).astype(F32)
    onehot = jnp.concatenate(
        [ones_where(lane + float(n * LANES) == key).astype(BF16) for n in range(picked.shape[0] // LANES)], axis=1
    )
    wide = 2 * LANES
    inside = (iota((entries, wide), 1) % LANES // NB).astype(F32) == jnp.concatenate([group, group], axis=1)
    for c in range(NB // 2):
        lanes = slice(c * wide, (c + 1) * wide)
        spaced[:, lanes] = jnp.where(inside, dot(onehot, picked[:, lanes]), 0.0).astype(BF16)
    blocks = dot(spaced[...], fold[...]).astype(BF16)
    back[pl.ds(b * BATCH, BATCH)] = blocks.reshape(BATCH, CAP, WIDTH)


def potential_of(charge, below, above, left, right):
    rows = charge.shape[0]
    lane = iota((rows, LANES), 1)
    row = iota((rows, LANES), 0)
    swapped = pltpu.roll(charge, CY, 1)
    first_of_above = pltpu.roll(above, CY, 1)[0:1]
    last_of_below = pltpu.roll(below, CY, 1)[rows - 1 : rows]
    up = jnp.where(row == rows - 1, first_of_above, pltpu.roll(swapped, rows - 1, 0))
    next_x = jnp.where(lane < CY, swapped, up)
    down = jnp.where(row == 0, last_of_below, pltpu.roll(swapped, 1, 0))
    last_x = jnp.where(lane < CY, down, swapped)
    next_y = jnp.where(lane % CY == CY - 1, pltpu.roll(right, CY - 1, 1), pltpu.roll(charge, LANES - 1, 1))
    last_y = jnp.where(lane % CY == 0, pltpu.roll(left, LANES - CY + 1, 1), pltpu.roll(charge, 1, 1))
    slope_x = 0.5 * (next_x - last_x)
    slope_y = 0.5 * (next_y - last_y)
    return charge * lax.rsqrt(
        1.0 + charge * charge + gradient_weight * (slope_x * slope_x + slope_y * slope_y)
    )


def whole_kernel(
    tiles_hbm, slots_hbm, sizes_hbm, density_hbm, extent_hbm, basis_hbm, ones_hbm, spread_hbm, fold_hbm,
    out_hbm, potential_hbm,
    tiles_ref, slots_ref, sizes_ref, density_ref, extent_ref, ones_ref, spread_ref, fold_ref, out_ref, potential_ref,
    basis, weighted, chunks, recv, back, returned, codes, handed, got, marks, picks, picks_turned, spread, fold, gathered, keys, groups,
    square, matrix, picked, spaced, charge, halo,
    send_sems, recv_sems, hand_sem, code_sem, return_sem, halo_send, halo_recv, local_sem,
):
    devices = chunks.shape[0]
    functions, cells = basis.shape
    atoms = functions // NB
    column_tiles = functions // LANES
    batches = devices // BATCH
    gx, gy = lax.axis_index("gx"), lax.axis_index("gy")
    load = pltpu.make_async_copy(basis_hbm, basis, local_sem.at[0])
    inputs = [
        pltpu.make_async_copy(source, target, local_sem.at[1 + n])
        for n, (source, target) in enumerate((
            (tiles_hbm, tiles_ref), (slots_hbm, slots_ref), (sizes_hbm, sizes_ref), (density_hbm, density_ref),
            (ones_hbm, ones_ref), (extent_hbm, extent_ref), (spread_hbm, spread_ref), (fold_hbm, fold_ref),
        ))
    ]
    for copy in inputs:
        copy.start()
    load.start()
    barrier = pltpu.get_barrier_semaphore()

    def greet(b, carry):
        for j, place in enumerate(places(b, gx, gy, True)):
            def signal():
                pl.semaphore_signal(barrier, inc=1, device_id=place, device_id_type=MESH)

            if j == 0:
                pl.when(b > 0)(signal)
            else:
                signal()
        return carry

    lax.fori_loop(0, batches, greet, 0)
    gathered[...] = jnp.zeros_like(gathered)
    for c in range(column_tiles):
        low, high = (c + 1) * LANES, (c + 2) * LANES
        if c % 2 == 1:
            square[c, low:high, :] = jnp.zeros((high - low, LANES), F32)
        low, high = key_offset(c) + GROUPS * (c + 1), key_offset(c + 1)
        high = picked.shape[0] if c + 1 == column_tiles else high
        if low < high:
            picked[low:high, :] = jnp.zeros((high - low, picked.shape[1]), BF16)
    for copy in inputs[:5]:
        copy.wait()
    pairs = density_ref.shape[0]
    before, turned, eye = (ones_ref[:, n * WIDTH : (n + 1) * WIDTH].astype(BF16) for n in range(3))
    mask = size_mask_of(sizes_ref[...], eye)
    masked = jnp.where(mask, density_ref[...].astype(F32), 0.0).astype(BF16)
    blocks = jnp.concatenate([masked, dot(masked, turned).astype(BF16)], axis=0)
    asked = plan(tiles_ref[...], slots_ref, tile_of(iota((devices, 1), 0), gx, gy), before, marks)
    pl.semaphore_wait(barrier, devices - 1)
    steps = devices // STEP

    def push(batch, carry):
        for j, (column, place) in enumerate(zip(columns_of(batch), places(batch, gx, gy, True))):
            slot, spot = column * BATCH + j, batch * BATCH + j

            def start():
                remote(chunks.at[slot], recv.at[spot], send_sems.at[1], recv_sems.at[batch], place).start()

            def keep():
                pltpu.make_async_copy(chunks.at[0], recv.at[0], recv_sems.at[0]).start()

            if j == 0:
                pl.when(batch > 0)(start)
                pl.when(batch == 0)(keep)
            else:
                start()
        return carry

    def fill(n, carry):
        pack(n, blocks, marks, chunks, picks)
        return carry

    early = 2
    lax.fori_loop(0, steps // 2, fill, 0)
    lax.fori_loop(0, early, push, 0)
    lax.fori_loop(steps // 2, steps, fill, 0)
    tile = tile_of(iota((1, devices * CAP), 1) // CAP, gx, gy).astype(F32)
    encode(asked, tile, picks, codes)
    pltpu.make_async_copy(codes.at[pl.ds(0, ROWS)], handed.at[pl.ds(0, ROWS)], hand_sem).start()
    for column in range(1, batches):
        rows = pl.ds(column * ROWS, ROWS)
        dc = column // 4
        other = (gy % 2 + dc) % 2
        place = (gx, ((gy // 2 + column % 4 * (1 + 2 * other)) % 4) * 2 + other)
        remote(codes.at[rows], handed.at[rows], send_sems.at[0], hand_sem, place).start()
    for copy in inputs[5:]:
        copy.wait()
    spread[...] = spread_ref[...].astype(BF16)
    fold[...] = fold_ref[...].astype(BF16)
    load.wait()
    mask_basis(basis, extent_ref[...])
    held = handed.shape[0]
    remote(handed, handed, send_sems.at[0], hand_sem, (gx, gy)).wait_recv()
    pltpu.make_async_copy(handed, got.at[pl.ds(0, held)], code_sem).start()
    along = [
        (((gx // 4 + dx * (1 + 2 * (gy % 2))) % 4) * 4 + (gx % 4 + dy * (1 + 2 * (gy % 2))) % 4, gy)
        for dx, dy in INNER
    ]
    for j in range(1, BATCH):
        remote(handed, got.at[pl.ds(j * held, held)], send_sems.at[0], code_sem, along[j]).start()
    lax.fori_loop(early, batches, push, 0)

    remote(got, got, send_sems.at[0], code_sem, (gx, gy)).wait_recv()

    def arrive(n, carry):
        slots = pl.ds(n * BATCH, BATCH)
        remote(recv.at[slots], recv.at[slots], send_sems.at[1], recv_sems.at[n], (gx, gy)).wait_recv()
        collect(recv, got, n, spread, gathered, keys, groups)
        return carry

    lax.fori_loop(0, batches, arrive, 0)
    for c in range(column_tiles):
        low = key_offset(c)
        count = GROUPS * (c + 1)
        for i in range(NB):
            block = gathered[low : low + count, i * LANES : (i + 1) * LANES]
            square[c, pl.ds(i, count, stride=NB), :] = block
        matrix[:, c * LANES : (c + 1) * LANES] = square[c].astype(BF16)
    step = 2 * LANES
    cuts = [0] + list(range(LANES, functions + 1, 2 * LANES))
    for c in range(cells // step):
        columns = basis[:, c * step : (c + 1) * step]
        total = jnp.zeros((1, step), F32)
        for low, high in zip(cuts, cuts[1:]):
            product = dot(matrix[low:high, low:], columns[low:])
            product = product * columns[low:high].astype(F32)
            total = total + jnp.sum(product, axis=0, keepdims=True)
        charge[2 * c : 2 * c + 1, :] = total[:, :LANES]
        charge[2 * c + 1 : 2 * c + 2, :] = total[:, LANES:]
    edges = [
        remote(charge, halo.at[n], halo_send.at[n], halo_recv.at[n], place)
        for n, place in enumerate(
            (((gx + 1) % 16, gy), ((gx + 15) % 16, gy), (gx, (gy + 7) % 8), (gx, (gy + 1) % 8))
        )
    ]
    for copy in edges:
        copy.start()
    for copy in edges:
        copy.wait()
    potential = potential_of(charge[...], halo[0], halo[1], halo[3], halo[2])
    for half in range(2):
        rows = potential if half == 0 else pltpu.roll(potential, CY, 1)
        potential_ref[pl.ds(half, CX // 2, stride=2), :] = rows[:, :CY]
    potential_out = pltpu.make_async_copy(potential_ref, potential_hbm, local_sem.at[1])
    potential_out.start()
    for c in range(cells // LANES):
        lanes = slice(c * LANES, (c + 1) * LANES)
        weighted[:, lanes] = (basis[:, lanes].astype(F32) * potential[c : c + 1]).astype(BF16)
    for start, high in zip(cuts, cuts[1:]):
        product = dot(basis[:high, :], weighted[start:high, :], NT)
        for c in range(start // LANES, high // LANES):
            square[c, :high, :] = product[:, c * LANES - start : (c + 1) * LANES - start]
            low = key_offset(c)
            count = GROUPS * (c + 1)
            for i in range(NB):
                block = square[c, pl.ds(i, count, stride=NB), :]
                picked[low : low + count, i * LANES : (i + 1) * LANES] = block.astype(BF16)
    keep = pltpu.make_async_copy(back.at[0], returned.at[0], return_sem)

    def give(n, carry):
        pick(n, picked, keys, groups, fold, spaced, back)
        for j, (column, place) in enumerate(zip(columns_of(n), places(n, gx, gy, False))):
            slot, spot = column * BATCH + j, n * BATCH + j

            def start():
                remote(back.at[spot], returned.at[slot], send_sems.at[2], return_sem, place).start()

            if j == 0:
                pl.when(n > 0)(start)
                pl.when(n == 0)(keep.start)
            else:
                start()
        return carry

    lax.fori_loop(0, batches, give, 0)
    for half in range(2):
        for n in range(devices * CAP // 512):
            part = picks[n * 512 : (n + 1) * 512, half * pairs : (half + 1) * pairs].astype(F32)
            lanes = half * devices * CAP + n * 512
            picks_turned[:, lanes : lanes + 512] = jnp.transpose(part).astype(BF16)
    mask = size_mask_of(sizes_ref[...], eye)
    remote(returned, returned, send_sems.at[2], return_sem, (gx, gy)).wait_recv()
    blocks = returned[...].reshape(devices * CAP, WIDTH)
    blocks = jnp.concatenate([blocks, dot(blocks, turned).astype(BF16)], axis=0)
    out_ref[...] = jnp.where(mask, dot(picks_turned[...], blocks) * float(cells) ** -0.5, 0.0)
    out = pltpu.make_async_copy(out_ref, out_hbm, local_sem.at[2])
    out.start()
    out.wait()
    potential_out.wait()
    others = pl.ds(0, devices - 1)
    rows = pl.ds(ROWS, held - ROWS)
    remote(handed.at[rows], handed.at[rows], send_sems.at[0], hand_sem, (gx, gy)).wait_send()
    rows = pl.ds(held, got.shape[0] - held)
    remote(got.at[rows], got.at[rows], send_sems.at[0], code_sem, (gx, gy)).wait_send()
    remote(chunks.at[others], recv.at[others], send_sems.at[1], recv_sems.at[0], (gx, gy)).wait_send()
    remote(back.at[others], returned.at[others], send_sems.at[2], return_sem, (gx, gy)).wait_send()


def finish_kernel(summed, field, out, potential):
    out[...] = summed[...]
    potential[...] = field[...]


VMEM_SPEC = pl.BlockSpec(memory_space=pltpu.VMEM)
ANY_SPEC = pl.BlockSpec(memory_space=pl.ANY)
DMA = pltpu.SemaphoreType.DMA


def shards(density, pair_tiles, pair_slots, pair_sizes, basis_table, tile_extent):
    devices = lax.axis_size("gx") * lax.axis_size("gy")
    pairs, targets = pair_tiles.shape
    atoms = tile_extent.shape[2]
    functions, cells = basis_table.shape[1:]
    rows = cells // LANES
    key_rows = key_offset(functions // LANES)
    chunk = pltpu.VMEM((devices, CAP, WIDTH), BF16)
    entries = devices * CAP
    spaced = NB * LANES
    results = pl.pallas_call(
        whole_kernel,
        name="whole",
        out_shape=[
            jax.ShapeDtypeStruct((pairs, WIDTH), F32),
            jax.ShapeDtypeStruct((CX, CY), F32),
        ],
        in_specs=[ANY_SPEC] * 9,
        out_specs=[ANY_SPEC] * 2,
        scratch_shapes=[
            pltpu.VMEM((targets, pairs), I32),
            pltpu.VMEM((targets, 2, pairs), I32),
            pltpu.VMEM((2, pairs), I32),
            pltpu.VMEM((pairs, WIDTH), BF16),
            pltpu.VMEM((2, atoms), I32),
            pltpu.VMEM((WIDTH, 3 * WIDTH), F32),
            pltpu.VMEM((WIDTH, spaced), F32),
            pltpu.VMEM((spaced, WIDTH), F32),
            pltpu.VMEM((pairs, WIDTH), F32),
            pltpu.VMEM((CX, CY), F32),
            pltpu.VMEM((functions, cells), BF16),
            pltpu.VMEM((functions, cells), BF16),
            chunk,
            chunk,
            chunk,
            chunk,
            pltpu.VMEM((devices * CAP // LANES, 1, LANES), F32),
            pltpu.VMEM((devices * CAP // LANES, 1, LANES), F32),
            pltpu.VMEM((devices * CAP // LANES * BATCH, 1, LANES), F32),
            pltpu.VMEM((devices, pairs), F32),
            pltpu.VMEM((entries, 2 * pairs), BF16),
            pltpu.VMEM((pairs, 2 * entries), BF16),
            pltpu.VMEM((WIDTH, spaced), BF16),
            pltpu.VMEM((spaced, WIDTH), BF16),
            pltpu.VMEM((key_rows, spaced), F32),
            pltpu.VMEM((entries, LANES), F32),
            pltpu.VMEM((entries, LANES), F32),
            pltpu.VMEM((functions // LANES, functions, LANES), F32),
            pltpu.VMEM((functions, functions), BF16),
            pltpu.VMEM((-(-key_rows // LANES) * LANES, spaced), BF16),
            pltpu.VMEM((BATCH * CAP, spaced), BF16),
            pltpu.VMEM((rows, LANES), F32),
            pltpu.VMEM((4, rows, LANES), F32),
            DMA((3,)),
            DMA((devices // BATCH,)),
            DMA,
            DMA,
            DMA,
            DMA((4,)),
            DMA((4,)),
            DMA((9,)),
        ],
        compiler_params=pltpu.CompilerParams(
            vmem_limit_bytes=VMEM_BYTES, collective_id=1, has_side_effects=True
        ),
    )(pair_tiles.T, pair_slots.transpose(1, 2, 0), pair_sizes.T, density, tile_extent[0], basis_table[0], *constants())
    return tuple(pl.pallas_call(
        finish_kernel,
        name="finish",
        out_shape=[jax.ShapeDtypeStruct(result.shape, result.dtype) for result in results],
        in_specs=[VMEM_SPEC] * 2,
        out_specs=[VMEM_SPEC] * 2,
        compiler_params=pltpu.CompilerParams(vmem_limit_bytes=VMEM_BYTES),
    )(*results))


def solution(mesh):
    in_specs = (
        P(("gx", "gy"), None),
        P(("gx", "gy"), None),
        P(("gx", "gy"), None, None),
        P(("gx", "gy"), None),
        P(("gx", "gy"), None, None),
        P(("gx", "gy"), None, None),
    )
    out_specs = (P(("gx", "gy"), None), P("gx", "gy"))
    return jax.shard_map(shards, mesh=mesh, in_specs=in_specs, out_specs=out_specs, check_vma=False)
```

```python
import functools

import jax
import jax.numpy as jnp
import numpy as np
from jax import lax
from jax.experimental import pallas as pl
from jax.experimental.pallas import tpu as pltpu
from jax.sharding import PartitionSpec as P

NB = 16
CX = 32
CY = 64
LANES = 128
GROUPS = LANES // NB
WIDTH = NB * NB
CAP = 16
BATCH = 16
STEP = 32
MESH = pl.DeviceIdType.MESH
F32 = jnp.float32
BF16 = jnp.bfloat16
I32 = jnp.int32
VMEM_BYTES = 60 * 1024 * 1024
gradient_weight = 1.0
NT = (((1,), (1,)), ((), ()))


def iota(shape, dim):
    return lax.broadcasted_iota(I32, shape, dim)


def dot(a, b, dims=(((1,), (0,)), ((), ()))):
    return lax.dot_general(a, b, dims, preferred_element_type=F32)


def ones_where(condition):
    return jnp.where(condition, 1.0, 0.0)


def size_mask_of(sizes, eye):
    pairs = sizes.shape[1]
    wide = sizes.astype(F32)
    first = dot(eye, jnp.broadcast_to(wide[0:1], (WIDTH, pairs)).astype(BF16), NT)
    second = dot(eye, jnp.broadcast_to(wide[1:2], (WIDTH, pairs)).astype(BF16), NT)
    lane = iota((pairs, WIDTH), 1)
    row = (lane // NB).astype(F32)
    col = (lane % NB).astype(F32)
    return (row < first) & (col < second)


def key_offset(column_tile):
    half = column_tile // 2
    return 16 * (half + 1) * (half + column_tile % 2)


def plan(tiles, slots_ref, tile_id, before, marks):
    targets, pairs = tiles.shape
    devices = marks.shape[0]
    chosen = jnp.zeros((devices, pairs), F32)
    kind = jnp.zeros((devices, pairs), F32)
    asked = []
    for k in range(targets):
        mark = ones_where(tiles[k : k + 1] == tile_id)
        slots = slots_ref[k].astype(F32)
        first, second = slots[0:1], slots[1:2]
        chosen = chosen + mark
        kind = kind + mark * (ones_where(first < second) + 2.0 * ones_where(first > second))
        asked += [tiles[k : k + 1].astype(F32), jnp.minimum(first, second), jnp.maximum(first, second)]
    rank = dot(chosen.astype(BF16), before)
    marks[...] = jnp.where(chosen > 0.5, rank * 4.0 + kind, -4.0)
    return jnp.concatenate(asked + [jnp.zeros((16 - 3 * targets, pairs), F32)], axis=0).astype(BF16)


def pack(b, tile, asked, blocks, marks, chunks, codes, picks):
    pairs = marks.shape[1]
    entries = STEP * CAP
    own = (4 * (iota((entries, pairs), 0) % CAP)).astype(F32)
    rows = jnp.broadcast_to(marks[pl.ds(b * STEP, STEP), :][:, None, :], (STEP, CAP, pairs))
    rows = rows.reshape(entries, pairs) - own
    same, upper, lower = ones_where(rows == 0.0), ones_where(rows == 1.0), ones_where(rows == 2.0)
    straight = (same + upper).astype(BF16)
    across = lower.astype(BF16)
    here = pl.ds(pl.multiple_of(b * entries, entries), entries)
    picks[here, :pairs] = straight
    picks[here, pairs:] = across
    weights = jnp.concatenate([(same + 2.0 * upper).astype(BF16), (2.0 * lower).astype(BF16)], axis=1)
    chunks[pl.ds(b * STEP, STEP)] = dot(weights, blocks).astype(BF16).reshape(STEP, CAP, WIDTH)
    told = dot(asked, straight + across, NT)
    first = jnp.zeros((1, entries), F32)
    second = jnp.zeros((1, entries), F32)
    for k in range(asked.shape[0] // 3):
        hit = told[3 * k : 3 * k + 1] == tile
        first = first + jnp.where(hit, told[3 * k + 1 : 3 * k + 2], 0.0)
        second = second + jnp.where(hit, told[3 * k + 2 : 3 * k + 3], 0.0)
    column_tile = jnp.floor(second * (1.0 / GROUPS))
    half = jnp.floor(column_tile * 0.5)
    key = 16.0 * (half + 1.0) * (column_tile - half) + first
    code = key * GROUPS + (second - column_tile * GROUPS)
    for n in range(entries // LANES):
        codes[b * (entries // LANES) + n] = code[:, n * LANES : (n + 1) * LANES]


INNER = [(j % 4, (j // 4 + j) % 4, (j + 3 * (j // 4)) % 4) for j in range(BATCH)]


def places(b, gx, gy, outward):
    core = gy % 2
    other = (core + b % 2) % 2
    turn = 1 + 2 * core if outward else 3 - 2 * other
    x, y, z = gx // 4, gx % 4, gy // 2
    xs = [((x + d * turn) % 4) * 4 for d in range(4)]
    ys = [(y + d * turn) % 4 for d in range(4)]
    zs = [((z + (b // 2 + d) * turn) % 4) * 2 + other for d in range(4)]
    return [(xs[dx] + ys[dy], zs[dz]) for dx, dy, dz in INNER]


def tile_of(slot, gx, gy):
    b, j = slot >> 4, slot & 15
    dx, dy, dz = j & 3, ((j >> 2) + j) & 3, ((b >> 1) + j + 3 * (j >> 2)) & 3
    core = gy % 2
    turn = 1 + 2 * core
    px = ((gx // 4 + dx * turn) & 3) * 4 + ((gx % 4 + dy * turn) & 3)
    return px * 8 + ((gy // 2 + dz * turn) & 3) * 2 + ((core + b) & 1)


def remote(source, target, send_sem, recv_sem, place):
    return pltpu.make_async_remote_copy(
        src_ref=source, dst_ref=target, send_sem=send_sem, recv_sem=recv_sem, device_id=place, device_id_type=MESH,
    )


def mask_basis(basis, extent):
    functions, cells = basis.shape
    atoms = functions // NB
    extent = extent.astype(F32)
    own = ones_where(iota((functions, atoms), 0) // NB == iota((functions, atoms), 1)).astype(BF16)
    half = (iota((functions, LANES), 1) // CY).astype(F32)
    low = dot(own, jnp.broadcast_to(extent[0:1], (LANES, atoms)).astype(BF16), NT) - half
    high = dot(own, jnp.broadcast_to(extent[1:2], (LANES, atoms)).astype(BF16), NT) - half
    for c in range(cells // LANES):
        row = c * (LANES // CY)
        inside = low <= float(row) if row < CX // 2 else high > float(row)
        lanes = slice(c * LANES, (c + 1) * LANES)
        basis[:, lanes] = basis[:, lanes] * ones_where(inside).astype(BF16)


def constants():
    row, lane = np.arange(WIDTH)[:, None], np.arange(WIDTH)[None, :]
    before = row < lane
    turned = (row // NB == lane % NB) & (row % NB == lane // NB)
    wide = np.arange(NB * LANES)[None, :]
    spread = (row // NB == wide // LANES) & (row % NB == wide % NB)
    square = np.concatenate([before, turned, row == lane], axis=1)
    return [np.asarray(x, np.float32) for x in (square, spread, spread.T)]


def collect(recv, got, b, spread, gathered, keys, groups):
    entries = BATCH * CAP
    own = iota((GROUPS, LANES), 0) == iota((GROUPS, LANES), 1) // CAP
    code = []
    for h in range(BATCH // GROUPS):
        lines = got[pl.ds(b * BATCH + h * GROUPS, GROUPS), 0, :]
        code.append(jnp.sum(jnp.where(own, lines, 0.0), axis=0, keepdims=True))
    code = jnp.concatenate(code, axis=1)
    key_row = jnp.floor(code * (1.0 / GROUPS))
    group_row = code - key_row * GROUPS
    key_rows = gathered.shape[0]
    onehot = ones_where(iota((key_rows, entries), 0).astype(F32) == key_row).astype(BF16)
    key = jnp.transpose(jnp.broadcast_to(key_row, (LANES, entries)))
    group = jnp.transpose(jnp.broadcast_to(group_row, (LANES, entries)))
    here = pl.ds(pl.multiple_of(b * entries, entries), entries)
    keys[here, :] = key
    groups[here, :] = group
    blocks = recv[pl.ds(b * BATCH, BATCH)].reshape(entries, WIDTH)
    wide = 2 * LANES
    inside = (iota((entries, wide), 1) % LANES // NB).astype(F32) == jnp.concatenate([group, group], axis=1)
    for c in range(NB // 2):
        lanes = slice(c * wide, (c + 1) * wide)
        spaced = jnp.where(inside, dot(blocks, spread[:, lanes]), 0.0).astype(BF16)
        gathered[:, lanes] = gathered[:, lanes] + dot(onehot, spaced)


def pick(b, picked, keys, groups, fold, spaced, back):
    entries = BATCH * CAP
    here = pl.ds(pl.multiple_of(b * entries, entries), entries)
    key, group = keys[here, :], groups[here, :]
    lane = iota((entries, LANES), 1).astype(F32)
    onehot = jnp.concatenate(
        [ones_where(lane + float(n * LANES) == key).astype(BF16) for n in range(picked.shape[0] // LANES)], axis=1
    )
    wide = 2 * LANES
    inside = (iota((entries, wide), 1) % LANES // NB).astype(F32) == jnp.concatenate([group, group], axis=1)
    for c in range(NB // 2):
        lanes = slice(c * wide, (c + 1) * wide)
        spaced[:, lanes] = jnp.where(inside, dot(onehot, picked[:, lanes]), 0.0).astype(BF16)
    blocks = dot(spaced[...], fold[...]).astype(BF16)
    back[pl.ds(b * BATCH, BATCH)] = blocks.reshape(BATCH, CAP, WIDTH)


def potential_of(charge, below, above, left, right):
    rows = charge.shape[0]
    lane = iota((rows, LANES), 1)
    row = iota((rows, LANES), 0)
    swapped = pltpu.roll(charge, CY, 1)
    first_of_above = pltpu.roll(above, CY, 1)[0:1]
    last_of_below = pltpu.roll(below, CY, 1)[rows - 1 : rows]
    up = jnp.where(row == rows - 1, first_of_above, pltpu.roll(swapped, rows - 1, 0))
    next_x = jnp.where(lane < CY, swapped, up)
    down = jnp.where(row == 0, last_of_below, pltpu.roll(swapped, 1, 0))
    last_x = jnp.where(lane < CY, down, swapped)
    next_y = jnp.where(lane % CY == CY - 1, pltpu.roll(right, CY - 1, 1), pltpu.roll(charge, LANES - 1, 1))
    last_y = jnp.where(lane % CY == 0, pltpu.roll(left, LANES - CY + 1, 1), pltpu.roll(charge, 1, 1))
    slope_x = 0.5 * (next_x - last_x)
    slope_y = 0.5 * (next_y - last_y)
    return charge * lax.rsqrt(
        1.0 + charge * charge + gradient_weight * (slope_x * slope_x + slope_y * slope_y)
    )


def whole_kernel(
    tiles_hbm, slots_hbm, sizes_hbm, density_hbm, extent_hbm, basis_hbm, ones_hbm, spread_hbm, fold_hbm,
    out_hbm, potential_hbm,
    tiles_ref, slots_ref, sizes_ref, density_ref, extent_ref, ones_ref, spread_ref, fold_ref, out_ref, potential_ref,
    basis, weighted, chunks, recv, back, returned, codes, got, marks, picks, picks_turned, spread, fold, gathered, keys, groups,
    square, matrix, picked, spaced, charge, halo,
    send_sems, recv_sems, code_sems, return_sem, halo_send, halo_recv, local_sem,
):
    devices = chunks.shape[0]
    functions, cells = basis.shape
    atoms = functions // NB
    column_tiles = functions // LANES
    batches = devices // BATCH
    gx, gy = lax.axis_index("gx"), lax.axis_index("gy")
    load = pltpu.make_async_copy(basis_hbm, basis, local_sem.at[0])
    inputs = [
        pltpu.make_async_copy(source, target, local_sem.at[1 + n])
        for n, (source, target) in enumerate((
            (tiles_hbm, tiles_ref), (slots_hbm, slots_ref), (sizes_hbm, sizes_ref), (density_hbm, density_ref),
            (ones_hbm, ones_ref), (extent_hbm, extent_ref), (spread_hbm, spread_ref), (fold_hbm, fold_ref),
        ))
    ]
    for copy in inputs:
        copy.start()
    load.start()
    barrier = pltpu.get_barrier_semaphore()

    def greet(b, carry):
        for j, place in enumerate(places(b, gx, gy, True)):
            def signal():
                pl.semaphore_signal(barrier, inc=1, device_id=place, device_id_type=MESH)

            if j == 0:
                pl.when(b > 0)(signal)
            else:
                signal()
        return carry

    lax.fori_loop(0, batches, greet, 0)
    gathered[...] = jnp.zeros_like(gathered)
    for c in range(column_tiles):
        low, high = (c + 1) * LANES, (c // 3 + 1) * 3 * LANES
        if low < high:
            square[c, low:high, :] = jnp.zeros((high - low, LANES), F32)
        low, high = key_offset(c) + GROUPS * (c + 1), key_offset(c + 1)
        high = picked.shape[0] if c + 1 == column_tiles else high
        if low < high:
            picked[low:high, :] = jnp.zeros((high - low, picked.shape[1]), BF16)
    for copy in inputs[:5]:
        copy.wait()
    pairs = density_ref.shape[0]
    before, turned, eye = (ones_ref[:, n * WIDTH : (n + 1) * WIDTH].astype(BF16) for n in range(3))
    mask = size_mask_of(sizes_ref[...], eye)
    masked = jnp.where(mask, density_ref[...].astype(F32), 0.0).astype(BF16)
    blocks = jnp.concatenate([masked, dot(masked, turned).astype(BF16)], axis=0)
    asked = plan(tiles_ref[...], slots_ref, tile_of(iota((devices, 1), 0), gx, gy), before, marks)
    rows_per_batch = BATCH * CAP // LANES

    def push(b, carry):
        for j, place in enumerate(places(b, gx, gy, True)):
            slot = b * BATCH + j
            row = b * rows_per_batch + j * CAP // LANES

            def start():
                remote(codes.at[row], got.at[slot], send_sems.at[0], code_sems.at[b], place).start()
                remote(chunks.at[slot], recv.at[slot], send_sems.at[1], recv_sems.at[b], place).start()

            def keep():
                pltpu.make_async_copy(codes.at[0], got.at[0], code_sems.at[0]).start()
                pltpu.make_async_copy(chunks.at[0], recv.at[0], recv_sems.at[0]).start()

            if j == 0:
                pl.when(b > 0)(start)
                pl.when(b == 0)(keep)
            else:
                start()
        return carry

    def fill(n, carry):
        tile = tile_of(n * STEP + iota((1, STEP * CAP), 1) // CAP, gx, gy).astype(F32)
        pack(n, tile, asked, blocks, marks, chunks, codes, picks)
        return carry

    lax.fori_loop(0, devices // STEP, fill, 0)
    pl.semaphore_wait(barrier, devices - 1)
    lax.fori_loop(0, batches, push, 0)
    for copy in inputs[5:]:
        copy.wait()
    spread[...] = spread_ref[...].astype(BF16)
    fold[...] = fold_ref[...].astype(BF16)
    load.wait()
    mask_basis(basis, extent_ref[...])

    def arrive(b, carry):
        slots = pl.ds(b * BATCH, BATCH)
        remote(got.at[slots], got.at[slots], send_sems.at[0], code_sems.at[b], (gx, gy)).wait_recv()
        remote(recv.at[slots], recv.at[slots], send_sems.at[1], recv_sems.at[b], (gx, gy)).wait_recv()
        collect(recv, got, b, spread, gathered, keys, groups)
        return carry

    lax.fori_loop(0, batches, arrive, 0)
    for c in range(column_tiles):
        low = key_offset(c)
        count = GROUPS * (c + 1)
        for i in range(NB):
            block = gathered[low : low + count, i * LANES : (i + 1) * LANES]
            square[c, pl.ds(i, count, stride=NB), :] = block
        matrix[:, c * LANES : (c + 1) * LANES] = square[c].astype(BF16)
    step = 2 * LANES
    part = 3 * LANES
    for c in range(cells // step):
        columns = basis[:, c * step : (c + 1) * step]
        total = jnp.zeros((1, step), F32)
        for low in range(0, functions, part):
            product = dot(matrix[low : low + part, low:], columns[low:])
            product = product * columns[low : low + part].astype(F32)
            total = total + jnp.sum(product, axis=0, keepdims=True)
        charge[2 * c : 2 * c + 1, :] = total[:, :LANES]
        charge[2 * c + 1 : 2 * c + 2, :] = total[:, LANES:]
    edges = [
        remote(charge, halo.at[n], halo_send.at[n], halo_recv.at[n], place)
        for n, place in enumerate(
            (((gx + 1) % 16, gy), ((gx + 15) % 16, gy), (gx, (gy + 7) % 8), (gx, (gy + 1) % 8))
        )
    ]
    for copy in edges:
        copy.start()
    for copy in edges:
        copy.wait()
    potential = potential_of(charge[...], halo[0], halo[1], halo[3], halo[2])
    for half in range(2):
        rows = potential if half == 0 else pltpu.roll(potential, CY, 1)
        potential_ref[pl.ds(half, CX // 2, stride=2), :] = rows[:, :CY]
    potential_out = pltpu.make_async_copy(potential_ref, potential_hbm, local_sem.at[1])
    potential_out.start()
    for c in range(cells // LANES):
        lanes = slice(c * LANES, (c + 1) * LANES)
        weighted[:, lanes] = (basis[:, lanes].astype(F32) * potential[c : c + 1]).astype(BF16)
    for start in range(0, column_tiles, 2):
        stop = min(start + 2, column_tiles)
        rows = weighted[start * LANES : stop * LANES, :]
        high = stop * LANES
        product = dot(basis[:high, :], rows, NT)
        for c in range(start, stop):
            square[c, :high, :] = product[:, (c - start) * LANES : (c - start + 1) * LANES]
            low = key_offset(c)
            count = GROUPS * (c + 1)
            for i in range(NB):
                block = square[c, pl.ds(i, count, stride=NB), :]
                picked[low : low + count, i * LANES : (i + 1) * LANES] = block.astype(BF16)
    keep = pltpu.make_async_copy(back.at[0], returned.at[0], return_sem)

    def give(b, carry):
        pick(b, picked, keys, groups, fold, spaced, back)
        for j, place in enumerate(places(b, gx, gy, False)):
            slot = b * BATCH + j

            def start():
                remote(back.at[slot], returned.at[slot], send_sems.at[2], return_sem, place).start()

            if j == 0:
                pl.when(b > 0)(start)
                pl.when(b == 0)(keep.start)
            else:
                start()
        return carry

    lax.fori_loop(0, batches, give, 0)
    for half in range(2):
        for n in range(devices * CAP // 512):
            part = picks[n * 512 : (n + 1) * 512, half * pairs : (half + 1) * pairs].astype(F32)
            lanes = half * devices * CAP + n * 512
            picks_turned[:, lanes : lanes + 512] = jnp.transpose(part).astype(BF16)
    mask = size_mask_of(sizes_ref[...], eye)
    remote(returned, returned, send_sems.at[2], return_sem, (gx, gy)).wait_recv()
    blocks = returned[...].reshape(devices * CAP, WIDTH)
    blocks = jnp.concatenate([blocks, dot(blocks, turned).astype(BF16)], axis=0)
    out_ref[...] = jnp.where(mask, dot(picks_turned[...], blocks) * float(cells) ** -0.5, 0.0)
    out = pltpu.make_async_copy(out_ref, out_hbm, local_sem.at[2])
    out.start()
    out.wait()
    potential_out.wait()
    others = pl.ds(0, devices - 1)
    remote(got.at[others], got.at[others], send_sems.at[0], code_sems.at[0], (gx, gy)).wait_send()
    remote(chunks.at[others], recv.at[others], send_sems.at[1], recv_sems.at[0], (gx, gy)).wait_send()
    remote(back.at[others], returned.at[others], send_sems.at[2], return_sem, (gx, gy)).wait_send()


def finish_kernel(summed, field, out, potential):
    out[...] = summed[...]
    potential[...] = field[...]


VMEM_SPEC = pl.BlockSpec(memory_space=pltpu.VMEM)
ANY_SPEC = pl.BlockSpec(memory_space=pl.ANY)
DMA = pltpu.SemaphoreType.DMA


def shards(density, pair_tiles, pair_slots, pair_sizes, basis_table, tile_extent):
    devices = lax.axis_size("gx") * lax.axis_size("gy")
    pairs, targets = pair_tiles.shape
    atoms = tile_extent.shape[2]
    functions, cells = basis_table.shape[1:]
    rows = cells // LANES
    key_rows = key_offset(functions // LANES)
    chunk = pltpu.VMEM((devices, CAP, WIDTH), BF16)
    entries = devices * CAP
    spaced = NB * LANES
    results = pl.pallas_call(
        whole_kernel,
        name="whole",
        out_shape=[
            jax.ShapeDtypeStruct((pairs, WIDTH), F32),
            jax.ShapeDtypeStruct((CX, CY), F32),
        ],
        in_specs=[ANY_SPEC] * 9,
        out_specs=[ANY_SPEC] * 2,
        scratch_shapes=[
            pltpu.VMEM((targets, pairs), I32),
            pltpu.VMEM((targets, 2, pairs), I32),
            pltpu.VMEM((2, pairs), I32),
            pltpu.VMEM((pairs, WIDTH), BF16),
            pltpu.VMEM((2, atoms), I32),
            pltpu.VMEM((WIDTH, 3 * WIDTH), F32),
            pltpu.VMEM((WIDTH, spaced), F32),
            pltpu.VMEM((spaced, WIDTH), F32),
            pltpu.VMEM((pairs, WIDTH), F32),
            pltpu.VMEM((CX, CY), F32),
            pltpu.VMEM((functions, cells), BF16),
            pltpu.VMEM((functions, cells), BF16),
            chunk,
            chunk,
            chunk,
            chunk,
            pltpu.VMEM((devices * CAP // LANES, 1, LANES), F32),
            pltpu.VMEM((devices, 1, LANES), F32),
            pltpu.VMEM((devices, pairs), F32),
            pltpu.VMEM((entries, 2 * pairs), BF16),
            pltpu.VMEM((pairs, 2 * entries), BF16),
            pltpu.VMEM((WIDTH, spaced), BF16),
            pltpu.VMEM((spaced, WIDTH), BF16),
            pltpu.VMEM((key_rows, spaced), F32),
            pltpu.VMEM((entries, LANES), F32),
            pltpu.VMEM((entries, LANES), F32),
            pltpu.VMEM((functions // LANES, functions, LANES), F32),
            pltpu.VMEM((functions, functions), BF16),
            pltpu.VMEM((-(-key_rows // LANES) * LANES, spaced), BF16),
            pltpu.VMEM((BATCH * CAP, spaced), BF16),
            pltpu.VMEM((rows, LANES), F32),
            pltpu.VMEM((4, rows, LANES), F32),
            DMA((3,)),
            DMA((devices // BATCH,)),
            DMA((devices // BATCH,)),
            DMA,
            DMA((4,)),
            DMA((4,)),
            DMA((9,)),
        ],
        compiler_params=pltpu.CompilerParams(
            vmem_limit_bytes=VMEM_BYTES, collective_id=1, has_side_effects=True
        ),
    )(pair_tiles.T, pair_slots.transpose(1, 2, 0), pair_sizes.T, density, tile_extent[0], basis_table[0], *constants())
    return tuple(pl.pallas_call(
        finish_kernel,
        name="finish",
        out_shape=[jax.ShapeDtypeStruct(result.shape, result.dtype) for result in results],
        in_specs=[VMEM_SPEC] * 2,
        out_specs=[VMEM_SPEC] * 2,
        compiler_params=pltpu.CompilerParams(vmem_limit_bytes=VMEM_BYTES),
    )(*results))


def solution(mesh):
    in_specs = (
        P(("gx", "gy"), None),
        P(("gx", "gy"), None),
        P(("gx", "gy"), None, None),
        P(("gx", "gy"), None),
        P(("gx", "gy"), None, None),
        P(("gx", "gy"), None, None),
    )
    out_specs = (P(("gx", "gy"), None), P("gx", "gy"))
    return jax.shard_map(shards, mesh=mesh, in_specs=in_specs, out_specs=out_specs, check_vma=False)
```

```python
import functools

import jax
import jax.numpy as jnp
import numpy as np
from jax import lax
from jax.experimental import pallas as pl
from jax.experimental.pallas import tpu as pltpu
from jax.sharding import PartitionSpec as P

NB = 16
CX = 32
CY = 64
LANES = 128
GROUPS = LANES // NB
WIDTH = NB * NB
CAP = 16
BATCH = 16
STEP = 32
MESH = pl.DeviceIdType.MESH
F32 = jnp.float32
BF16 = jnp.bfloat16
I32 = jnp.int32
VMEM_BYTES = 60 * 1024 * 1024
gradient_weight = 1.0
NT = (((1,), (1,)), ((), ()))


def iota(shape, dim):
    return lax.broadcasted_iota(I32, shape, dim)


def dot(a, b, dims=(((1,), (0,)), ((), ()))):
    return lax.dot_general(a, b, dims, preferred_element_type=F32)


def ones_where(condition):
    return jnp.where(condition, 1.0, 0.0)


def size_mask_of(sizes, eye):
    pairs = sizes.shape[1]
    wide = sizes.astype(F32)
    first = dot(eye, jnp.broadcast_to(wide[0:1], (WIDTH, pairs)).astype(BF16), NT)
    second = dot(eye, jnp.broadcast_to(wide[1:2], (WIDTH, pairs)).astype(BF16), NT)
    lane = iota((pairs, WIDTH), 1)
    row = (lane // NB).astype(F32)
    col = (lane % NB).astype(F32)
    return (row < first) & (col < second)


def key_offset(column_tile):
    half = column_tile // 2
    return 16 * (half + 1) * (half + column_tile % 2)


def plan(tiles, slots_ref, tile_id, before, marks):
    targets, pairs = tiles.shape
    devices = marks.shape[0]
    chosen = jnp.zeros((devices, pairs), F32)
    kind = jnp.zeros((devices, pairs), F32)
    asked = []
    for k in range(targets):
        mark = ones_where(tiles[k : k + 1] == tile_id)
        slots = slots_ref[k].astype(F32)
        first, second = slots[0:1], slots[1:2]
        chosen = chosen + mark
        kind = kind + mark * (ones_where(first < second) + 2.0 * ones_where(first > second))
        asked += [tiles[k : k + 1].astype(F32), jnp.minimum(first, second), jnp.maximum(first, second)]
    rank = dot(chosen.astype(BF16), before)
    marks[...] = jnp.where(chosen > 0.5, rank * 4.0 + kind, -4.0)
    return jnp.concatenate(asked + [jnp.zeros((16 - 3 * targets, pairs), F32)], axis=0).astype(BF16)


def pack(b, tile, asked, blocks, marks, chunks, codes, picks):
    pairs = marks.shape[1]
    entries = STEP * CAP
    own = (4 * (iota((entries, pairs), 0) % CAP)).astype(F32)
    rows = jnp.broadcast_to(marks[pl.ds(b * STEP, STEP), :][:, None, :], (STEP, CAP, pairs))
    rows = rows.reshape(entries, pairs) - own
    same, upper, lower = ones_where(rows == 0.0), ones_where(rows == 1.0), ones_where(rows == 2.0)
    straight = upper.astype(BF16)
    across = (same + lower).astype(BF16)
    here = pl.ds(pl.multiple_of(b * entries, entries), entries)
    picks[here, :pairs] = straight
    picks[here, pairs:] = across
    weights = jnp.concatenate([(same + 2.0 * upper).astype(BF16), (2.0 * lower).astype(BF16)], axis=1)
    chunks[pl.ds(b * STEP, STEP)] = dot(weights, blocks).astype(BF16).reshape(STEP, CAP, WIDTH)
    told = dot(asked, straight + across, NT)
    first = jnp.zeros((1, entries), F32)
    second = jnp.zeros((1, entries), F32)
    for k in range(asked.shape[0] // 3):
        hit = told[3 * k : 3 * k + 1] == tile
        first = first + jnp.where(hit, told[3 * k + 1 : 3 * k + 2], 0.0)
        second = second + jnp.where(hit, told[3 * k + 2 : 3 * k + 3], 0.0)
    column_tile = jnp.floor(second * (1.0 / GROUPS))
    half = jnp.floor(column_tile * 0.5)
    key = 16.0 * (half + 1.0) * (column_tile - half) + first
    code = key * GROUPS + (second - column_tile * GROUPS)
    for n in range(entries // LANES):
        codes[b * (entries // LANES) + n] = code[:, n * LANES : (n + 1) * LANES]


INNER = [(j % 4, (j // 4 + j) % 4, (j + 3 * (j // 4)) % 4) for j in range(BATCH)]


def places(b, gx, gy, outward):
    core = gy % 2
    other = (core + b % 2) % 2
    turn = 1 + 2 * core if outward else 3 - 2 * other
    x, y, z = gx // 4, gx % 4, gy // 2
    xs = [((x + d * turn) % 4) * 4 for d in range(4)]
    ys = [(y + d * turn) % 4 for d in range(4)]
    zs = [((z + (b // 2 + d) * turn) % 4) * 2 + other for d in range(4)]
    return [(xs[dx] + ys[dy], zs[dz]) for dx, dy, dz in INNER]


def tile_of(slot, gx, gy):
    b, j = slot >> 4, slot & 15
    dx, dy, dz = j & 3, ((j >> 2) + j) & 3, ((b >> 1) + j + 3 * (j >> 2)) & 3
    core = gy % 2
    turn = 1 + 2 * core
    px = ((gx // 4 + dx * turn) & 3) * 4 + ((gx % 4 + dy * turn) & 3)
    return px * 8 + ((gy // 2 + dz * turn) & 3) * 2 + ((core + b) & 1)


def remote(source, target, send_sem, recv_sem, place):
    return pltpu.make_async_remote_copy(
        src_ref=source, dst_ref=target, send_sem=send_sem, recv_sem=recv_sem, device_id=place, device_id_type=MESH,
    )


def mask_basis(basis, extent):
    functions, cells = basis.shape
    atoms = functions // NB
    extent = extent.astype(F32)
    own = ones_where(iota((functions, atoms), 0) // NB == iota((functions, atoms), 1)).astype(BF16)
    half = (iota((functions, LANES), 1) // CY).astype(F32)
    low = dot(own, jnp.broadcast_to(extent[0:1], (LANES, atoms)).astype(BF16), NT) - half
    high = dot(own, jnp.broadcast_to(extent[1:2], (LANES, atoms)).astype(BF16), NT) - half
    for c in range(cells // LANES):
        row = c * (LANES // CY)
        inside = low <= float(row) if row < CX // 2 else high > float(row)
        lanes = slice(c * LANES, (c + 1) * LANES)
        basis[:, lanes] = basis[:, lanes] * ones_where(inside).astype(BF16)


def constants():
    row, lane = np.arange(WIDTH)[:, None], np.arange(WIDTH)[None, :]
    before = row < lane
    turned = (row // NB == lane % NB) & (row % NB == lane // NB)
    wide = np.arange(NB * LANES)[None, :]
    spread = (row // NB == wide // LANES) & (row % NB == wide % NB)
    square = np.concatenate([before, turned, row == lane], axis=1)
    return [np.asarray(x, np.float32) for x in (square, spread, spread.T)]


def collect(recv, got, b, spread, gathered, keys, groups):
    entries = BATCH * CAP
    own = iota((GROUPS, LANES), 0) == iota((GROUPS, LANES), 1) // CAP
    code = []
    for h in range(BATCH // GROUPS):
        lines = got[pl.ds(b * BATCH + h * GROUPS, GROUPS), 0, :]
        code.append(jnp.sum(jnp.where(own, lines, 0.0), axis=0, keepdims=True))
    code = jnp.concatenate(code, axis=1)
    key_row = jnp.floor(code * (1.0 / GROUPS))
    group_row = code - key_row * GROUPS
    key_rows = gathered.shape[0]
    onehot = ones_where(iota((key_rows, entries), 0).astype(F32) == key_row).astype(BF16)
    key = jnp.transpose(jnp.broadcast_to(key_row, (LANES, entries)))
    group = jnp.transpose(jnp.broadcast_to(group_row, (LANES, entries)))
    here = pl.ds(pl.multiple_of(b * entries, entries), entries)
    keys[here, :] = key
    groups[here, :] = group
    blocks = recv[pl.ds(b * BATCH, BATCH)].reshape(entries, WIDTH)
    wide = 2 * LANES
    inside = (iota((entries, wide), 1) % LANES // NB).astype(F32) == jnp.concatenate([group, group], axis=1)
    for c in range(NB // 2):
        lanes = slice(c * wide, (c + 1) * wide)
        spaced = jnp.where(inside, dot(blocks, spread[:, lanes]), 0.0).astype(BF16)
        gathered[:, lanes] = gathered[:, lanes] + dot(onehot, spaced)


def pick(b, picked, keys, groups, fold, spaced, back):
    entries = BATCH * CAP
    here = pl.ds(pl.multiple_of(b * entries, entries), entries)
    key, group = keys[here, :], groups[here, :]
    lane = iota((entries, LANES), 1).astype(F32)
    onehot = jnp.concatenate(
        [ones_where(lane + float(n * LANES) == key).astype(BF16) for n in range(picked.shape[0] // LANES)], axis=1
    )
    wide = 2 * LANES
    inside = (iota((entries, wide), 1) % LANES // NB).astype(F32) == jnp.concatenate([group, group], axis=1)
    for c in range(NB // 2):
        lanes = slice(c * wide, (c + 1) * wide)
        spaced[:, lanes] = jnp.where(inside, dot(onehot, picked[:, lanes]), 0.0).astype(BF16)
    blocks = dot(spaced[...], fold[...]).astype(BF16)
    back[pl.ds(b * BATCH, BATCH)] = blocks.reshape(BATCH, CAP, WIDTH)


def potential_of(charge, below, above, left, right):
    rows = charge.shape[0]
    lane = iota((rows, LANES), 1)
    row = iota((rows, LANES), 0)
    swapped = pltpu.roll(charge, CY, 1)
    first_of_above = pltpu.roll(above, CY, 1)[0:1]
    last_of_below = pltpu.roll(below, CY, 1)[rows - 1 : rows]
    up = jnp.where(row == rows - 1, first_of_above, pltpu.roll(swapped, rows - 1, 0))
    next_x = jnp.where(lane < CY, swapped, up)
    down = jnp.where(row == 0, last_of_below, pltpu.roll(swapped, 1, 0))
    last_x = jnp.where(lane < CY, down, swapped)
    next_y = jnp.where(lane % CY == CY - 1, pltpu.roll(right, CY - 1, 1), pltpu.roll(charge, LANES - 1, 1))
    last_y = jnp.where(lane % CY == 0, pltpu.roll(left, LANES - CY + 1, 1), pltpu.roll(charge, 1, 1))
    slope_x = 0.5 * (next_x - last_x)
    slope_y = 0.5 * (next_y - last_y)
    return charge * lax.rsqrt(
        1.0 + charge * charge + gradient_weight * (slope_x * slope_x + slope_y * slope_y)
    )


def whole_kernel(
    tiles_hbm, slots_hbm, sizes_hbm, density_hbm, extent_hbm, basis_hbm, ones_hbm, spread_hbm, fold_hbm,
    out_hbm, potential_hbm,
    tiles_ref, slots_ref, sizes_ref, density_ref, extent_ref, ones_ref, spread_ref, fold_ref, out_ref, potential_ref,
    basis, weighted, upright, chunks, recv, back, returned, codes, got, marks, picks, picks_turned, spread, fold, gathered, keys, groups,
    square, matrix, picked, spaced, charge, halo,
    send_sems, recv_sems, code_sems, return_sem, halo_send, halo_recv, local_sem,
):
    devices = chunks.shape[0]
    functions, cells = basis.shape
    atoms = functions // NB
    column_tiles = functions // LANES
    batches = devices // BATCH
    gx, gy = lax.axis_index("gx"), lax.axis_index("gy")
    load = pltpu.make_async_copy(basis_hbm, basis, local_sem.at[0])
    inputs = [
        pltpu.make_async_copy(source, target, local_sem.at[1 + n])
        for n, (source, target) in enumerate((
            (tiles_hbm, tiles_ref), (slots_hbm, slots_ref), (sizes_hbm, sizes_ref), (density_hbm, density_ref),
            (ones_hbm, ones_ref), (extent_hbm, extent_ref), (spread_hbm, spread_ref), (fold_hbm, fold_ref),
        ))
    ]
    for copy in inputs:
        copy.start()
    load.start()
    barrier = pltpu.get_barrier_semaphore()

    def greet(b, carry):
        for j, place in enumerate(places(b, gx, gy, True)):
            def signal():
                pl.semaphore_signal(barrier, inc=1, device_id=place, device_id_type=MESH)

            if j == 0:
                pl.when(b > 0)(signal)
            else:
                signal()
        return carry

    lax.fori_loop(0, batches, greet, 0)
    gathered[...] = jnp.zeros_like(gathered)
    for c in range(column_tiles):
        low, high = (c + 1) * LANES, (c // 3 + 1) * 3 * LANES
        if low < high:
            square[c, low:high, :] = jnp.zeros((high - low, LANES), F32)
        low, high = key_offset(c) + GROUPS * (c + 1), key_offset(c + 1)
        high = picked.shape[0] if c + 1 == column_tiles else high
        if low < high:
            picked[low:high, :] = jnp.zeros((high - low, picked.shape[1]), BF16)
    for copy in inputs[:5]:
        copy.wait()
    pairs = density_ref.shape[0]
    before, turned, eye = (ones_ref[:, n * WIDTH : (n + 1) * WIDTH].astype(BF16) for n in range(3))
    mask = size_mask_of(sizes_ref[...], eye)
    masked = jnp.where(mask, density_ref[...].astype(F32), 0.0).astype(BF16)
    blocks = jnp.concatenate([masked, dot(masked, turned).astype(BF16)], axis=0)
    asked = plan(tiles_ref[...], slots_ref, tile_of(iota((devices, 1), 0), gx, gy), before, marks)
    rows_per_batch = BATCH * CAP // LANES

    def push(b, carry):
        for j, place in enumerate(places(b, gx, gy, True)):
            slot = b * BATCH + j
            row = b * rows_per_batch + j * CAP // LANES

            def start():
                remote(codes.at[row], got.at[slot], send_sems.at[0], code_sems.at[b], place).start()
                remote(chunks.at[slot], recv.at[slot], send_sems.at[1], recv_sems.at[b], place).start()

            def keep():
                pltpu.make_async_copy(codes.at[0], got.at[0], code_sems.at[0]).start()
                pltpu.make_async_copy(chunks.at[0], recv.at[0], recv_sems.at[0]).start()

            if j == 0:
                pl.when(b > 0)(start)
                pl.when(b == 0)(keep)
            else:
                start()
        return carry

    def fill(n, carry):
        tile = tile_of(n * STEP + iota((1, STEP * CAP), 1) // CAP, gx, gy).astype(F32)
        pack(n, tile, asked, blocks, marks, chunks, codes, picks)
        return carry

    lax.fori_loop(0, devices // STEP, fill, 0)
    pl.semaphore_wait(barrier, devices - 1)
    lax.fori_loop(0, batches, push, 0)
    for copy in inputs[5:]:
        copy.wait()
    spread[...] = spread_ref[...].astype(BF16)
    fold[...] = fold_ref[...].astype(BF16)
    load.wait()
    mask_basis(basis, extent_ref[...])
    for c in range(column_tiles):
        lanes = slice(c * LANES, (c + 1) * LANES)
        upright[:, lanes] = jnp.transpose(basis[lanes, :].astype(F32)).astype(BF16)

    def arrive(b, carry):
        slots = pl.ds(b * BATCH, BATCH)
        remote(got.at[slots], got.at[slots], send_sems.at[0], code_sems.at[b], (gx, gy)).wait_recv()
        remote(recv.at[slots], recv.at[slots], send_sems.at[1], recv_sems.at[b], (gx, gy)).wait_recv()
        collect(recv, got, b, spread, gathered, keys, groups)
        return carry

    lax.fori_loop(0, batches, arrive, 0)
    for c in range(column_tiles):
        low = key_offset(c)
        count = GROUPS * (c + 1)
        for i in range(NB):
            block = gathered[low : low + count, i * LANES : (i + 1) * LANES]
            square[c, pl.ds(i, count, stride=NB), :] = block
        matrix[:, c * LANES : (c + 1) * LANES] = square[c].astype(BF16)
    step = 2 * LANES
    part = 3 * LANES
    for c in range(cells // step):
        columns = basis[:, c * step : (c + 1) * step]
        total = jnp.zeros((1, step), F32)
        for low in range(0, functions, part):
            product = dot(matrix[low : low + part, low:], columns[low:])
            product = product * columns[low : low + part].astype(F32)
            total = total + jnp.sum(product, axis=0, keepdims=True)
        charge[2 * c : 2 * c + 1, :] = total[:, :LANES]
        charge[2 * c + 1 : 2 * c + 2, :] = total[:, LANES:]
    edges = [
        remote(charge, halo.at[n], halo_send.at[n], halo_recv.at[n], place)
        for n, place in enumerate(
            (((gx + 1) % 16, gy), ((gx + 15) % 16, gy), (gx, (gy + 7) % 8), (gx, (gy + 1) % 8))
        )
    ]
    for copy in edges:
        copy.start()
    for copy in edges:
        copy.wait()
    potential = potential_of(charge[...], halo[0], halo[1], halo[3], halo[2])
    for half in range(2):
        rows = potential if half == 0 else pltpu.roll(potential, CY, 1)
        potential_ref[pl.ds(half, CX // 2, stride=2), :] = rows[:, :CY]
    potential_out = pltpu.make_async_copy(potential_ref, potential_hbm, local_sem.at[1])
    potential_out.start()
    for c in range(cells // LANES):
        lanes = slice(c * LANES, (c + 1) * LANES)
        weighted[:, lanes] = (basis[:, lanes].astype(F32) * potential[c : c + 1]).astype(BF16)
    for start in range(0, column_tiles, 2):
        stop = min(start + 2, column_tiles)
        high = stop * LANES
        product = dot(weighted[:high, :], upright[:, start * LANES : high])
        for c in range(start, stop):
            square[c, :high, :] = product[:, (c - start) * LANES : (c - start + 1) * LANES]
            low = key_offset(c)
            count = GROUPS * (c + 1)
            for i in range(NB):
                block = square[c, pl.ds(i, count, stride=NB), :]
                picked[low : low + count, i * LANES : (i + 1) * LANES] = block.astype(BF16)
    keep = pltpu.make_async_copy(back.at[0], returned.at[0], return_sem)

    def give(b, carry):
        pick(b, picked, keys, groups, fold, spaced, back)
        for j, place in enumerate(places(b, gx, gy, False)):
            slot = b * BATCH + j

            def start():
                remote(back.at[slot], returned.at[slot], send_sems.at[2], return_sem, place).start()

            if j == 0:
                pl.when(b > 0)(start)
                pl.when(b == 0)(keep.start)
            else:
                start()
        return carry

    lax.fori_loop(0, batches, give, 0)
    for half in range(2):
        for n in range(devices * CAP // 512):
            part = picks[n * 512 : (n + 1) * 512, half * pairs : (half + 1) * pairs].astype(F32)
            lanes = half * devices * CAP + n * 512
            picks_turned[:, lanes : lanes + 512] = jnp.transpose(part).astype(BF16)
    mask = size_mask_of(sizes_ref[...], eye)
    remote(returned, returned, send_sems.at[2], return_sem, (gx, gy)).wait_recv()
    blocks = returned[...].reshape(devices * CAP, WIDTH)
    blocks = jnp.concatenate([blocks, dot(blocks, turned).astype(BF16)], axis=0)
    out_ref[...] = jnp.where(mask, dot(picks_turned[...], blocks) * float(cells) ** -0.5, 0.0)
    out = pltpu.make_async_copy(out_ref, out_hbm, local_sem.at[2])
    out.start()
    out.wait()
    potential_out.wait()
    others = pl.ds(0, devices - 1)
    remote(got.at[others], got.at[others], send_sems.at[0], code_sems.at[0], (gx, gy)).wait_send()
    remote(chunks.at[others], recv.at[others], send_sems.at[1], recv_sems.at[0], (gx, gy)).wait_send()
    remote(back.at[others], returned.at[others], send_sems.at[2], return_sem, (gx, gy)).wait_send()


def finish_kernel(summed, field, out, potential):
    out[...] = summed[...]
    potential[...] = field[...]


VMEM_SPEC = pl.BlockSpec(memory_space=pltpu.VMEM)
ANY_SPEC = pl.BlockSpec(memory_space=pl.ANY)
DMA = pltpu.SemaphoreType.DMA


def shards(density, pair_tiles, pair_slots, pair_sizes, basis_table, tile_extent):
    devices = lax.axis_size("gx") * lax.axis_size("gy")
    pairs, targets = pair_tiles.shape
    atoms = tile_extent.shape[2]
    functions, cells = basis_table.shape[1:]
    rows = cells // LANES
    key_rows = key_offset(functions // LANES)
    chunk = pltpu.VMEM((devices, CAP, WIDTH), BF16)
    entries = devices * CAP
    spaced = NB * LANES
    results = pl.pallas_call(
        whole_kernel,
        name="whole",
        out_shape=[
            jax.ShapeDtypeStruct((pairs, WIDTH), F32),
            jax.ShapeDtypeStruct((CX, CY), F32),
        ],
        in_specs=[ANY_SPEC] * 9,
        out_specs=[ANY_SPEC] * 2,
        scratch_shapes=[
            pltpu.VMEM((targets, pairs), I32),
            pltpu.VMEM((targets, 2, pairs), I32),
            pltpu.VMEM((2, pairs), I32),
            pltpu.VMEM((pairs, WIDTH), BF16),
            pltpu.VMEM((2, atoms), I32),
            pltpu.VMEM((WIDTH, 3 * WIDTH), F32),
            pltpu.VMEM((WIDTH, spaced), F32),
            pltpu.VMEM((spaced, WIDTH), F32),
            pltpu.VMEM((pairs, WIDTH), F32),
            pltpu.VMEM((CX, CY), F32),
            pltpu.VMEM((functions, cells), BF16),
            pltpu.VMEM((functions, cells), BF16),
            pltpu.VMEM((cells, functions), BF16),
            chunk,
            chunk,
            chunk,
            chunk,
            pltpu.VMEM((devices * CAP // LANES, 1, LANES), F32),
            pltpu.VMEM((devices, 1, LANES), F32),
            pltpu.VMEM((devices, pairs), F32),
            pltpu.VMEM((entries, 2 * pairs), BF16),
            pltpu.VMEM((pairs, 2 * entries), BF16),
            pltpu.VMEM((WIDTH, spaced), BF16),
            pltpu.VMEM((spaced, WIDTH), BF16),
            pltpu.VMEM((key_rows, spaced), F32),
            pltpu.VMEM((entries, LANES), F32),
            pltpu.VMEM((entries, LANES), F32),
            pltpu.VMEM((functions // LANES, functions, LANES), F32),
            pltpu.VMEM((functions, functions), BF16),
            pltpu.VMEM((-(-key_rows // LANES) * LANES, spaced), BF16),
            pltpu.VMEM((BATCH * CAP, spaced), BF16),
            pltpu.VMEM((rows, LANES), F32),
            pltpu.VMEM((4, rows, LANES), F32),
            DMA((3,)),
            DMA((devices // BATCH,)),
            DMA((devices // BATCH,)),
            DMA,
            DMA((4,)),
            DMA((4,)),
            DMA((9,)),
        ],
        compiler_params=pltpu.CompilerParams(
            vmem_limit_bytes=VMEM_BYTES, collective_id=1, has_side_effects=True
        ),
    )(pair_tiles.T, pair_slots.transpose(1, 2, 0), pair_sizes.T, density, tile_extent[0], basis_table[0], *constants())
    return tuple(pl.pallas_call(
        finish_kernel,
        name="finish",
        out_shape=[jax.ShapeDtypeStruct(result.shape, result.dtype) for result in results],
        in_specs=[VMEM_SPEC] * 2,
        out_specs=[VMEM_SPEC] * 2,
        compiler_params=pltpu.CompilerParams(vmem_limit_bytes=VMEM_BYTES),
    )(*results))


def solution(mesh):
    in_specs = (
        P(("gx", "gy"), None),
        P(("gx", "gy"), None),
        P(("gx", "gy"), None, None),
        P(("gx", "gy"), None),
        P(("gx", "gy"), None, None),
        P(("gx", "gy"), None, None),
    )
    out_specs = (P(("gx", "gy"), None), P("gx", "gy"))
    return jax.shard_map(shards, mesh=mesh, in_specs=in_specs, out_specs=out_specs, check_vma=False)
```

```python
import functools

import jax
import jax.numpy as jnp
import numpy as np
from jax import lax
from jax.experimental import pallas as pl
from jax.experimental.pallas import tpu as pltpu
from jax.sharding import PartitionSpec as P

NB = 16
CX = 32
CY = 64
LANES = 128
GROUPS = LANES // NB
WIDTH = NB * NB
CAP = 16
BATCH = 16
STEP = 32
MESH = pl.DeviceIdType.MESH
F32 = jnp.float32
BF16 = jnp.bfloat16
I32 = jnp.int32
VMEM_BYTES = 60 * 1024 * 1024
gradient_weight = 1.0
NT = (((1,), (1,)), ((), ()))


def iota(shape, dim):
    return lax.broadcasted_iota(I32, shape, dim)


def dot(a, b, dims=(((1,), (0,)), ((), ()))):
    return lax.dot_general(a, b, dims, preferred_element_type=F32)


def span(n, size):
    return pl.ds(n * size if isinstance(n, int) else pl.multiple_of(n * size, size), size)


def ones_where(condition):
    return jnp.where(condition, 1.0, 0.0)


def size_mask_of(sizes, eye):
    pairs = sizes.shape[1]
    wide = sizes.astype(F32)
    first = dot(eye, jnp.broadcast_to(wide[0:1], (WIDTH, pairs)).astype(BF16), NT)
    second = dot(eye, jnp.broadcast_to(wide[1:2], (WIDTH, pairs)).astype(BF16), NT)
    lane = iota((pairs, WIDTH), 1)
    row = (lane // NB).astype(F32)
    col = (lane % NB).astype(F32)
    return (row < first) & (col < second)


def key_offset(column_tile):
    half = column_tile // 2
    return 16 * (half + 1) * (half + column_tile % 2)


def plan(tiles, slots_ref, tile_id, before, marks):
    targets, pairs = tiles.shape
    devices = marks.shape[0]
    chosen = jnp.zeros((devices, pairs), F32)
    kind = jnp.zeros((devices, pairs), F32)
    asked = []
    for k in range(targets):
        mark = ones_where(tiles[k : k + 1] == tile_id)
        slots = slots_ref[k].astype(F32)
        first, second = slots[0:1], slots[1:2]
        chosen = chosen + mark
        kind = kind + mark * (ones_where(first < second) + 2.0 * ones_where(first > second))
        asked += [tiles[k : k + 1].astype(F32), jnp.minimum(first, second), jnp.maximum(first, second)]
    rank = dot(chosen.astype(BF16), before)
    marks[...] = jnp.where(chosen > 0.5, rank * 4.0 + kind, -4.0)
    return jnp.concatenate(asked + [jnp.zeros((16 - 3 * targets, pairs), F32)], axis=0).astype(BF16)


def pack(b, tile, asked, blocks, marks, chunks, codes, picks):
    pairs = marks.shape[1]
    entries = STEP * CAP
    own = (4 * (iota((entries, pairs), 0) % CAP)).astype(F32)
    rows = jnp.broadcast_to(marks[pl.ds(b * STEP, STEP), :][:, None, :], (STEP, CAP, pairs))
    rows = rows.reshape(entries, pairs) - own
    same, upper, lower = ones_where(rows == 0.0), ones_where(rows == 1.0), ones_where(rows == 2.0)
    straight = upper.astype(BF16)
    across = (same + lower).astype(BF16)
    here = span(b, entries)
    picks[here, :pairs] = straight
    picks[here, pairs:] = across
    weights = jnp.concatenate([(same + 2.0 * upper).astype(BF16), (2.0 * lower).astype(BF16)], axis=1)
    chunks[pl.ds(b * STEP, STEP)] = dot(weights, blocks).astype(BF16).reshape(STEP, CAP, WIDTH)
    told = dot(asked, straight + across, NT)
    first = jnp.zeros((1, entries), F32)
    second = jnp.zeros((1, entries), F32)
    for k in range(asked.shape[0] // 3):
        hit = told[3 * k : 3 * k + 1] == tile
        first = first + jnp.where(hit, told[3 * k + 1 : 3 * k + 2], 0.0)
        second = second + jnp.where(hit, told[3 * k + 2 : 3 * k + 3], 0.0)
    column_tile = jnp.floor(second * (1.0 / GROUPS))
    half = jnp.floor(column_tile * 0.5)
    key = 16.0 * (half + 1.0) * (column_tile - half) + first
    code = key * GROUPS + (second - column_tile * GROUPS)
    for n in range(entries // LANES):
        codes[b * (entries // LANES) + n] = code[:, n * LANES : (n + 1) * LANES]


INNER = [(j % 4, (j // 4 + j) % 4, (j + 3 * (j // 4)) % 4) for j in range(BATCH)]


def places(b, gx, gy, outward):
    core = gy % 2
    other = (core + b % 2) % 2
    turn = 1 + 2 * core if outward else 3 - 2 * other
    x, y, z = gx // 4, gx % 4, gy // 2
    xs = [((x + d * turn) % 4) * 4 for d in range(4)]
    ys = [(y + d * turn) % 4 for d in range(4)]
    zs = [((z + (b // 2 + d) * turn) % 4) * 2 + other for d in range(4)]
    return [(xs[dx] + ys[dy], zs[dz]) for dx, dy, dz in INNER]


def tile_of(slot, gx, gy):
    b, j = slot >> 4, slot & 15
    dx, dy, dz = j & 3, ((j >> 2) + j) & 3, ((b >> 1) + j + 3 * (j >> 2)) & 3
    core = gy % 2
    turn = 1 + 2 * core
    px = ((gx // 4 + dx * turn) & 3) * 4 + ((gx % 4 + dy * turn) & 3)
    return px * 8 + ((gy // 2 + dz * turn) & 3) * 2 + ((core + b) & 1)


def remote(source, target, send_sem, recv_sem, place):
    return pltpu.make_async_remote_copy(
        src_ref=source, dst_ref=target, send_sem=send_sem, recv_sem=recv_sem, device_id=place, device_id_type=MESH,
    )


def mask_basis(basis, extent):
    functions, cells = basis.shape
    atoms = functions // NB
    extent = extent.astype(F32)
    own = ones_where(iota((functions, atoms), 0) // NB == iota((functions, atoms), 1)).astype(BF16)
    half = (iota((functions, LANES), 1) // CY).astype(F32)
    low = dot(own, jnp.broadcast_to(extent[0:1], (LANES, atoms)).astype(BF16), NT) - half
    high = dot(own, jnp.broadcast_to(extent[1:2], (LANES, atoms)).astype(BF16), NT) - half
    for c in range(cells // LANES):
        row = c * (LANES // CY)
        inside = low <= float(row) if row < CX // 2 else high > float(row)
        lanes = slice(c * LANES, (c + 1) * LANES)
        basis[:, lanes] = basis[:, lanes] * ones_where(inside).astype(BF16)


def constants():
    row, lane = np.arange(WIDTH)[:, None], np.arange(WIDTH)[None, :]
    before = row < lane
    turned = (row // NB == lane % NB) & (row % NB == lane // NB)
    wide = np.arange(NB * LANES)[None, :]
    spread = (row // NB == wide // LANES) & (row % NB == wide % NB)
    square = np.concatenate([before, turned, row == lane], axis=1)
    return [np.asarray(x, np.float32) for x in (square, spread, spread.T)]


def collect(recv, got, b, spread, gathered, keys, groups):
    entries = BATCH * CAP
    own = iota((GROUPS, LANES), 0) == iota((GROUPS, LANES), 1) // CAP
    code = []
    for h in range(BATCH // GROUPS):
        lines = got[pl.ds(b * BATCH + h * GROUPS, GROUPS), 0, :]
        code.append(jnp.sum(jnp.where(own, lines, 0.0), axis=0, keepdims=True))
    code = jnp.concatenate(code, axis=1)
    key_row = jnp.floor(code * (1.0 / GROUPS))
    group_row = code - key_row * GROUPS
    key_rows = gathered.shape[0]
    onehot = ones_where(iota((key_rows, entries), 0).astype(F32) == key_row).astype(BF16)
    key = jnp.transpose(jnp.broadcast_to(key_row, (LANES, entries)))
    group = jnp.transpose(jnp.broadcast_to(group_row, (LANES, entries)))
    here = span(b, entries)
    keys[here, :] = key
    groups[here, :] = group
    blocks = recv[pl.ds(b * BATCH, BATCH)].reshape(entries, WIDTH)
    wide = 2 * LANES
    inside = (iota((entries, wide), 1) % LANES // NB).astype(F32) == jnp.concatenate([group, group], axis=1)
    for c in range(NB // 2):
        lanes = slice(c * wide, (c + 1) * wide)
        spaced = jnp.where(inside, dot(blocks, spread[:, lanes]), 0.0).astype(BF16)
        gathered[:, lanes] = gathered[:, lanes] + dot(onehot, spaced)


def pick(b, picked, keys, groups, fold, spaced, back):
    entries = BATCH * CAP
    here = span(b, entries)
    key, group = keys[here, :], groups[here, :]
    lane = iota((entries, LANES), 1).astype(F32)
    onehot = jnp.concatenate(
        [ones_where(lane + float(n * LANES) == key).astype(BF16) for n in range(picked.shape[0] // LANES)], axis=1
    )
    wide = 2 * LANES
    inside = (iota((entries, wide), 1) % LANES // NB).astype(F32) == jnp.concatenate([group, group], axis=1)
    for c in range(NB // 2):
        lanes = slice(c * wide, (c + 1) * wide)
        spaced[:, lanes] = jnp.where(inside, dot(onehot, picked[:, lanes]), 0.0).astype(BF16)
    blocks = dot(spaced[...], fold[...]).astype(BF16)
    back[pl.ds(b * BATCH, BATCH)] = blocks.reshape(BATCH, CAP, WIDTH)


def potential_of(charge, below, above, left, right):
    rows = charge.shape[0]
    lane = iota((rows, LANES), 1)
    row = iota((rows, LANES), 0)
    swapped = pltpu.roll(charge, CY, 1)
    first_of_above = pltpu.roll(above, CY, 1)[0:1]
    last_of_below = pltpu.roll(below, CY, 1)[rows - 1 : rows]
    up = jnp.where(row == rows - 1, first_of_above, pltpu.roll(swapped, rows - 1, 0))
    next_x = jnp.where(lane < CY, swapped, up)
    down = jnp.where(row == 0, last_of_below, pltpu.roll(swapped, 1, 0))
    last_x = jnp.where(lane < CY, down, swapped)
    next_y = jnp.where(lane % CY == CY - 1, pltpu.roll(right, CY - 1, 1), pltpu.roll(charge, LANES - 1, 1))
    last_y = jnp.where(lane % CY == 0, pltpu.roll(left, LANES - CY + 1, 1), pltpu.roll(charge, 1, 1))
    slope_x = 0.5 * (next_x - last_x)
    slope_y = 0.5 * (next_y - last_y)
    return charge * lax.rsqrt(
        1.0 + charge * charge + gradient_weight * (slope_x * slope_x + slope_y * slope_y)
    )


def whole_kernel(
    tiles_hbm, slots_hbm, sizes_hbm, density_hbm, extent_hbm, basis_hbm, ones_hbm, spread_hbm, fold_hbm,
    out_hbm, potential_hbm,
    tiles_ref, slots_ref, sizes_ref, density_ref, extent_ref, ones_ref, spread_ref, fold_ref, out_ref, potential_ref,
    basis, weighted, upright, chunks, recv, back, returned, codes, got, marks, picks, picks_turned, spread, fold, gathered, keys, groups,
    square, matrix, picked, spaced, charge, halo,
    send_sems, recv_sems, code_sems, return_sem, halo_send, halo_recv, local_sem,
):
    devices = chunks.shape[0]
    functions, cells = basis.shape
    atoms = functions // NB
    column_tiles = functions // LANES
    batches = devices // BATCH
    gx, gy = lax.axis_index("gx"), lax.axis_index("gy")
    load = pltpu.make_async_copy(basis_hbm, basis, local_sem.at[0])
    inputs = [
        pltpu.make_async_copy(source, target, local_sem.at[1 + n])
        for n, (source, target) in enumerate((
            (tiles_hbm, tiles_ref), (slots_hbm, slots_ref), (sizes_hbm, sizes_ref), (density_hbm, density_ref),
            (ones_hbm, ones_ref), (extent_hbm, extent_ref), (spread_hbm, spread_ref), (fold_hbm, fold_ref),
        ))
    ]
    for copy in inputs:
        copy.start()
    load.start()
    barrier = pltpu.get_barrier_semaphore()

    def greet(b, carry):
        for j, place in enumerate(places(b, gx, gy, True)):
            def signal():
                pl.semaphore_signal(barrier, inc=1, device_id=place, device_id_type=MESH)

            if j == 0:
                pl.when(b > 0)(signal)
            else:
                signal()
        return carry

    lax.fori_loop(0, batches, greet, 0)
    gathered[...] = jnp.zeros_like(gathered)
    for c in range(column_tiles):
        low, high = (c + 1) * LANES, (c // 3 + 1) * 3 * LANES
        if low < high:
            square[c, low:high, :] = jnp.zeros((high - low, LANES), F32)
        low, high = key_offset(c) + GROUPS * (c + 1), key_offset(c + 1)
        high = picked.shape[0] if c + 1 == column_tiles else high
        if low < high:
            picked[low:high, :] = jnp.zeros((high - low, picked.shape[1]), BF16)
    for copy in inputs[:5]:
        copy.wait()
    pairs = density_ref.shape[0]
    before, turned, eye = (ones_ref[:, n * WIDTH : (n + 1) * WIDTH].astype(BF16) for n in range(3))
    mask = size_mask_of(sizes_ref[...], eye)
    masked = jnp.where(mask, density_ref[...].astype(F32), 0.0).astype(BF16)
    blocks = jnp.concatenate([masked, dot(masked, turned).astype(BF16)], axis=0)
    asked = plan(tiles_ref[...], slots_ref, tile_of(iota((devices, 1), 0), gx, gy), before, marks)
    rows_per_batch = BATCH * CAP // LANES

    def push(b, carry):
        for j, place in enumerate(places(b, gx, gy, True)):
            slot = b * BATCH + j
            row = b * rows_per_batch + j * CAP // LANES

            def start():
                remote(codes.at[row], got.at[slot], send_sems.at[0], code_sems.at[b], place).start()
                remote(chunks.at[slot], recv.at[slot], send_sems.at[1], recv_sems.at[b], place).start()

            def keep():
                pltpu.make_async_copy(codes.at[0], got.at[0], code_sems.at[0]).start()
                pltpu.make_async_copy(chunks.at[0], recv.at[0], recv_sems.at[0]).start()

            if j == 0:
                pl.when(b > 0)(start)
                pl.when(b == 0)(keep)
            else:
                start()
        return carry

    for n in range(devices // STEP):
        tile = tile_of(n * STEP + iota((1, STEP * CAP), 1) // CAP, gx, gy).astype(F32)
        pack(n, tile, asked, blocks, marks, chunks, codes, picks)
    pl.semaphore_wait(barrier, devices - 1)
    lax.fori_loop(0, batches, push, 0)
    for copy in inputs[5:]:
        copy.wait()
    spread[...] = spread_ref[...].astype(BF16)
    fold[...] = fold_ref[...].astype(BF16)
    load.wait()
    mask_basis(basis, extent_ref[...])
    for c in range(column_tiles):
        lanes = slice(c * LANES, (c + 1) * LANES)
        upright[:, lanes] = jnp.transpose(basis[lanes, :].astype(F32)).astype(BF16)

    def arrive(b, carry):
        slots = pl.ds(b * BATCH, BATCH)
        remote(got.at[slots], got.at[slots], send_sems.at[0], code_sems.at[b], (gx, gy)).wait_recv()
        remote(recv.at[slots], recv.at[slots], send_sems.at[1], recv_sems.at[b], (gx, gy)).wait_recv()
        collect(recv, got, b, spread, gathered, keys, groups)
        return carry

    lax.fori_loop(0, batches, arrive, 0)
    for c in range(column_tiles):
        low = key_offset(c)
        count = GROUPS * (c + 1)
        for i in range(NB):
            block = gathered[low : low + count, i * LANES : (i + 1) * LANES]
            square[c, pl.ds(i, count, stride=NB), :] = block
        matrix[:, c * LANES : (c + 1) * LANES] = square[c].astype(BF16)
    step = 2 * LANES
    part = 3 * LANES
    for c in range(cells // step):
        columns = basis[:, c * step : (c + 1) * step]
        total = jnp.zeros((1, step), F32)
        for low in range(0, functions, part):
            product = dot(matrix[low : low + part, low:], columns[low:])
            product = product * columns[low : low + part].astype(F32)
            total = total + jnp.sum(product, axis=0, keepdims=True)
        charge[2 * c : 2 * c + 1, :] = total[:, :LANES]
        charge[2 * c + 1 : 2 * c + 2, :] = total[:, LANES:]
    edges = [
        remote(charge, halo.at[n], halo_send.at[n], halo_recv.at[n], place)
        for n, place in enumerate(
            (((gx + 1) % 16, gy), ((gx + 15) % 16, gy), (gx, (gy + 7) % 8), (gx, (gy + 1) % 8))
        )
    ]
    for copy in edges:
        copy.start()
    for copy in edges:
        copy.wait()
    potential = potential_of(charge[...], halo[0], halo[1], halo[3], halo[2])
    for half in range(2):
        rows = potential if half == 0 else pltpu.roll(potential, CY, 1)
        potential_ref[pl.ds(half, CX // 2, stride=2), :] = rows[:, :CY]
    potential_out = pltpu.make_async_copy(potential_ref, potential_hbm, local_sem.at[1])
    potential_out.start()
    for c in range(cells // LANES):
        lanes = slice(c * LANES, (c + 1) * LANES)
        weighted[:, lanes] = (basis[:, lanes].astype(F32) * potential[c : c + 1]).astype(BF16)
    for start in range(0, column_tiles, 2):
        stop = min(start + 2, column_tiles)
        high = stop * LANES
        product = dot(weighted[:high, :], upright[:, start * LANES : high])
        for c in range(start, stop):
            square[c, :high, :] = product[:, (c - start) * LANES : (c - start + 1) * LANES]
            low = key_offset(c)
            count = GROUPS * (c + 1)
            for i in range(NB):
                block = square[c, pl.ds(i, count, stride=NB), :]
                picked[low : low + count, i * LANES : (i + 1) * LANES] = block.astype(BF16)
    keep = pltpu.make_async_copy(back.at[0], returned.at[0], return_sem)

    for b in range(batches):
        pick(b, picked, keys, groups, fold, spaced.at[b % 2], back)
        for j, place in enumerate(places(b, gx, gy, False)):
            slot = b * BATCH + j
            if slot == 0:
                keep.start()
            else:
                remote(back.at[slot], returned.at[slot], send_sems.at[2], return_sem, place).start()
    for half in range(2):
        for n in range(devices * CAP // 512):
            part = picks[n * 512 : (n + 1) * 512, half * pairs : (half + 1) * pairs].astype(F32)
            lanes = half * devices * CAP + n * 512
            picks_turned[:, lanes : lanes + 512] = jnp.transpose(part).astype(BF16)
    mask = size_mask_of(sizes_ref[...], eye)
    remote(returned, returned, send_sems.at[2], return_sem, (gx, gy)).wait_recv()
    blocks = returned[...].reshape(devices * CAP, WIDTH)
    blocks = jnp.concatenate([blocks, dot(blocks, turned).astype(BF16)], axis=0)
    out_ref[...] = jnp.where(mask, dot(picks_turned[...], blocks) * float(cells) ** -0.5, 0.0)
    out = pltpu.make_async_copy(out_ref, out_hbm, local_sem.at[2])
    out.start()
    out.wait()
    potential_out.wait()
    others = pl.ds(0, devices - 1)
    remote(got.at[others], got.at[others], send_sems.at[0], code_sems.at[0], (gx, gy)).wait_send()
    remote(chunks.at[others], recv.at[others], send_sems.at[1], recv_sems.at[0], (gx, gy)).wait_send()
    remote(back.at[others], returned.at[others], send_sems.at[2], return_sem, (gx, gy)).wait_send()


def finish_kernel(summed, field, out, potential):
    out[...] = summed[...]
    potential[...] = field[...]


VMEM_SPEC = pl.BlockSpec(memory_space=pltpu.VMEM)
ANY_SPEC = pl.BlockSpec(memory_space=pl.ANY)
DMA = pltpu.SemaphoreType.DMA


def shards(density, pair_tiles, pair_slots, pair_sizes, basis_table, tile_extent):
    devices = lax.axis_size("gx") * lax.axis_size("gy")
    pairs, targets = pair_tiles.shape
    atoms = tile_extent.shape[2]
    functions, cells = basis_table.shape[1:]
    rows = cells // LANES
    key_rows = key_offset(functions // LANES)
    chunk = pltpu.VMEM((devices, CAP, WIDTH), BF16)
    entries = devices * CAP
    spaced = NB * LANES
    results = pl.pallas_call(
        whole_kernel,
        name="whole",
        out_shape=[
            jax.ShapeDtypeStruct((pairs, WIDTH), F32),
            jax.ShapeDtypeStruct((CX, CY), F32),
        ],
        in_specs=[ANY_SPEC] * 9,
        out_specs=[ANY_SPEC] * 2,
        scratch_shapes=[
            pltpu.VMEM((targets, pairs), I32),
            pltpu.VMEM((targets, 2, pairs), I32),
            pltpu.VMEM((2, pairs), I32),
            pltpu.VMEM((pairs, WIDTH), BF16),
            pltpu.VMEM((2, atoms), I32),
            pltpu.VMEM((WIDTH, 3 * WIDTH), F32),
            pltpu.VMEM((WIDTH, spaced), F32),
            pltpu.VMEM((spaced, WIDTH), F32),
            pltpu.VMEM((pairs, WIDTH), F32),
            pltpu.VMEM((CX, CY), F32),
            pltpu.VMEM((functions, cells), BF16),
            pltpu.VMEM((functions, cells), BF16),
            pltpu.VMEM((cells, functions), BF16),
            chunk,
            chunk,
            chunk,
            chunk,
            pltpu.VMEM((devices * CAP // LANES, 1, LANES), F32),
            pltpu.VMEM((devices, 1, LANES), F32),
            pltpu.VMEM((devices, pairs), F32),
            pltpu.VMEM((entries, 2 * pairs), BF16),
            pltpu.VMEM((pairs, 2 * entries), BF16),
            pltpu.VMEM((WIDTH, spaced), BF16),
            pltpu.VMEM((spaced, WIDTH), BF16),
            pltpu.VMEM((key_rows, spaced), F32),
            pltpu.VMEM((entries, LANES), F32),
            pltpu.VMEM((entries, LANES), F32),
            pltpu.VMEM((functions // LANES, functions, LANES), F32),
            pltpu.VMEM((functions, functions), BF16),
            pltpu.VMEM((-(-key_rows // LANES) * LANES, spaced), BF16),
            pltpu.VMEM((2, BATCH * CAP, spaced), BF16),
            pltpu.VMEM((rows, LANES), F32),
            pltpu.VMEM((4, rows, LANES), F32),
            DMA((3,)),
            DMA((devices // BATCH,)),
            DMA((devices // BATCH,)),
            DMA,
            DMA((4,)),
            DMA((4,)),
            DMA((9,)),
        ],
        compiler_params=pltpu.CompilerParams(
            vmem_limit_bytes=VMEM_BYTES, collective_id=1, has_side_effects=True
        ),
    )(pair_tiles.T, pair_slots.transpose(1, 2, 0), pair_sizes.T, density, tile_extent[0], basis_table[0], *constants())
    return tuple(pl.pallas_call(
        finish_kernel,
        name="finish",
        out_shape=[jax.ShapeDtypeStruct(result.shape, result.dtype) for result in results],
        in_specs=[VMEM_SPEC] * 2,
        out_specs=[VMEM_SPEC] * 2,
        compiler_params=pltpu.CompilerParams(vmem_limit_bytes=VMEM_BYTES),
    )(*results))


def solution(mesh):
    in_specs = (
        P(("gx", "gy"), None),
        P(("gx", "gy"), None),
        P(("gx", "gy"), None, None),
        P(("gx", "gy"), None),
        P(("gx", "gy"), None, None),
        P(("gx", "gy"), None, None),
    )
    out_specs = (P(("gx", "gy"), None), P("gx", "gy"))
    return jax.shard_map(shards, mesh=mesh, in_specs=in_specs, out_specs=out_specs, check_vma=False)
```

```python
import functools

import jax
import jax.numpy as jnp
import numpy as np
from jax import lax
from jax.experimental import pallas as pl
from jax.experimental.pallas import tpu as pltpu
from jax.sharding import PartitionSpec as P

NB = 16
CX = 32
CY = 64
LANES = 128
GROUPS = LANES // NB
WIDTH = NB * NB
CAP = 16
BATCH = 16
STEP = 32
MESH = pl.DeviceIdType.MESH
F32 = jnp.float32
BF16 = jnp.bfloat16
I32 = jnp.int32
VMEM_BYTES = 60 * 1024 * 1024
gradient_weight = 1.0
NT = (((1,), (1,)), ((), ()))


def iota(shape, dim):
    return lax.broadcasted_iota(I32, shape, dim)


def dot(a, b, dims=(((1,), (0,)), ((), ()))):
    return lax.dot_general(a, b, dims, preferred_element_type=F32)


def ones_where(condition):
    return jnp.where(condition, 1.0, 0.0)


def size_mask_of(sizes, eye):
    pairs = sizes.shape[1]
    wide = sizes.astype(F32)
    first = dot(eye, jnp.broadcast_to(wide[0:1], (WIDTH, pairs)).astype(BF16), NT)
    second = dot(eye, jnp.broadcast_to(wide[1:2], (WIDTH, pairs)).astype(BF16), NT)
    lane = iota((pairs, WIDTH), 1)
    row = (lane // NB).astype(F32)
    col = (lane % NB).astype(F32)
    return (row < first) & (col < second)


def key_offset(column_tile):
    half = column_tile // 2
    return 16 * (half + 1) * (half + column_tile % 2)


def plan(tiles, slots_ref, tile_id, before, marks):
    targets, pairs = tiles.shape
    devices = marks.shape[0]
    chosen = jnp.zeros((devices, pairs), F32)
    kind = jnp.zeros((devices, pairs), F32)
    asked = []
    for k in range(targets):
        mark = ones_where(tiles[k : k + 1] == tile_id)
        slots = slots_ref[k].astype(F32)
        first, second = slots[0:1], slots[1:2]
        chosen = chosen + mark
        kind = kind + mark * (ones_where(first < second) + 2.0 * ones_where(first > second))
        asked += [tiles[k : k + 1].astype(F32), jnp.minimum(first, second), jnp.maximum(first, second)]
    rank = dot(chosen.astype(BF16), before)
    marks[...] = jnp.where(chosen > 0.5, rank * 4.0 + kind, -4.0)
    return jnp.concatenate(asked + [jnp.zeros((16 - 3 * targets, pairs), F32)], axis=0).astype(BF16)


def pack(b, tile, asked, blocks, marks, chunks, codes, picks):
    pairs = marks.shape[1]
    entries = STEP * CAP
    own = (4 * (iota((entries, pairs), 0) % CAP)).astype(F32)
    rows = jnp.broadcast_to(marks[pl.ds(b * STEP, STEP), :][:, None, :], (STEP, CAP, pairs))
    rows = rows.reshape(entries, pairs) - own
    same, upper, lower = ones_where(rows == 0.0), ones_where(rows == 1.0), ones_where(rows == 2.0)
    straight = upper.astype(BF16)
    across = (same + lower).astype(BF16)
    here = pl.ds(pl.multiple_of(b * entries, entries), entries)
    picks[here, :pairs] = straight
    picks[here, pairs:] = across
    weights = jnp.concatenate([(same + 2.0 * upper).astype(BF16), (2.0 * lower).astype(BF16)], axis=1)
    chunks[pl.ds(b * STEP, STEP)] = dot(weights, blocks).astype(BF16).reshape(STEP, CAP, WIDTH)
    told = dot(asked, straight + across, NT)
    first = jnp.zeros((1, entries), F32)
    second = jnp.zeros((1, entries), F32)
    for k in range(asked.shape[0] // 3):
        hit = told[3 * k : 3 * k + 1] == tile
        first = first + jnp.where(hit, told[3 * k + 1 : 3 * k + 2], 0.0)
        second = second + jnp.where(hit, told[3 * k + 2 : 3 * k + 3], 0.0)
    column_tile = jnp.floor(second * (1.0 / GROUPS))
    half = jnp.floor(column_tile * 0.5)
    key = 16.0 * (half + 1.0) * (column_tile - half) + first
    code = key * GROUPS + (second - column_tile * GROUPS)
    for n in range(entries // LANES):
        codes[b * (entries // LANES) + n] = code[:, n * LANES : (n + 1) * LANES]


INNER = [(j % 4, (j // 4 + j) % 4, (j + 3 * (j // 4)) % 4) for j in range(BATCH)]


def places(b, gx, gy, outward):
    core = gy % 2
    other = (core + b % 2) % 2
    turn = 1 + 2 * core if outward else 3 - 2 * other
    x, y, z = gx // 4, gx % 4, gy // 2
    xs = [((x + d * turn) % 4) * 4 for d in range(4)]
    ys = [(y + d * turn) % 4 for d in range(4)]
    zs = [((z + (b // 2 + d) * turn) % 4) * 2 + other for d in range(4)]
    return [(xs[dx] + ys[dy], zs[dz]) for dx, dy, dz in INNER]


def tile_of(slot, gx, gy):
    b, j = slot >> 4, slot & 15
    dx, dy, dz = j & 3, ((j >> 2) + j) & 3, ((b >> 1) + j + 3 * (j >> 2)) & 3
    core = gy % 2
    turn = 1 + 2 * core
    px = ((gx // 4 + dx * turn) & 3) * 4 + ((gx % 4 + dy * turn) & 3)
    return px * 8 + ((gy // 2 + dz * turn) & 3) * 2 + ((core + b) & 1)


def remote(source, target, send_sem, recv_sem, place):
    return pltpu.make_async_remote_copy(
        src_ref=source, dst_ref=target, send_sem=send_sem, recv_sem=recv_sem, device_id=place, device_id_type=MESH,
    )


def mask_basis(basis, extent):
    functions, cells = basis.shape
    atoms = functions // NB
    extent = extent.astype(F32)
    own = ones_where(iota((functions, atoms), 0) // NB == iota((functions, atoms), 1)).astype(BF16)
    half = (iota((functions, LANES), 1) // CY).astype(F32)
    low = dot(own, jnp.broadcast_to(extent[0:1], (LANES, atoms)).astype(BF16), NT) - half
    high = dot(own, jnp.broadcast_to(extent[1:2], (LANES, atoms)).astype(BF16), NT) - half
    for c in range(cells // LANES):
        row = c * (LANES // CY)
        inside = low <= float(row) if row < CX // 2 else high > float(row)
        lanes = slice(c * LANES, (c + 1) * LANES)
        basis[:, lanes] = basis[:, lanes] * ones_where(inside).astype(BF16)


def constants():
    row, lane = np.arange(WIDTH)[:, None], np.arange(WIDTH)[None, :]
    before = row < lane
    turned = (row // NB == lane % NB) & (row % NB == lane // NB)
    wide = np.arange(NB * LANES)[None, :]
    spread = (row // NB == wide // LANES) & (row % NB == wide % NB)
    square = np.concatenate([before, turned, row == lane], axis=1)
    return [np.asarray(x, np.float32) for x in (square, spread, spread.T)]


def collect(recv, got, b, spread, gathered, keys, groups):
    entries = BATCH * CAP
    own = iota((GROUPS, LANES), 0) == iota((GROUPS, LANES), 1) // CAP
    code = []
    for h in range(BATCH // GROUPS):
        lines = got[pl.ds(b * BATCH + h * GROUPS, GROUPS), 0, :]
        code.append(jnp.sum(jnp.where(own, lines, 0.0), axis=0, keepdims=True))
    code = jnp.concatenate(code, axis=1)
    key_row = jnp.floor(code * (1.0 / GROUPS))
    group_row = code - key_row * GROUPS
    key_rows = gathered.shape[0]
    onehot = ones_where(iota((key_rows, entries), 0).astype(F32) == key_row).astype(BF16)
    key = jnp.transpose(jnp.broadcast_to(key_row, (LANES, entries)))
    group = jnp.transpose(jnp.broadcast_to(group_row, (LANES, entries)))
    here = pl.ds(pl.multiple_of(b * entries, entries), entries)
    keys[here, :] = key
    groups[here, :] = group
    blocks = recv[pl.ds(b * BATCH, BATCH)].reshape(entries, WIDTH)
    wide = 2 * LANES
    inside = (iota((entries, wide), 1) % LANES // NB).astype(F32) == jnp.concatenate([group, group], axis=1)
    for c in range(NB // 2):
        lanes = slice(c * wide, (c + 1) * wide)
        spaced = jnp.where(inside, dot(blocks, spread[:, lanes]), 0.0).astype(BF16)
        gathered[:, lanes] = gathered[:, lanes] + dot(onehot, spaced)


def pick(b, picked, keys, groups, fold, spaced, back):
    entries = BATCH * CAP
    here = pl.ds(pl.multiple_of(b * entries, entries), entries)
    key, group = keys[here, :], groups[here, :]
    lane = iota((entries, LANES), 1).astype(F32)
    onehot = jnp.concatenate(
        [ones_where(lane + float(n * LANES) == key).astype(BF16) for n in range(picked.shape[0] // LANES)], axis=1
    )
    wide = 2 * LANES
    inside = (iota((entries, wide), 1) % LANES // NB).astype(F32) == jnp.concatenate([group, group], axis=1)
    for c in range(NB // 2):
        lanes = slice(c * wide, (c + 1) * wide)
        spaced[:, lanes] = jnp.where(inside, dot(onehot, picked[:, lanes]), 0.0).astype(BF16)
    blocks = dot(spaced[...], fold[...]).astype(BF16)
    back[pl.ds(b * BATCH, BATCH)] = blocks.reshape(BATCH, CAP, WIDTH)


def potential_of(charge, below, above, left, right):
    rows = charge.shape[0]
    lane = iota((rows, LANES), 1)
    row = iota((rows, LANES), 0)
    swapped = pltpu.roll(charge, CY, 1)
    first_of_above = pltpu.roll(above, CY, 1)[0:1]
    last_of_below = pltpu.roll(below, CY, 1)[rows - 1 : rows]
    up = jnp.where(row == rows - 1, first_of_above, pltpu.roll(swapped, rows - 1, 0))
    next_x = jnp.where(lane < CY, swapped, up)
    down = jnp.where(row == 0, last_of_below, pltpu.roll(swapped, 1, 0))
    last_x = jnp.where(lane < CY, down, swapped)
    next_y = jnp.where(lane % CY == CY - 1, pltpu.roll(right, CY - 1, 1), pltpu.roll(charge, LANES - 1, 1))
    last_y = jnp.where(lane % CY == 0, pltpu.roll(left, LANES - CY + 1, 1), pltpu.roll(charge, 1, 1))
    slope_x = 0.5 * (next_x - last_x)
    slope_y = 0.5 * (next_y - last_y)
    return charge * lax.rsqrt(
        1.0 + charge * charge + gradient_weight * (slope_x * slope_x + slope_y * slope_y)
    )


def whole_kernel(
    tiles_hbm, slots_hbm, sizes_hbm, density_hbm, extent_hbm, basis_hbm, ones_hbm, spread_hbm, fold_hbm,
    out_hbm, potential_hbm,
    tiles_ref, slots_ref, sizes_ref, density_ref, extent_ref, ones_ref, spread_ref, fold_ref, out_ref, potential_ref,
    basis, permuted, weighted, upright, chunks, recv, back, returned, codes, got, marks, picks, picks_turned, spread, fold, gathered, keys, groups,
    matrix, picked, spaced, charge, halo,
    send_sems, recv_sems, code_sems, return_sem, halo_send, halo_recv, local_sem,
):
    devices = chunks.shape[0]
    functions, cells = basis.shape
    atoms = functions // NB
    column_tiles = functions // LANES
    batches = devices // BATCH
    gx, gy = lax.axis_index("gx"), lax.axis_index("gy")
    load = pltpu.make_async_copy(basis_hbm, basis, local_sem.at[0])
    inputs = [
        pltpu.make_async_copy(source, target, local_sem.at[1 + n])
        for n, (source, target) in enumerate((
            (tiles_hbm, tiles_ref), (slots_hbm, slots_ref), (sizes_hbm, sizes_ref), (density_hbm, density_ref),
            (ones_hbm, ones_ref), (extent_hbm, extent_ref), (spread_hbm, spread_ref), (fold_hbm, fold_ref),
        ))
    ]
    for copy in inputs:
        copy.start()
    load.start()
    barrier = pltpu.get_barrier_semaphore()

    def greet(b, carry):
        for j, place in enumerate(places(b, gx, gy, True)):
            def signal():
                pl.semaphore_signal(barrier, inc=1, device_id=place, device_id_type=MESH)

            if j == 0:
                pl.when(b > 0)(signal)
            else:
                signal()
        return carry

    lax.fori_loop(0, batches, greet, 0)
    gathered[...] = jnp.zeros_like(gathered)
    for c in range(column_tiles):
        low, high = (c + 1) * LANES, (c // 3 + 1) * 3 * LANES
        if low < high:
            matrix[low:high, c * LANES : (c + 1) * LANES] = jnp.zeros((high - low, LANES), BF16)
    low, high = key_offset(column_tiles), picked.shape[0]
    picked[low:high, :] = jnp.zeros((high - low, picked.shape[1]), BF16)
    for copy in inputs[:5]:
        copy.wait()
    pairs = density_ref.shape[0]
    before, turned, eye = (ones_ref[:, n * WIDTH : (n + 1) * WIDTH].astype(BF16) for n in range(3))
    mask = size_mask_of(sizes_ref[...], eye)
    masked = jnp.where(mask, density_ref[...].astype(F32), 0.0).astype(BF16)
    blocks = jnp.concatenate([masked, dot(masked, turned).astype(BF16)], axis=0)
    asked = plan(tiles_ref[...], slots_ref, tile_of(iota((devices, 1), 0), gx, gy), before, marks)
    rows_per_batch = BATCH * CAP // LANES

    def push(b, carry):
        for j, place in enumerate(places(b, gx, gy, True)):
            slot = b * BATCH + j
            row = b * rows_per_batch + j * CAP // LANES

            def start():
                remote(codes.at[row], got.at[slot], send_sems.at[0], code_sems.at[b], place).start()
                remote(chunks.at[slot], recv.at[slot], send_sems.at[1], recv_sems.at[b], place).start()

            def keep():
                pltpu.make_async_copy(codes.at[0], got.at[0], code_sems.at[0]).start()
                pltpu.make_async_copy(chunks.at[0], recv.at[0], recv_sems.at[0]).start()

            if j == 0:
                pl.when(b > 0)(start)
                pl.when(b == 0)(keep)
            else:
                start()
        return carry

    def fill(n, carry):
        tile = tile_of(n * STEP + iota((1, STEP * CAP), 1) // CAP, gx, gy).astype(F32)
        pack(n, tile, asked, blocks, marks, chunks, codes, picks)
        return carry

    lax.fori_loop(0, devices // STEP, fill, 0)
    pl.semaphore_wait(barrier, devices - 1)
    lax.fori_loop(0, batches, push, 0)
    for copy in inputs[5:]:
        copy.wait()
    spread[...] = spread_ref[...].astype(BF16)
    fold[...] = fold_ref[...].astype(BF16)
    load.wait()
    mask_basis(basis, extent_ref[...])
    row, lane = iota((LANES, LANES), 0), iota((LANES, LANES), 1)
    regroup = ones_where(lane == row % GROUPS * NB + row // GROUPS).astype(BF16)
    for c in range(column_tiles):
        lanes = slice(c * LANES, (c + 1) * LANES)
        upright[:, lanes] = jnp.transpose(basis[lanes, :].astype(F32)).astype(BF16)
        permuted[lanes, :] = dot(regroup, basis[lanes, :]).astype(BF16)

    def arrive(b, carry):
        slots = pl.ds(b * BATCH, BATCH)
        remote(got.at[slots], got.at[slots], send_sems.at[0], code_sems.at[b], (gx, gy)).wait_recv()
        remote(recv.at[slots], recv.at[slots], send_sems.at[1], recv_sems.at[b], (gx, gy)).wait_recv()
        collect(recv, got, b, spread, gathered, keys, groups)
        return carry

    lax.fori_loop(0, batches, arrive, 0)
    for c in range(column_tiles):
        for n in range(c + 1):
            low = key_offset(c) + n * GROUPS
            block = [gathered[low : low + GROUPS, i * LANES : (i + 1) * LANES] for i in range(NB)]
            block = jnp.concatenate(block, axis=0).astype(BF16)
            matrix[n * LANES : (n + 1) * LANES, c * LANES : (c + 1) * LANES] = block
    step = 2 * LANES
    part = 3 * LANES
    for c in range(cells // step):
        columns = basis[:, c * step : (c + 1) * step]
        total = jnp.zeros((1, step), F32)
        for low in range(0, functions, part):
            product = dot(matrix[low : low + part, low:], columns[low:])
            product = product * permuted[low : low + part, c * step : (c + 1) * step].astype(F32)
            total = total + jnp.sum(product, axis=0, keepdims=True)
        charge[2 * c : 2 * c + 1, :] = total[:, :LANES]
        charge[2 * c + 1 : 2 * c + 2, :] = total[:, LANES:]
    edges = [
        remote(charge, halo.at[n], halo_send.at[n], halo_recv.at[n], place)
        for n, place in enumerate(
            (((gx + 1) % 16, gy), ((gx + 15) % 16, gy), (gx, (gy + 7) % 8), (gx, (gy + 1) % 8))
        )
    ]
    for copy in edges:
        copy.start()
    for copy in edges:
        copy.wait()
    potential = potential_of(charge[...], halo[0], halo[1], halo[3], halo[2])
    for half in range(2):
        rows = potential if half == 0 else pltpu.roll(potential, CY, 1)
        potential_ref[pl.ds(half, CX // 2, stride=2), :] = rows[:, :CY]
    potential_out = pltpu.make_async_copy(potential_ref, potential_hbm, local_sem.at[1])
    potential_out.start()
    for c in range(cells // LANES):
        lanes = slice(c * LANES, (c + 1) * LANES)
        weighted[:, lanes] = (permuted[:, lanes].astype(F32) * potential[c : c + 1]).astype(BF16)
    for start in range(0, column_tiles, 2):
        stop = min(start + 2, column_tiles)
        high = stop * LANES
        product = dot(weighted[:high, :], upright[:, start * LANES : high])
        for c in range(start, stop):
            tile = product[:, c * LANES - start * LANES : (c + 1 - start) * LANES]
            for n in range(0, c + 1, 2):
                low = key_offset(c) + n * GROUPS
                for i in range(NB):
                    pieces = [
                        tile[m * LANES + i * GROUPS : m * LANES + (i + 1) * GROUPS]
                        if m <= c else jnp.zeros((GROUPS, LANES), F32)
                        for m in (n, n + 1)
                    ]
                    piece = jnp.concatenate(pieces, axis=0).astype(BF16)
                    picked[low : low + 2 * GROUPS, i * LANES : (i + 1) * LANES] = piece
    keep = pltpu.make_async_copy(back.at[0], returned.at[0], return_sem)

    def give(b, carry):
        pick(b, picked, keys, groups, fold, spaced, back)
        for j, place in enumerate(places(b, gx, gy, False)):
            slot = b * BATCH + j

            def start():
                remote(back.at[slot], returned.at[slot], send_sems.at[2], return_sem, place).start()

            if j == 0:
                pl.when(b > 0)(start)
                pl.when(b == 0)(keep.start)
            else:
                start()
        return carry

    lax.fori_loop(0, batches, give, 0)
    for half in range(2):
        for n in range(devices * CAP // 512):
            part = picks[n * 512 : (n + 1) * 512, half * pairs : (half + 1) * pairs].astype(F32)
            lanes = half * devices * CAP + n * 512
            picks_turned[:, lanes : lanes + 512] = jnp.transpose(part).astype(BF16)
    mask = size_mask_of(sizes_ref[...], eye)
    remote(returned, returned, send_sems.at[2], return_sem, (gx, gy)).wait_recv()
    blocks = returned[...].reshape(devices * CAP, WIDTH)
    blocks = jnp.concatenate([blocks, dot(blocks, turned).astype(BF16)], axis=0)
    out_ref[...] = jnp.where(mask, dot(picks_turned[...], blocks) * float(cells) ** -0.5, 0.0)
    out = pltpu.make_async_copy(out_ref, out_hbm, local_sem.at[2])
    out.start()
    out.wait()
    potential_out.wait()
    others = pl.ds(0, devices - 1)
    remote(got.at[others], got.at[others], send_sems.at[0], code_sems.at[0], (gx, gy)).wait_send()
    remote(chunks.at[others], recv.at[others], send_sems.at[1], recv_sems.at[0], (gx, gy)).wait_send()
    remote(back.at[others], returned.at[others], send_sems.at[2], return_sem, (gx, gy)).wait_send()


def finish_kernel(summed, field, out, potential):
    out[...] = summed[...]
    potential[...] = field[...]


VMEM_SPEC = pl.BlockSpec(memory_space=pltpu.VMEM)
ANY_SPEC = pl.BlockSpec(memory_space=pl.ANY)
DMA = pltpu.SemaphoreType.DMA


def shards(density, pair_tiles, pair_slots, pair_sizes, basis_table, tile_extent):
    devices = lax.axis_size("gx") * lax.axis_size("gy")
    pairs, targets = pair_tiles.shape
    atoms = tile_extent.shape[2]
    functions, cells = basis_table.shape[1:]
    rows = cells // LANES
    key_rows = key_offset(functions // LANES)
    chunk = pltpu.VMEM((devices, CAP, WIDTH), BF16)
    entries = devices * CAP
    spaced = NB * LANES
    results = pl.pallas_call(
        whole_kernel,
        name="whole",
        out_shape=[
            jax.ShapeDtypeStruct((pairs, WIDTH), F32),
            jax.ShapeDtypeStruct((CX, CY), F32),
        ],
        in_specs=[ANY_SPEC] * 9,
        out_specs=[ANY_SPEC] * 2,
        scratch_shapes=[
            pltpu.VMEM((targets, pairs), I32),
            pltpu.VMEM((targets, 2, pairs), I32),
            pltpu.VMEM((2, pairs), I32),
            pltpu.VMEM((pairs, WIDTH), BF16),
            pltpu.VMEM((2, atoms), I32),
            pltpu.VMEM((WIDTH, 3 * WIDTH), F32),
            pltpu.VMEM((WIDTH, spaced), F32),
            pltpu.VMEM((spaced, WIDTH), F32),
            pltpu.VMEM((pairs, WIDTH), F32),
            pltpu.VMEM((CX, CY), F32),
            pltpu.VMEM((functions, cells), BF16),
            pltpu.VMEM((functions, cells), BF16),
            pltpu.VMEM((functions, cells), BF16),
            pltpu.VMEM((cells, functions), BF16),
            chunk,
            chunk,
            chunk,
            chunk,
            pltpu.VMEM((devices * CAP // LANES, 1, LANES), F32),
            pltpu.VMEM((devices, 1, LANES), F32),
            pltpu.VMEM((devices, pairs), F32),
            pltpu.VMEM((entries, 2 * pairs), BF16),
            pltpu.VMEM((pairs, 2 * entries), BF16),
            pltpu.VMEM((WIDTH, spaced), BF16),
            pltpu.VMEM((spaced, WIDTH), BF16),
            pltpu.VMEM((key_rows, spaced), F32),
            pltpu.VMEM((entries, LANES), F32),
            pltpu.VMEM((entries, LANES), F32),
            pltpu.VMEM((functions, functions), BF16),
            pltpu.VMEM((-(-key_rows // LANES) * LANES, spaced), BF16),
            pltpu.VMEM((BATCH * CAP, spaced), BF16),
            pltpu.VMEM((rows, LANES), F32),
            pltpu.VMEM((4, rows, LANES), F32),
            DMA((3,)),
            DMA((devices // BATCH,)),
            DMA((devices // BATCH,)),
            DMA,
            DMA((4,)),
            DMA((4,)),
            DMA((9,)),
        ],
        compiler_params=pltpu.CompilerParams(
            vmem_limit_bytes=VMEM_BYTES, collective_id=1, has_side_effects=True
        ),
    )(pair_tiles.T, pair_slots.transpose(1, 2, 0), pair_sizes.T, density, tile_extent[0], basis_table[0], *constants())
    return tuple(pl.pallas_call(
        finish_kernel,
        name="finish",
        out_shape=[jax.ShapeDtypeStruct(result.shape, result.dtype) for result in results],
        in_specs=[VMEM_SPEC] * 2,
        out_specs=[VMEM_SPEC] * 2,
        compiler_params=pltpu.CompilerParams(vmem_limit_bytes=VMEM_BYTES),
    )(*results))


def solution(mesh):
    in_specs = (
        P(("gx", "gy"), None),
        P(("gx", "gy"), None),
        P(("gx", "gy"), None, None),
        P(("gx", "gy"), None),
        P(("gx", "gy"), None, None),
        P(("gx", "gy"), None, None),
    )
    out_specs = (P(("gx", "gy"), None), P("gx", "gy"))
    return jax.shard_map(shards, mesh=mesh, in_specs=in_specs, out_specs=out_specs, check_vma=False)
```

```python
import functools

import jax
import jax.numpy as jnp
import numpy as np
from jax import lax
from jax.experimental import pallas as pl
from jax.experimental.pallas import tpu as pltpu
from jax.sharding import PartitionSpec as P

NB = 16
CX = 32
CY = 64
LANES = 128
GROUPS = LANES // NB
WIDTH = NB * NB
CAP = 16
BATCH = 16
STEP = 32
MESH = pl.DeviceIdType.MESH
F32 = jnp.float32
BF16 = jnp.bfloat16
I32 = jnp.int32
VMEM_BYTES = 60 * 1024 * 1024
gradient_weight = 1.0
NT = (((1,), (1,)), ((), ()))


def iota(shape, dim):
    return lax.broadcasted_iota(I32, shape, dim)


def dot(a, b, dims=(((1,), (0,)), ((), ()))):
    return lax.dot_general(a, b, dims, preferred_element_type=F32)


def ones_where(condition):
    return jnp.where(condition, 1.0, 0.0)


def size_mask_of(sizes, eye):
    pairs = sizes.shape[1]
    wide = sizes.astype(F32)
    first = dot(eye, jnp.broadcast_to(wide[0:1], (WIDTH, pairs)).astype(BF16), NT)
    second = dot(eye, jnp.broadcast_to(wide[1:2], (WIDTH, pairs)).astype(BF16), NT)
    lane = iota((pairs, WIDTH), 1)
    row = (lane // NB).astype(F32)
    col = (lane % NB).astype(F32)
    return (row < first) & (col < second)


def key_offset(column_tile):
    half = column_tile // 2
    return 16 * (half + 1) * (half + column_tile % 2)


def plan(tiles, slots_ref, tile_id, before, marks):
    targets, pairs = tiles.shape
    devices = marks.shape[0]
    chosen = jnp.zeros((devices, pairs), F32)
    kind = jnp.zeros((devices, pairs), F32)
    asked = []
    for k in range(targets):
        mark = ones_where(tiles[k : k + 1] == tile_id)
        slots = slots_ref[k].astype(F32)
        first, second = slots[0:1], slots[1:2]
        chosen = chosen + mark
        kind = kind + mark * (ones_where(first < second) + 2.0 * ones_where(first > second))
        asked += [tiles[k : k + 1].astype(F32), jnp.minimum(first, second), jnp.maximum(first, second)]
    rank = dot(chosen.astype(BF16), before)
    marks[...] = jnp.where(chosen > 0.5, rank * 4.0 + kind, -4.0)
    return jnp.concatenate(asked + [jnp.zeros((16 - 3 * targets, pairs), F32)], axis=0).astype(BF16)


def pack(b, tile, asked, blocks, marks, chunks, codes, picks):
    pairs = marks.shape[1]
    entries = STEP * CAP
    own = (4 * (iota((entries, pairs), 0) % CAP)).astype(F32)
    rows = jnp.broadcast_to(marks[pl.ds(b * STEP, STEP), :][:, None, :], (STEP, CAP, pairs))
    rows = rows.reshape(entries, pairs) - own
    same, upper, lower = ones_where(rows == 0.0), ones_where(rows == 1.0), ones_where(rows == 2.0)
    straight = upper.astype(BF16)
    across = (same + lower).astype(BF16)
    here = pl.ds(pl.multiple_of(b * entries, entries), entries)
    picks[here, :pairs] = straight
    picks[here, pairs:] = across
    weights = jnp.concatenate([(same + 2.0 * upper).astype(BF16), (2.0 * lower).astype(BF16)], axis=1)
    chunks[pl.ds(b * STEP, STEP)] = dot(weights, blocks).astype(BF16).reshape(STEP, CAP, WIDTH)
    told = dot(asked, straight + across, NT)
    first = jnp.zeros((1, entries), F32)
    second = jnp.zeros((1, entries), F32)
    for k in range(asked.shape[0] // 3):
        hit = told[3 * k : 3 * k + 1] == tile
        first = first + jnp.where(hit, told[3 * k + 1 : 3 * k + 2], 0.0)
        second = second + jnp.where(hit, told[3 * k + 2 : 3 * k + 3], 0.0)
    column_tile = jnp.floor(second * (1.0 / GROUPS))
    half = jnp.floor(column_tile * 0.5)
    key = 16.0 * (half + 1.0) * (column_tile - half) + first
    code = key * GROUPS + (second - column_tile * GROUPS)
    for n in range(entries // LANES):
        codes[b * (entries // LANES) + n] = code[:, n * LANES : (n + 1) * LANES]


INNER = [(j % 4, (j // 4 + j) % 4, (j + 3 * (j // 4)) % 4) for j in range(BATCH)]


def places(b, gx, gy, outward):
    core = gy % 2
    other = (core + b % 2) % 2
    turn = 1 + 2 * core if outward else 3 - 2 * other
    x, y, z = gx // 4, gx % 4, gy // 2
    xs = [((x + d * turn) % 4) * 4 for d in range(4)]
    ys = [(y + d * turn) % 4 for d in range(4)]
    zs = [((z + (b // 2 + d) * turn) % 4) * 2 + other for d in range(4)]
    return [(xs[dx] + ys[dy], zs[dz]) for dx, dy, dz in INNER]


def tile_of(slot, gx, gy):
    b, j = slot >> 4, slot & 15
    dx, dy, dz = j & 3, ((j >> 2) + j) & 3, ((b >> 1) + j + 3 * (j >> 2)) & 3
    core = gy % 2
    turn = 1 + 2 * core
    px = ((gx // 4 + dx * turn) & 3) * 4 + ((gx % 4 + dy * turn) & 3)
    return px * 8 + ((gy // 2 + dz * turn) & 3) * 2 + ((core + b) & 1)


def remote(source, target, send_sem, recv_sem, place):
    return pltpu.make_async_remote_copy(
        src_ref=source, dst_ref=target, send_sem=send_sem, recv_sem=recv_sem, device_id=place, device_id_type=MESH,
    )


def mask_basis(basis, extent):
    functions, cells = basis.shape
    atoms = functions // NB
    extent = extent.astype(F32)
    own = ones_where(iota((functions, atoms), 0) // NB == iota((functions, atoms), 1)).astype(BF16)
    half = (iota((functions, LANES), 1) // CY).astype(F32)
    low = dot(own, jnp.broadcast_to(extent[0:1], (LANES, atoms)).astype(BF16), NT) - half
    high = dot(own, jnp.broadcast_to(extent[1:2], (LANES, atoms)).astype(BF16), NT) - half
    for c in range(cells // LANES):
        row = c * (LANES // CY)
        inside = low <= float(row) if row < CX // 2 else high > float(row)
        lanes = slice(c * LANES, (c + 1) * LANES)
        basis[:, lanes] = basis[:, lanes] * ones_where(inside).astype(BF16)


def constants():
    row, lane = np.arange(WIDTH)[:, None], np.arange(WIDTH)[None, :]
    before = row < lane
    turned = (row // NB == lane % NB) & (row % NB == lane // NB)
    wide = np.arange(NB * LANES)[None, :]
    spread = (row // NB == wide // LANES) & (row % NB == wide % NB)
    square = np.concatenate([before, turned, row == lane], axis=1)
    return [np.asarray(x, np.float32) for x in (square, spread, spread.T)]


def collect(recv, got, b, spread, gathered, keys, groups):
    entries = BATCH * CAP
    own = iota((GROUPS, LANES), 0) == iota((GROUPS, LANES), 1) // CAP
    code = []
    for h in range(BATCH // GROUPS):
        lines = got[pl.ds(b * BATCH + h * GROUPS, GROUPS), 0, :]
        code.append(jnp.sum(jnp.where(own, lines, 0.0), axis=0, keepdims=True))
    code = jnp.concatenate(code, axis=1)
    key_row = jnp.floor(code * (1.0 / GROUPS))
    group_row = code - key_row * GROUPS
    key_rows = gathered.shape[0]
    onehot = ones_where(iota((key_rows, entries), 0).astype(F32) == key_row).astype(BF16)
    key = jnp.transpose(jnp.broadcast_to(key_row, (LANES, entries)))
    group = jnp.transpose(jnp.broadcast_to(group_row, (LANES, entries)))
    here = pl.ds(pl.multiple_of(b * entries, entries), entries)
    keys[here, :] = key
    groups[here, :] = group
    blocks = recv[pl.ds(b * BATCH, BATCH)].reshape(entries, WIDTH)
    wide = 2 * LANES
    inside = (iota((entries, wide), 1) % LANES // NB).astype(F32) == jnp.concatenate([group, group], axis=1)
    for c in range(NB // 2):
        lanes = slice(c * wide, (c + 1) * wide)
        spaced = jnp.where(inside, dot(blocks, spread[:, lanes]), 0.0).astype(BF16)
        gathered[:, lanes] = gathered[:, lanes] + dot(onehot, spaced)


def pick(b, picked, keys, groups, fold, spaced, back):
    entries = BATCH * CAP
    here = pl.ds(pl.multiple_of(b * entries, entries), entries)
    key, group = keys[here, :], groups[here, :]
    lane = iota((entries, LANES), 1).astype(F32)
    onehot = jnp.concatenate(
        [ones_where(lane + float(n * LANES) == key).astype(BF16) for n in range(picked.shape[0] // LANES)], axis=1
    )
    wide = 2 * LANES
    inside = (iota((entries, wide), 1) % LANES // NB).astype(F32) == jnp.concatenate([group, group], axis=1)
    for c in range(NB // 2):
        lanes = slice(c * wide, (c + 1) * wide)
        spaced[:, lanes] = jnp.where(inside, dot(onehot, picked[:, lanes]), 0.0).astype(BF16)
    blocks = dot(spaced[...], fold[...]).astype(BF16)
    back[pl.ds(b * BATCH, BATCH)] = blocks.reshape(BATCH, CAP, WIDTH)


def potential_of(charge, below, above, left, right):
    rows = charge.shape[0]
    lane = iota((rows, LANES), 1)
    row = iota((rows, LANES), 0)
    swapped = pltpu.roll(charge, CY, 1)
    first_of_above = pltpu.roll(above, CY, 1)[0:1]
    last_of_below = pltpu.roll(below, CY, 1)[rows - 1 : rows]
    up = jnp.where(row == rows - 1, first_of_above, pltpu.roll(swapped, rows - 1, 0))
    next_x = jnp.where(lane < CY, swapped, up)
    down = jnp.where(row == 0, last_of_below, pltpu.roll(swapped, 1, 0))
    last_x = jnp.where(lane < CY, down, swapped)
    next_y = jnp.where(lane % CY == CY - 1, pltpu.roll(right, CY - 1, 1), pltpu.roll(charge, LANES - 1, 1))
    last_y = jnp.where(lane % CY == 0, pltpu.roll(left, LANES - CY + 1, 1), pltpu.roll(charge, 1, 1))
    slope_x = 0.5 * (next_x - last_x)
    slope_y = 0.5 * (next_y - last_y)
    return charge * lax.rsqrt(
        1.0 + charge * charge + gradient_weight * (slope_x * slope_x + slope_y * slope_y)
    )


def whole_kernel(
    tiles_hbm, slots_hbm, sizes_hbm, density_hbm, extent_hbm, basis_hbm, ones_hbm, spread_hbm, fold_hbm,
    out_hbm, potential_hbm,
    tiles_ref, slots_ref, sizes_ref, density_ref, extent_ref, ones_ref, spread_ref, fold_ref, out_ref, potential_ref,
    basis, permuted, weighted, upright, chunks, recv, back, returned, codes, got, marks, picks, picks_turned, spread, fold, gathered, keys, groups,
    matrix, picked, spaced, charge, halo,
    send_sems, recv_sems, code_sems, return_sem, halo_send, halo_recv, local_sem,
):
    devices = chunks.shape[0]
    functions, cells = basis.shape
    atoms = functions // NB
    column_tiles = functions // LANES
    batches = devices // BATCH
    gx, gy = lax.axis_index("gx"), lax.axis_index("gy")
    load = pltpu.make_async_copy(basis_hbm, basis, local_sem.at[0])
    inputs = [
        pltpu.make_async_copy(source, target, local_sem.at[1 + n])
        for n, (source, target) in enumerate((
            (tiles_hbm, tiles_ref), (slots_hbm, slots_ref), (sizes_hbm, sizes_ref), (density_hbm, density_ref),
            (ones_hbm, ones_ref), (extent_hbm, extent_ref), (spread_hbm, spread_ref), (fold_hbm, fold_ref),
        ))
    ]
    for copy in inputs:
        copy.start()
    load.start()
    barrier = pltpu.get_barrier_semaphore()

    def greet(b, carry):
        for j, place in enumerate(places(b, gx, gy, True)):
            def signal():
                pl.semaphore_signal(barrier, inc=1, device_id=place, device_id_type=MESH)

            if j == 0:
                pl.when(b > 0)(signal)
            else:
                signal()
        return carry

    lax.fori_loop(0, batches, greet, 0)
    gathered[...] = jnp.zeros_like(gathered)
    for c in range(column_tiles):
        low, high = (c + 1) * LANES, (c // 3 + 1) * 3 * LANES
        if low < high:
            matrix[low:high, c * LANES : (c + 1) * LANES] = jnp.zeros((high - low, LANES), BF16)
    low, high = key_offset(column_tiles), picked.shape[0]
    picked[low:high, :] = jnp.zeros((high - low, picked.shape[1]), BF16)
    for copy in inputs[:5]:
        copy.wait()
    pairs = density_ref.shape[0]
    before, turned, eye = (ones_ref[:, n * WIDTH : (n + 1) * WIDTH].astype(BF16) for n in range(3))
    mask = size_mask_of(sizes_ref[...], eye)
    masked = jnp.where(mask, density_ref[...].astype(F32), 0.0).astype(BF16)
    blocks = jnp.concatenate([masked, dot(masked, turned).astype(BF16)], axis=0)
    asked = plan(tiles_ref[...], slots_ref, tile_of(iota((devices, 1), 0), gx, gy), before, marks)
    rows_per_batch = BATCH * CAP // LANES

    def push(b, carry):
        for j, place in enumerate(places(b, gx, gy, True)):
            slot = b * BATCH + j
            row = b * rows_per_batch + j * CAP // LANES

            def start():
                remote(codes.at[row], got.at[slot], send_sems.at[0], code_sems.at[b], place).start()
                remote(chunks.at[slot], recv.at[slot], send_sems.at[1], recv_sems.at[b], place).start()

            def keep():
                pltpu.make_async_copy(codes.at[0], got.at[0], code_sems.at[0]).start()
                pltpu.make_async_copy(chunks.at[0], recv.at[0], recv_sems.at[0]).start()

            if j == 0:
                pl.when(b > 0)(start)
                pl.when(b == 0)(keep)
            else:
                start()
        return carry

    def fill(n, carry):
        tile = tile_of(n * STEP + iota((1, STEP * CAP), 1) // CAP, gx, gy).astype(F32)
        pack(n, tile, asked, blocks, marks, chunks, codes, picks)
        return carry

    lax.fori_loop(0, devices // STEP, fill, 0)
    pl.semaphore_wait(barrier, devices - 1)
    lax.fori_loop(0, batches, push, 0)
    for copy in inputs[5:]:
        copy.wait()
    spread[...] = spread_ref[...].astype(BF16)
    fold[...] = fold_ref[...].astype(BF16)
    load.wait()
    mask_basis(basis, extent_ref[...])
    row, lane = iota((LANES, LANES), 0), iota((LANES, LANES), 1)
    regroup = ones_where(lane == row % GROUPS * NB + row // GROUPS).astype(BF16)
    for c in range(column_tiles):
        lanes = slice(c * LANES, (c + 1) * LANES)
        upright[:, lanes] = jnp.transpose(basis[lanes, :].astype(F32)).astype(BF16)
        permuted[lanes, :] = dot(regroup, basis[lanes, :]).astype(BF16)

    def arrive(b, carry):
        slots = pl.ds(b * BATCH, BATCH)
        remote(got.at[slots], got.at[slots], send_sems.at[0], code_sems.at[b], (gx, gy)).wait_recv()
        remote(recv.at[slots], recv.at[slots], send_sems.at[1], recv_sems.at[b], (gx, gy)).wait_recv()
        collect(recv, got, b, spread, gathered, keys, groups)
        return carry

    lax.fori_loop(0, batches, arrive, 0)
    for c in range(column_tiles):
        for n in range(c + 1):
            low = key_offset(c) + n * GROUPS
            block = [gathered[low : low + GROUPS, i * LANES : (i + 1) * LANES] for i in range(NB)]
            block = jnp.concatenate(block, axis=0).astype(BF16)
            matrix[n * LANES : (n + 1) * LANES, c * LANES : (c + 1) * LANES] = block
    step = 2 * LANES
    part = 3 * LANES
    for c in range(cells // step):
        columns = basis[:, c * step : (c + 1) * step]
        total = jnp.zeros((1, step), F32)
        for low in range(0, functions, part):
            product = dot(matrix[low : low + part, low:], columns[low:])
            product = product * permuted[low : low + part, c * step : (c + 1) * step].astype(F32)
            total = total + jnp.sum(product, axis=0, keepdims=True)
        charge[2 * c : 2 * c + 1, :] = total[:, :LANES]
        charge[2 * c + 1 : 2 * c + 2, :] = total[:, LANES:]
    edges = [
        remote(charge, halo.at[n], halo_send.at[n], halo_recv.at[n], place)
        for n, place in enumerate(
            (((gx + 1) % 16, gy), ((gx + 15) % 16, gy), (gx, (gy + 7) % 8), (gx, (gy + 1) % 8))
        )
    ]
    for copy in edges:
        copy.start()
    for copy in edges:
        copy.wait()
    potential = potential_of(charge[...], halo[0], halo[1], halo[3], halo[2])
    for half in range(2):
        rows = potential if half == 0 else pltpu.roll(potential, CY, 1)
        potential_ref[pl.ds(half, CX // 2, stride=2), :] = rows[:, :CY]
    potential_out = pltpu.make_async_copy(potential_ref, potential_hbm, local_sem.at[1])
    potential_out.start()
    for c in range(cells // LANES):
        lanes = slice(c * LANES, (c + 1) * LANES)
        weighted[:, lanes] = (permuted[:, lanes].astype(F32) * potential[c : c + 1]).astype(BF16)
    cuts = [0] + list(range(1, column_tiles + 1, 2))
    for start, stop in zip(cuts, cuts[1:]):
        high = stop * LANES
        product = dot(weighted[:high, :], upright[:, start * LANES : high])
        for c in range(start, stop):
            tile = product[:, c * LANES - start * LANES : (c + 1 - start) * LANES]
            for n in range(0, c + 1, 2):
                low = key_offset(c) + n * GROUPS
                for i in range(NB):
                    pieces = [
                        tile[m * LANES + i * GROUPS : m * LANES + (i + 1) * GROUPS]
                        if m <= c else jnp.zeros((GROUPS, LANES), F32)
                        for m in (n, n + 1)
                    ]
                    piece = jnp.concatenate(pieces, axis=0).astype(BF16)
                    picked[low : low + 2 * GROUPS, i * LANES : (i + 1) * LANES] = piece
    keep = pltpu.make_async_copy(back.at[0], returned.at[0], return_sem)

    def give(b, carry):
        pick(b, picked, keys, groups, fold, spaced, back)
        for j, place in enumerate(places(b, gx, gy, False)):
            slot = b * BATCH + j

            def start():
                remote(back.at[slot], returned.at[slot], send_sems.at[2], return_sem, place).start()

            if j == 0:
                pl.when(b > 0)(start)
                pl.when(b == 0)(keep.start)
            else:
                start()
        return carry

    lax.fori_loop(0, batches, give, 0)
    for half in range(2):
        for n in range(devices * CAP // 512):
            part = picks[n * 512 : (n + 1) * 512, half * pairs : (half + 1) * pairs].astype(F32)
            lanes = half * devices * CAP + n * 512
            picks_turned[:, lanes : lanes + 512] = jnp.transpose(part).astype(BF16)
    mask = size_mask_of(sizes_ref[...], eye)
    remote(returned, returned, send_sems.at[2], return_sem, (gx, gy)).wait_recv()
    blocks = returned[...].reshape(devices * CAP, WIDTH)
    blocks = jnp.concatenate([blocks, dot(blocks, turned).astype(BF16)], axis=0)
    out_ref[...] = jnp.where(mask, dot(picks_turned[...], blocks) * float(cells) ** -0.5, 0.0)
    out = pltpu.make_async_copy(out_ref, out_hbm, local_sem.at[2])
    out.start()
    out.wait()
    potential_out.wait()
    others = pl.ds(0, devices - 1)
    remote(got.at[others], got.at[others], send_sems.at[0], code_sems.at[0], (gx, gy)).wait_send()
    remote(chunks.at[others], recv.at[others], send_sems.at[1], recv_sems.at[0], (gx, gy)).wait_send()
    remote(back.at[others], returned.at[others], send_sems.at[2], return_sem, (gx, gy)).wait_send()


def finish_kernel(summed, field, out, potential):
    out[...] = summed[...]
    potential[...] = field[...]


VMEM_SPEC = pl.BlockSpec(memory_space=pltpu.VMEM)
ANY_SPEC = pl.BlockSpec(memory_space=pl.ANY)
DMA = pltpu.SemaphoreType.DMA


def shards(density, pair_tiles, pair_slots, pair_sizes, basis_table, tile_extent):
    devices = lax.axis_size("gx") * lax.axis_size("gy")
    pairs, targets = pair_tiles.shape
    atoms = tile_extent.shape[2]
    functions, cells = basis_table.shape[1:]
    rows = cells // LANES
    key_rows = key_offset(functions // LANES)
    chunk = pltpu.VMEM((devices, CAP, WIDTH), BF16)
    entries = devices * CAP
    spaced = NB * LANES
    results = pl.pallas_call(
        whole_kernel,
        name="whole",
        out_shape=[
            jax.ShapeDtypeStruct((pairs, WIDTH), F32),
            jax.ShapeDtypeStruct((CX, CY), F32),
        ],
        in_specs=[ANY_SPEC] * 9,
        out_specs=[ANY_SPEC] * 2,
        scratch_shapes=[
            pltpu.VMEM((targets, pairs), I32),
            pltpu.VMEM((targets, 2, pairs), I32),
            pltpu.VMEM((2, pairs), I32),
            pltpu.VMEM((pairs, WIDTH), BF16),
            pltpu.VMEM((2, atoms), I32),
            pltpu.VMEM((WIDTH, 3 * WIDTH), F32),
            pltpu.VMEM((WIDTH, spaced), F32),
            pltpu.VMEM((spaced, WIDTH), F32),
            pltpu.VMEM((pairs, WIDTH), F32),
            pltpu.VMEM((CX, CY), F32),
            pltpu.VMEM((functions, cells), BF16),
            pltpu.VMEM((functions, cells), BF16),
            pltpu.VMEM((functions, cells), BF16),
            pltpu.VMEM((cells, functions), BF16),
            chunk,
            chunk,
            chunk,
            chunk,
            pltpu.VMEM((devices * CAP // LANES, 1, LANES), F32),
            pltpu.VMEM((devices, 1, LANES), F32),
            pltpu.VMEM((devices, pairs), F32),
            pltpu.VMEM((entries, 2 * pairs), BF16),
            pltpu.VMEM((pairs, 2 * entries), BF16),
            pltpu.VMEM((WIDTH, spaced), BF16),
            pltpu.VMEM((spaced, WIDTH), BF16),
            pltpu.VMEM((key_rows, spaced), F32),
            pltpu.VMEM((entries, LANES), F32),
            pltpu.VMEM((entries, LANES), F32),
            pltpu.VMEM((functions, functions), BF16),
            pltpu.VMEM((-(-key_rows // LANES) * LANES, spaced), BF16),
            pltpu.VMEM((BATCH * CAP, spaced), BF16),
            pltpu.VMEM((rows, LANES), F32),
            pltpu.VMEM((4, rows, LANES), F32),
            DMA((3,)),
            DMA((devices // BATCH,)),
            DMA((devices // BATCH,)),
            DMA,
            DMA((4,)),
            DMA((4,)),
            DMA((9,)),
        ],
        compiler_params=pltpu.CompilerParams(
            vmem_limit_bytes=VMEM_BYTES, collective_id=1, has_side_effects=True
        ),
    )(pair_tiles.T, pair_slots.transpose(1, 2, 0), pair_sizes.T, density, tile_extent[0], basis_table[0], *constants())
    return tuple(pl.pallas_call(
        finish_kernel,
        name="finish",
        out_shape=[jax.ShapeDtypeStruct(result.shape, result.dtype) for result in results],
        in_specs=[VMEM_SPEC] * 2,
        out_specs=[VMEM_SPEC] * 2,
        compiler_params=pltpu.CompilerParams(vmem_limit_bytes=VMEM_BYTES),
    )(*results))


def solution(mesh):
    in_specs = (
        P(("gx", "gy"), None),
        P(("gx", "gy"), None),
        P(("gx", "gy"), None, None),
        P(("gx", "gy"), None),
        P(("gx", "gy"), None, None),
        P(("gx", "gy"), None, None),
    )
    out_specs = (P(("gx", "gy"), None), P("gx", "gy"))
    return jax.shard_map(shards, mesh=mesh, in_specs=in_specs, out_specs=out_specs, check_vma=False)
```

```python
import functools

import jax
import jax.numpy as jnp
import numpy as np
from jax import lax
from jax.experimental import pallas as pl
from jax.experimental.pallas import tpu as pltpu
from jax.sharding import PartitionSpec as P

NB = 16
CX = 32
CY = 64
LANES = 128
GROUPS = LANES // NB
WIDTH = NB * NB
CAP = 16
BATCH = 16
STEP = 32
MESH = pl.DeviceIdType.MESH
F32 = jnp.float32
BF16 = jnp.bfloat16
I32 = jnp.int32
VMEM_BYTES = 60 * 1024 * 1024
gradient_weight = 1.0
NT = (((1,), (1,)), ((), ()))


def iota(shape, dim):
    return lax.broadcasted_iota(I32, shape, dim)


def dot(a, b, dims=(((1,), (0,)), ((), ()))):
    return lax.dot_general(a, b, dims, preferred_element_type=F32)


def ones_where(condition):
    return jnp.where(condition, 1.0, 0.0)


def size_mask_of(sizes, eye):
    pairs = sizes.shape[1]
    wide = sizes.astype(F32)
    first = dot(eye, jnp.broadcast_to(wide[0:1], (WIDTH, pairs)).astype(BF16), NT)
    second = dot(eye, jnp.broadcast_to(wide[1:2], (WIDTH, pairs)).astype(BF16), NT)
    lane = iota((pairs, WIDTH), 1)
    row = (lane // NB).astype(F32)
    col = (lane % NB).astype(F32)
    return (row < first) & (col < second)


def key_offset(column_tile):
    half = column_tile // 2
    return 16 * (half + 1) * (half + column_tile % 2)


def plan(tiles, slots_ref, tile_id, before, marks):
    targets, pairs = tiles.shape
    devices = marks.shape[0]
    chosen = jnp.zeros((devices, pairs), F32)
    kind = jnp.zeros((devices, pairs), F32)
    asked = []
    for k in range(targets):
        mark = ones_where(tiles[k : k + 1] == tile_id)
        slots = slots_ref[k].astype(F32)
        first, second = slots[0:1], slots[1:2]
        chosen = chosen + mark
        kind = kind + mark * (ones_where(first < second) + 2.0 * ones_where(first > second))
        asked += [tiles[k : k + 1].astype(F32), jnp.minimum(first, second), jnp.maximum(first, second)]
    rank = dot(chosen.astype(BF16), before)
    marks[...] = jnp.where(chosen > 0.5, rank * 4.0 + kind, -4.0)
    return jnp.concatenate(asked + [jnp.zeros((16 - 3 * targets, pairs), F32)], axis=0).astype(BF16)


def pack(b, tile, asked, blocks, marks, chunks, codes, picks):
    pairs = marks.shape[1]
    entries = STEP * CAP
    own = (4 * (iota((entries, pairs), 0) % CAP)).astype(F32)
    rows = jnp.broadcast_to(marks[pl.ds(b * STEP, STEP), :][:, None, :], (STEP, CAP, pairs))
    rows = rows.reshape(entries, pairs) - own
    same, upper, lower = ones_where(rows == 0.0), ones_where(rows == 1.0), ones_where(rows == 2.0)
    straight = upper.astype(BF16)
    across = (same + lower).astype(BF16)
    here = pl.ds(pl.multiple_of(b * entries, entries), entries)
    picks[here, :pairs] = straight
    picks[here, pairs:] = across
    weights = jnp.concatenate([(same + 2.0 * upper).astype(BF16), (2.0 * lower).astype(BF16)], axis=1)
    chunks[pl.ds(b * STEP, STEP)] = dot(weights, blocks).astype(BF16).reshape(STEP, CAP, WIDTH)
    told = dot(asked, straight + across, NT)
    first = jnp.zeros((1, entries), F32)
    second = jnp.zeros((1, entries), F32)
    for k in range(asked.shape[0] // 3):
        hit = told[3 * k : 3 * k + 1] == tile
        first = first + jnp.where(hit, told[3 * k + 1 : 3 * k + 2], 0.0)
        second = second + jnp.where(hit, told[3 * k + 2 : 3 * k + 3], 0.0)
    column_tile = jnp.floor(second * (1.0 / GROUPS))
    half = jnp.floor(column_tile * 0.5)
    key = 16.0 * (half + 1.0) * (column_tile - half) + first
    code = key * GROUPS + (second - column_tile * GROUPS)
    for n in range(entries // LANES):
        codes[b * (entries // LANES) + n] = code[:, n * LANES : (n + 1) * LANES]


INNER = [(j % 4, (j // 4 + j) % 4, (j + 3 * (j // 4)) % 4) for j in range(BATCH)]


def places(b, gx, gy, outward):
    core = gy % 2
    other = (core + b % 2) % 2
    turn = 1 + 2 * core if outward else 3 - 2 * other
    x, y, z = gx // 4, gx % 4, gy // 2
    xs = [((x + d * turn) % 4) * 4 for d in range(4)]
    ys = [(y + d * turn) % 4 for d in range(4)]
    zs = [((z + (b // 2 + d) * turn) % 4) * 2 + other for d in range(4)]
    return [(xs[dx] + ys[dy], zs[dz]) for dx, dy, dz in INNER]


def tile_of(slot, gx, gy):
    b, j = slot >> 4, slot & 15
    dx, dy, dz = j & 3, ((j >> 2) + j) & 3, ((b >> 1) + j + 3 * (j >> 2)) & 3
    core = gy % 2
    turn = 1 + 2 * core
    px = ((gx // 4 + dx * turn) & 3) * 4 + ((gx % 4 + dy * turn) & 3)
    return px * 8 + ((gy // 2 + dz * turn) & 3) * 2 + ((core + b) & 1)


def remote(source, target, send_sem, recv_sem, place):
    return pltpu.make_async_remote_copy(
        src_ref=source, dst_ref=target, send_sem=send_sem, recv_sem=recv_sem, device_id=place, device_id_type=MESH,
    )


def mask_basis(basis, extent):
    functions, cells = basis.shape
    atoms = functions // NB
    extent = extent.astype(F32)
    own = ones_where(iota((functions, atoms), 0) // NB == iota((functions, atoms), 1)).astype(BF16)
    half = (iota((functions, LANES), 1) // CY).astype(F32)
    low = dot(own, jnp.broadcast_to(extent[0:1], (LANES, atoms)).astype(BF16), NT) - half
    high = dot(own, jnp.broadcast_to(extent[1:2], (LANES, atoms)).astype(BF16), NT) - half
    for c in range(cells // LANES):
        row = c * (LANES // CY)
        inside = low <= float(row) if row < CX // 2 else high > float(row)
        lanes = slice(c * LANES, (c + 1) * LANES)
        basis[:, lanes] = basis[:, lanes] * ones_where(inside).astype(BF16)


def constants():
    row, lane = np.arange(WIDTH)[:, None], np.arange(WIDTH)[None, :]
    before = row < lane
    turned = (row // NB == lane % NB) & (row % NB == lane // NB)
    wide = np.arange(NB * LANES)[None, :]
    spread = (row // NB == wide // LANES) & (row % NB == wide % NB)
    square = np.concatenate([before, turned, row == lane], axis=1)
    return [np.asarray(x, np.float32) for x in (square, spread, spread.T)]


def collect(recv, got, b, spread, gathered, keys, groups):
    entries = BATCH * CAP
    own = iota((GROUPS, LANES), 0) == iota((GROUPS, LANES), 1) // CAP
    code = []
    for h in range(BATCH // GROUPS):
        lines = got[pl.ds(b * BATCH + h * GROUPS, GROUPS), 0, :]
        code.append(jnp.sum(jnp.where(own, lines, 0.0), axis=0, keepdims=True))
    code = jnp.concatenate(code, axis=1)
    key_row = jnp.floor(code * (1.0 / GROUPS))
    group_row = code - key_row * GROUPS
    key_rows = gathered.shape[0]
    onehot = ones_where(iota((key_rows, entries), 0).astype(F32) == key_row).astype(BF16)
    key = jnp.transpose(jnp.broadcast_to(key_row, (LANES, entries)))
    group = jnp.transpose(jnp.broadcast_to(group_row, (LANES, entries)))
    here = pl.ds(pl.multiple_of(b * entries, entries), entries)
    keys[here, :] = key
    groups[here, :] = group
    blocks = recv[pl.ds(b * BATCH, BATCH)].reshape(entries, WIDTH)
    wide = 2 * LANES
    inside = (iota((entries, wide), 1) % LANES // NB).astype(F32) == jnp.concatenate([group, group], axis=1)
    for c in range(NB // 2):
        lanes = slice(c * wide, (c + 1) * wide)
        spaced = jnp.where(inside, dot(blocks, spread[:, lanes]), 0.0).astype(BF16)
        gathered[:, lanes] = gathered[:, lanes] + dot(onehot, spaced)


def pick(b, picked, keys, groups, fold, spaced, back):
    entries = BATCH * CAP
    here = pl.ds(pl.multiple_of(b * entries, entries), entries)
    key, group = keys[here, :], groups[here, :]
    lane = iota((entries, LANES), 1).astype(F32)
    onehot = jnp.concatenate(
        [ones_where(lane + float(n * LANES) == key).astype(BF16) for n in range(picked.shape[0] // LANES)], axis=1
    )
    wide = 2 * LANES
    inside = (iota((entries, wide), 1) % LANES // NB).astype(F32) == jnp.concatenate([group, group], axis=1)
    for c in range(NB // 2):
        lanes = slice(c * wide, (c + 1) * wide)
        spaced[:, lanes] = jnp.where(inside, dot(onehot, picked[:, lanes]), 0.0).astype(BF16)
    blocks = dot(spaced[...], fold[...]).astype(BF16)
    back[pl.ds(b * BATCH, BATCH)] = blocks.reshape(BATCH, CAP, WIDTH)


def potential_of(charge, below, above, left, right):
    rows = charge.shape[0]
    lane = iota((rows, LANES), 1)
    row = iota((rows, LANES), 0)
    swapped = pltpu.roll(charge, CY, 1)
    first_of_above = pltpu.roll(above, CY, 1)[0:1]
    last_of_below = pltpu.roll(below, CY, 1)[rows - 1 : rows]
    up = jnp.where(row == rows - 1, first_of_above, pltpu.roll(swapped, rows - 1, 0))
    next_x = jnp.where(lane < CY, swapped, up)
    down = jnp.where(row == 0, last_of_below, pltpu.roll(swapped, 1, 0))
    last_x = jnp.where(lane < CY, down, swapped)
    next_y = jnp.where(lane % CY == CY - 1, pltpu.roll(right, CY - 1, 1), pltpu.roll(charge, LANES - 1, 1))
    last_y = jnp.where(lane % CY == 0, pltpu.roll(left, LANES - CY + 1, 1), pltpu.roll(charge, 1, 1))
    slope_x = 0.5 * (next_x - last_x)
    slope_y = 0.5 * (next_y - last_y)
    return charge * lax.rsqrt(
        1.0 + charge * charge + gradient_weight * (slope_x * slope_x + slope_y * slope_y)
    )


def whole_kernel(
    tiles_hbm, slots_hbm, sizes_hbm, density_hbm, extent_hbm, basis_hbm, ones_hbm, spread_hbm, fold_hbm,
    out_hbm, potential_hbm,
    tiles_ref, slots_ref, sizes_ref, density_ref, extent_ref, ones_ref, spread_ref, fold_ref, out_ref, potential_ref,
    basis, permuted, weighted, upright, chunks, recv, back, returned, codes, got, marks, picks, picks_turned, spread, fold, gathered, keys, groups,
    matrix, picked, spaced, charge, halo,
    send_sems, recv_sems, code_sems, return_sem, halo_send, halo_recv, local_sem,
):
    devices = chunks.shape[0]
    functions, cells = basis.shape
    atoms = functions // NB
    column_tiles = functions // LANES
    batches = devices // BATCH
    gx, gy = lax.axis_index("gx"), lax.axis_index("gy")
    load = pltpu.make_async_copy(basis_hbm, basis, local_sem.at[0])
    inputs = [
        pltpu.make_async_copy(source, target, local_sem.at[1 + n])
        for n, (source, target) in enumerate((
            (tiles_hbm, tiles_ref), (slots_hbm, slots_ref), (sizes_hbm, sizes_ref), (density_hbm, density_ref),
            (ones_hbm, ones_ref), (extent_hbm, extent_ref), (spread_hbm, spread_ref), (fold_hbm, fold_ref),
        ))
    ]
    for copy in inputs:
        copy.start()
    load.start()
    barrier = pltpu.get_barrier_semaphore()

    def greet(b, carry):
        for j, place in enumerate(places(b, gx, gy, True)):
            def signal():
                pl.semaphore_signal(barrier, inc=1, device_id=place, device_id_type=MESH)

            if j == 0:
                pl.when(b > 0)(signal)
            else:
                signal()
        return carry

    lax.fori_loop(0, batches, greet, 0)
    gathered[...] = jnp.zeros_like(gathered)
    for c in range(column_tiles):
        low, high = (c + 1) * LANES, (c + 2) * LANES
        if c % 2 == 1:
            matrix[low:high, c * LANES : (c + 1) * LANES] = jnp.zeros((high - low, LANES), BF16)
    low, high = key_offset(column_tiles), picked.shape[0]
    picked[low:high, :] = jnp.zeros((high - low, picked.shape[1]), BF16)
    for copy in inputs[:5]:
        copy.wait()
    pairs = density_ref.shape[0]
    before, turned, eye = (ones_ref[:, n * WIDTH : (n + 1) * WIDTH].astype(BF16) for n in range(3))
    mask = size_mask_of(sizes_ref[...], eye)
    masked = jnp.where(mask, density_ref[...].astype(F32), 0.0).astype(BF16)
    blocks = jnp.concatenate([masked, dot(masked, turned).astype(BF16)], axis=0)
    asked = plan(tiles_ref[...], slots_ref, tile_of(iota((devices, 1), 0), gx, gy), before, marks)
    rows_per_batch = BATCH * CAP // LANES

    def push(b, carry):
        for j, place in enumerate(places(b, gx, gy, True)):
            slot = b * BATCH + j
            row = b * rows_per_batch + j * CAP // LANES

            def start():
                remote(codes.at[row], got.at[slot], send_sems.at[0], code_sems.at[b], place).start()
                remote(chunks.at[slot], recv.at[slot], send_sems.at[1], recv_sems.at[b], place).start()

            def keep():
                pltpu.make_async_copy(codes.at[0], got.at[0], code_sems.at[0]).start()
                pltpu.make_async_copy(chunks.at[0], recv.at[0], recv_sems.at[0]).start()

            if j == 0:
                pl.when(b > 0)(start)
                pl.when(b == 0)(keep)
            else:
                start()
        return carry

    def fill(n, carry):
        tile = tile_of(n * STEP + iota((1, STEP * CAP), 1) // CAP, gx, gy).astype(F32)
        pack(n, tile, asked, blocks, marks, chunks, codes, picks)
        return carry

    lax.fori_loop(0, devices // STEP, fill, 0)
    pl.semaphore_wait(barrier, devices - 1)
    lax.fori_loop(0, batches, push, 0)
    for copy in inputs[5:]:
        copy.wait()
    spread[...] = spread_ref[...].astype(BF16)
    fold[...] = fold_ref[...].astype(BF16)
    load.wait()
    mask_basis(basis, extent_ref[...])
    row, lane = iota((LANES, LANES), 0), iota((LANES, LANES), 1)
    regroup = ones_where(lane == row % GROUPS * NB + row // GROUPS).astype(BF16)
    for c in range(column_tiles):
        lanes = slice(c * LANES, (c + 1) * LANES)
        upright[:, lanes] = jnp.transpose(basis[lanes, :].astype(F32)).astype(BF16)
        permuted[lanes, :] = dot(regroup, basis[lanes, :]).astype(BF16)

    def arrive(b, carry):
        slots = pl.ds(b * BATCH, BATCH)
        remote(got.at[slots], got.at[slots], send_sems.at[0], code_sems.at[b], (gx, gy)).wait_recv()
        remote(recv.at[slots], recv.at[slots], send_sems.at[1], recv_sems.at[b], (gx, gy)).wait_recv()
        collect(recv, got, b, spread, gathered, keys, groups)
        return carry

    lax.fori_loop(0, batches, arrive, 0)
    for c in range(column_tiles):
        for n in range(c + 1):
            low = key_offset(c) + n * GROUPS
            block = [gathered[low : low + GROUPS, i * LANES : (i + 1) * LANES] for i in range(NB)]
            block = jnp.concatenate(block, axis=0).astype(BF16)
            matrix[n * LANES : (n + 1) * LANES, c * LANES : (c + 1) * LANES] = block
    step = 2 * LANES
    parts = [0] + list(range(LANES, functions + 1, 2 * LANES))
    for c in range(cells // step):
        columns = basis[:, c * step : (c + 1) * step]
        total = jnp.zeros((1, step), F32)
        for low, high in zip(parts, parts[1:]):
            product = dot(matrix[low:high, low:], columns[low:])
            product = product * permuted[low:high, c * step : (c + 1) * step].astype(F32)
            total = total + jnp.sum(product, axis=0, keepdims=True)
        charge[2 * c : 2 * c + 1, :] = total[:, :LANES]
        charge[2 * c + 1 : 2 * c + 2, :] = total[:, LANES:]
    edges = [
        remote(charge, halo.at[n], halo_send.at[n], halo_recv.at[n], place)
        for n, place in enumerate(
            (((gx + 1) % 16, gy), ((gx + 15) % 16, gy), (gx, (gy + 7) % 8), (gx, (gy + 1) % 8))
        )
    ]
    for copy in edges:
        copy.start()
    for copy in edges:
        copy.wait()
    potential = potential_of(charge[...], halo[0], halo[1], halo[3], halo[2])
    for half in range(2):
        rows = potential if half == 0 else pltpu.roll(potential, CY, 1)
        potential_ref[pl.ds(half, CX // 2, stride=2), :] = rows[:, :CY]
    potential_out = pltpu.make_async_copy(potential_ref, potential_hbm, local_sem.at[1])
    potential_out.start()
    for c in range(cells // LANES):
        lanes = slice(c * LANES, (c + 1) * LANES)
        weighted[:, lanes] = (permuted[:, lanes].astype(F32) * potential[c : c + 1]).astype(BF16)
    cuts = [0] + list(range(1, column_tiles + 1, 2))
    for start, stop in zip(cuts, cuts[1:]):
        high = stop * LANES
        product = dot(weighted[:high, :], upright[:, start * LANES : high])
        for c in range(start, stop):
            tile = product[:, c * LANES - start * LANES : (c + 1 - start) * LANES]
            for n in range(0, c + 1, 2):
                low = key_offset(c) + n * GROUPS
                for i in range(NB):
                    pieces = [
                        tile[m * LANES + i * GROUPS : m * LANES + (i + 1) * GROUPS]
                        if m <= c else jnp.zeros((GROUPS, LANES), F32)
                        for m in (n, n + 1)
                    ]
                    piece = jnp.concatenate(pieces, axis=0).astype(BF16)
                    picked[low : low + 2 * GROUPS, i * LANES : (i + 1) * LANES] = piece
    keep = pltpu.make_async_copy(back.at[0], returned.at[0], return_sem)

    def give(b, carry):
        pick(b, picked, keys, groups, fold, spaced, back)
        for j, place in enumerate(places(b, gx, gy, False)):
            slot = b * BATCH + j

            def start():
                remote(back.at[slot], returned.at[slot], send_sems.at[2], return_sem, place).start()

            if j == 0:
                pl.when(b > 0)(start)
                pl.when(b == 0)(keep.start)
            else:
                start()
        return carry

    lax.fori_loop(0, batches, give, 0)
    for half in range(2):
        for n in range(devices * CAP // 512):
            part = picks[n * 512 : (n + 1) * 512, half * pairs : (half + 1) * pairs].astype(F32)
            lanes = half * devices * CAP + n * 512
            picks_turned[:, lanes : lanes + 512] = jnp.transpose(part).astype(BF16)
    mask = size_mask_of(sizes_ref[...], eye)
    remote(returned, returned, send_sems.at[2], return_sem, (gx, gy)).wait_recv()
    blocks = returned[...].reshape(devices * CAP, WIDTH)
    blocks = jnp.concatenate([blocks, dot(blocks, turned).astype(BF16)], axis=0)
    out_ref[...] = jnp.where(mask, dot(picks_turned[...], blocks) * float(cells) ** -0.5, 0.0)
    out = pltpu.make_async_copy(out_ref, out_hbm, local_sem.at[2])
    out.start()
    out.wait()
    potential_out.wait()
    others = pl.ds(0, devices - 1)
    remote(got.at[others], got.at[others], send_sems.at[0], code_sems.at[0], (gx, gy)).wait_send()
    remote(chunks.at[others], recv.at[others], send_sems.at[1], recv_sems.at[0], (gx, gy)).wait_send()
    remote(back.at[others], returned.at[others], send_sems.at[2], return_sem, (gx, gy)).wait_send()


def finish_kernel(summed, field, out, potential):
    out[...] = summed[...]
    potential[...] = field[...]


VMEM_SPEC = pl.BlockSpec(memory_space=pltpu.VMEM)
ANY_SPEC = pl.BlockSpec(memory_space=pl.ANY)
DMA = pltpu.SemaphoreType.DMA


def shards(density, pair_tiles, pair_slots, pair_sizes, basis_table, tile_extent):
    devices = lax.axis_size("gx") * lax.axis_size("gy")
    pairs, targets = pair_tiles.shape
    atoms = tile_extent.shape[2]
    functions, cells = basis_table.shape[1:]
    rows = cells // LANES
    key_rows = key_offset(functions // LANES)
    chunk = pltpu.VMEM((devices, CAP, WIDTH), BF16)
    entries = devices * CAP
    spaced = NB * LANES
    results = pl.pallas_call(
        whole_kernel,
        name="whole",
        out_shape=[
            jax.ShapeDtypeStruct((pairs, WIDTH), F32),
            jax.ShapeDtypeStruct((CX, CY), F32),
        ],
        in_specs=[ANY_SPEC] * 9,
        out_specs=[ANY_SPEC] * 2,
        scratch_shapes=[
            pltpu.VMEM((targets, pairs), I32),
            pltpu.VMEM((targets, 2, pairs), I32),
            pltpu.VMEM((2, pairs), I32),
            pltpu.VMEM((pairs, WIDTH), BF16),
            pltpu.VMEM((2, atoms), I32),
            pltpu.VMEM((WIDTH, 3 * WIDTH), F32),
            pltpu.VMEM((WIDTH, spaced), F32),
            pltpu.VMEM((spaced, WIDTH), F32),
            pltpu.VMEM((pairs, WIDTH), F32),
            pltpu.VMEM((CX, CY), F32),
            pltpu.VMEM((functions, cells), BF16),
            pltpu.VMEM((functions, cells), BF16),
            pltpu.VMEM((functions, cells), BF16),
            pltpu.VMEM((cells, functions), BF16),
            chunk,
            chunk,
            chunk,
            chunk,
            pltpu.VMEM((devices * CAP // LANES, 1, LANES), F32),
            pltpu.VMEM((devices, 1, LANES), F32),
            pltpu.VMEM((devices, pairs), F32),
            pltpu.VMEM((entries, 2 * pairs), BF16),
            pltpu.VMEM((pairs, 2 * entries), BF16),
            pltpu.VMEM((WIDTH, spaced), BF16),
            pltpu.VMEM((spaced, WIDTH), BF16),
            pltpu.VMEM((key_rows, spaced), F32),
            pltpu.VMEM((entries, LANES), F32),
            pltpu.VMEM((entries, LANES), F32),
            pltpu.VMEM((functions, functions), BF16),
            pltpu.VMEM((-(-key_rows // LANES) * LANES, spaced), BF16),
            pltpu.VMEM((BATCH * CAP, spaced), BF16),
            pltpu.VMEM((rows, LANES), F32),
            pltpu.VMEM((4, rows, LANES), F32),
            DMA((3,)),
            DMA((devices // BATCH,)),
            DMA((devices // BATCH,)),
            DMA,
            DMA((4,)),
            DMA((4,)),
            DMA((9,)),
        ],
        compiler_params=pltpu.CompilerParams(
            vmem_limit_bytes=VMEM_BYTES, collective_id=1, has_side_effects=True
        ),
    )(pair_tiles.T, pair_slots.transpose(1, 2, 0), pair_sizes.T, density, tile_extent[0], basis_table[0], *constants())
    return tuple(pl.pallas_call(
        finish_kernel,
        name="finish",
        out_shape=[jax.ShapeDtypeStruct(result.shape, result.dtype) for result in results],
        in_specs=[VMEM_SPEC] * 2,
        out_specs=[VMEM_SPEC] * 2,
        compiler_params=pltpu.CompilerParams(vmem_limit_bytes=VMEM_BYTES),
    )(*results))


def solution(mesh):
    in_specs = (
        P(("gx", "gy"), None),
        P(("gx", "gy"), None),
        P(("gx", "gy"), None, None),
        P(("gx", "gy"), None),
        P(("gx", "gy"), None, None),
        P(("gx", "gy"), None, None),
    )
    out_specs = (P(("gx", "gy"), None), P("gx", "gy"))
    return jax.shard_map(shards, mesh=mesh, in_specs=in_specs, out_specs=out_specs, check_vma=False)
```
